128 devices in a mesh: az: 16 (over z_hi, x, core), gz: 8 (over y, z_lo).
Axes of the slice: x: 4, y: 4, z: 4 (z_hi: 2, z_lo: 2; z = z_hi * 2 + z_lo), core: 2. Of those that a mesh axis runs over, the one named last changes fastest.
Arguments:
- pressure: float32 [512, 64, 512], P('az', 'gz'), may hold values from -6 to 6
- divergence: float32 [512, 64, 512], P('az', 'gz'), may hold values from -6 to 6
- void_fraction: float32 [512, 64, 512], P('az', 'gz'), may hold values from 0 to 0.8
- bubble_volume: float32 [16384], P(('az', 'gz')), may hold values from 0.5 to 5
- bubble_count: int32 [128], P(('az', 'gz')), may hold values from 16 to 128, as said below
- bubble_cell: int32 [16384], P(('az', 'gz')), may hold values from 0 to 131071
Outputs:
- pressure_out: float32 [512, 64, 512], P('az', 'gz')
- scaled_residual: float32 [512, 64, 512], P('az', 'gz')
The draws below stay inside these ranges and needn't reach their ends.
Inputs may be any that keep to these rules, and one draw needn't show every extreme that they name: `bubble_count`: bubble slots below the count are live; the devices of three neighbouring azimuth owners have all 128 slots live in every draw.
All inputs are finite; a program needn't handle non-finite values.
Results may differ from the reference program's by a relative error of at most 0.0003.
Values sent between devices are 32-bit elements; how exact they have to be, the bound alone decides.
No kernel may reach another device: no remote copies, remote signals or barrier semaphores. Data moves between devices by JAX's collectives and lax.ppermute only.
A program may use at most 256 MiB of HBM per device.

```python
import math
import jax
import jax.numpy as jnp

AZ_DEV = 32
HT_DEV = 8
RADIAL = 512
SLOTS = 128
LEVELS = 4
SWEEPS = 1
COARSE_SWEEPS = 32
AZIMUTH = 512
HEIGHT = 64
BUBBLES = 16384
N_AZ = 16
N_GZ = 8
DEVICES = 128


def draw_bubble_count(key, part):
    first_key, second_key = jax.random.split(jax.random.fold_in(key, 17))
    start = jax.random.randint(first_key, (), 0, N_AZ)
    owners = jnp.arange(DEVICES, dtype=jnp.int32) // N_GZ
    plume = (owners - start) % N_AZ < 3
    sparse = jax.random.randint(second_key, (DEVICES,), SLOTS // 8, SLOTS // 3 + 1)
    return jnp.where(plume, SLOTS, sparse).astype(jnp.int32)


def set_ends(entries, stream_key, least, high):
    extent = entries.shape
    index_at = [jax.random.randint(jax.random.fold_in(stream_key, axis), (), 0, extent[axis]) for axis in range(len(extent))]
    entries = entries.at[tuple(index_at)].set(least)
    longest = extent.index(max(extent))
    index_at[longest] = (index_at[longest] + 1) % extent[longest]
    return entries.at[tuple(index_at)].set(high)


def level_of(own_key, extent, shards, low, largest):
    gain = 1.0
    for axis_at, shards_of in shards:
        draws = jax.random.uniform(jax.random.fold_in(jax.random.fold_in(own_key, 6), axis_at), (shards_of,), jnp.float32, low / len(shards), largest / len(shards))
        gain = gain * jnp.repeat(jnp.exp(draws), extent[axis_at] // shards_of).reshape((-1,) + (1,) * (len(extent) - 1 - axis_at))
    return gain


def normal_values(key, dims, scale, most, cuts=(), kind=jnp.bfloat16):
    level = level_of(key, dims, cuts, -0.22, 0.18) if cuts else 1.0
    entries = jax.random.normal(key, dims, jnp.float32) * scale * level
    return jnp.minimum(jnp.maximum(entries, -most), most).astype(kind)


def setup_inputs(seed: int = 0) -> dict:
    key_list = jax.random.split(jax.random.key(seed), 7)
    pressure = normal_values(key_list[0], (AZIMUTH, HEIGHT, RADIAL), 1.0, 6.0, ((0, 16), (1, 8)), jnp.float32)
    divergence = normal_values(key_list[1], (AZIMUTH, HEIGHT, RADIAL), 1.0, 6.0, ((0, 16), (1, 8)), jnp.float32)
    void_fraction = jnp.clip(0.8 * jax.random.uniform(key_list[2], (AZIMUTH, HEIGHT, RADIAL), jnp.float32) ** level_of(key_list[2], (AZIMUTH, HEIGHT, RADIAL), ((0, 16), (1, 8)), -0.2, 0.2), 0.0, 0.8)
    bubble_volume = jnp.clip(jnp.exp(math.log(5.0) - 2.3025851 * jax.random.uniform(key_list[3], (BUBBLES,), jnp.float32) ** level_of(key_list[3], (BUBBLES,), ((0, 128),), -0.2, 0.2)), 0.5, 5.0)
    bubble_count = draw_bubble_count(jax.random.fold_in(key_list[6], 71), 0)
    bubble_cell = set_ends(jax.random.randint(key_list[5], (BUBBLES,), 0, AZ_DEV * HT_DEV * RADIAL), jax.random.fold_in(key_list[5], 1), 0, (AZ_DEV * HT_DEV * RADIAL) - 1).astype(jnp.int32)
    return {"pressure": pressure, "divergence": divergence, "void_fraction": void_fraction, "bubble_volume": bubble_volume, "bubble_count": bubble_count, "bubble_cell": bubble_cell}


SIGMA = 0.02
OMEGA = 0.8


def radial_ratios(size):
    positions = jnp.arange(1, size, dtype=jnp.float32)
    return positions / (positions + 0.5), positions / (positions - 0.5)


def weights_global(mobility, level_no):
    az_n, ht_n, rad_n = mobility.shape
    angle_step = 2.0 * math.pi / az_n
    radius = jnp.arange(rad_n, dtype=jnp.float32) + 0.5
    metric = (radius * angle_step) ** 2
    wa_minus = 0.5 * (jnp.roll(mobility, 1, 0) + mobility) / metric
    wa_plus = jnp.roll(wa_minus, -1, 0)
    z_face = 0.5 * (mobility[:, :-1] + mobility[:, 1:])
    zero_z = jnp.zeros((az_n, 1, rad_n), jnp.float32)
    wz_minus = jnp.concatenate([zero_z, z_face], 1)
    wz_plus = jnp.concatenate([z_face, zero_z], 1)
    r_face = 0.5 * (mobility[:, :, :-1] + mobility[:, :, 1:])
    inward, outward = radial_ratios(rad_n)
    zero_r = jnp.zeros((az_n, ht_n, 1), jnp.float32)
    wr_inner = jnp.concatenate([zero_r, r_face * inward], 2)
    wr_outer = jnp.concatenate([r_face * outward, zero_r], 2)
    diagonal = wa_minus + wa_plus + wz_minus + wz_plus + wr_inner + wr_outer + SIGMA * 4.0 ** level_no
    return (wa_minus, wa_plus, wz_minus, wz_plus, wr_inner, wr_outer, diagonal)


def apply_global(iterate, weights):
    wa_minus, wa_plus, wz_minus, wz_plus, wr_inner, wr_outer, diagonal = weights
    az_n, ht_n, rad_n = iterate.shape
    zero_z = jnp.zeros((az_n, 1, rad_n), jnp.float32)
    zero_r = jnp.zeros((az_n, ht_n, 1), jnp.float32)
    below = jnp.concatenate([zero_z, iterate[:, :-1]], 1)
    above = jnp.concatenate([iterate[:, 1:], zero_z], 1)
    inner = jnp.concatenate([zero_r, iterate[:, :, :-1]], 2)
    outer = jnp.concatenate([iterate[:, :, 1:], zero_r], 2)
    neighbours = (wa_minus * jnp.roll(iterate, 1, 0) + wa_plus * jnp.roll(iterate, -1, 0)
                  + wz_minus * below + wz_plus * above + wr_inner * inner + wr_outer * outer)
    return diagonal * iterate - neighbours


def smooth_global(iterate, source_term, weights, sweep_count):
    for _ in range(sweep_count):
        iterate = iterate + OMEGA * (source_term - apply_global(iterate, weights)) / weights[6]
    return iterate


def coarsen(array_in):
    az_n, ht_n, rad_n = array_in.shape
    return array_in.reshape(az_n // 2, 2, ht_n // 2, 2, rad_n // 2, 2).sum(axis=(1, 3, 5))


def refine(correction):
    return jnp.repeat(jnp.repeat(jnp.repeat(correction, 2, 0), 2, 1), 2, 2)


def cycle(level_no, iterate, source_term, all_weights):
    weights = all_weights[level_no]
    if level_no == LEVELS - 1:
        return smooth_global(iterate, source_term, weights, COARSE_SWEEPS)
    iterate = smooth_global(iterate, source_term, weights, SWEEPS)
    remainder = source_term - apply_global(iterate, weights)
    coarse_rhs = 0.5 * coarsen(remainder)
    correction = cycle(level_no + 1, jnp.zeros_like(coarse_rhs), coarse_rhs, all_weights)
    iterate = iterate + refine(correction)
    return smooth_global(iterate, source_term, weights, SWEEPS)


def reference(pressure, divergence, void_fraction, bubble_volume, bubble_count, bubble_cell):
    slot_pos = jnp.arange(SLOTS, dtype=jnp.int32)
    counts = bubble_count.reshape(N_AZ, N_GZ, 1)
    live_vol = bubble_volume.reshape(N_AZ, N_GZ, SLOTS) * (slot_pos[None, None, :] < counts).astype(jnp.float32)
    arrived = jnp.roll(live_vol, 1, axis=0)
    cells = bubble_cell.reshape(N_AZ, N_GZ, SLOTS)
    az_idx = jnp.arange(N_AZ, dtype=jnp.int32)[:, None, None] * AZ_DEV + cells // (HT_DEV * RADIAL)
    ht_idx = jnp.arange(N_GZ, dtype=jnp.int32)[None, :, None] * HT_DEV + (cells // RADIAL) % HT_DEV
    rad_idx = cells % RADIAL
    rhs_zero = divergence.at[az_idx, ht_idx, rad_idx].add(arrived)
    mobility = 1.0 / (1.0 - void_fraction)
    all_weights = []
    for level_no in range(LEVELS):
        if level_no > 0:
            mobility = 0.125 * coarsen(mobility)
        all_weights.append(weights_global(mobility, level_no))
    pressure_out = cycle(0, pressure, rhs_zero, all_weights)
    scaled_residual = (rhs_zero - apply_global(pressure_out, all_weights[0])) / all_weights[0][6]
    return pressure_out, scaled_residual
```

```python
import functools
import math

import jax
import jax.numpy as jnp
from jax import lax
from jax.experimental import pallas as pl
from jax.experimental.pallas import tpu as pltpu
from jax.sharding import PartitionSpec as P

SIGMA = 0.02
OMEGA = 0.8
COARSE_SWEEPS = 32
F32 = jnp.float32

NA, NH, NR = 32, 8, 512
A1, H1, R1 = 16, 4, 256
A2, H2, R2 = 8, 2, 128
AZ2, G2 = 128, 8
AZ3 = 64
N_AZ, N_GZ = 16, 8
SLOTS = 128


def struct(*shape):
    return jax.ShapeDtypeStruct(shape, F32)


def call(kernel, outs, ins, scratch=(), smem=(), limit=48):
    specs = [
        pl.BlockSpec(memory_space=pltpu.SMEM if i in smem else pltpu.VMEM) for i in range(len(ins))
    ]
    return pl.pallas_call(
        kernel,
        out_shape=outs,
        in_specs=specs,
        out_specs=[pl.BlockSpec(memory_space=pltpu.VMEM) for _ in outs],
        scratch_shapes=list(scratch),
        compiler_params=pltpu.CompilerParams(vmem_limit_bytes=limit * 1024 * 1024),
    )(*ins)


def iota(shape, dim):
    return lax.broadcasted_iota(jnp.int32, shape, dim)


def dot(a, b):
    return jnp.dot(a, b, precision=lax.Precision.HIGHEST, preferred_element_type=F32)


def radial_consts(shape, size, step, rad):
    i = rad.astype(F32)
    metric = ((i + 0.5) * step) ** 2
    ca = 0.5 / metric
    ri = jnp.where(rad > 0, 0.5 * i / (i + 0.5), 0.0)
    ro = jnp.where(rad < size - 1, 0.5 * (i + 1.0) / (i + 0.5), 0.0)
    return ca, ri, ro


def pair_cols(n):
    return (iota((n, n // 2), 0) // 2 == iota((n, n // 2), 1)).astype(F32)


def dup_cols(n):
    return (iota((n, 2 * n), 0) == iota((n, 2 * n), 1) // 2).astype(F32)


def pair_rows_h(rows):
    return (iota((rows // 2, rows), 1) // 2 == iota((rows // 2, rows), 0)).astype(F32)


def block_rows(az, ht):
    out = (az // 2) * (ht // 2)
    r = iota((out, az * ht), 1)
    o = iota((out, az * ht), 0)
    target = (r // (2 * ht)) * (ht // 2) + (r % ht) // 2
    return (target == o).astype(F32)


def position():
    return lax.axis_index("az"), lax.axis_index("gz")


def pick(par, even, odd):
    return jnp.where(par == 0, even, odd)


class Halo:
    def __init__(self, x_ref, c_ref, z_ref, y_ref):
        a, g = position()
        self.pa, self.pg = a % 2, g % 2
        self.x, self.c, self.z, self.y = x_ref, c_ref, z_ref, y_ref

    def prev(self, rows, lanes):
        return pick(self.pa, self.x[rows, lanes], self.c[rows, lanes])

    def next(self, rows, lanes):
        return pick(self.pa, self.c[rows, lanes], self.x[rows, lanes])

    def below(self, rows, lanes):
        return pick(self.pg, self.y[rows, lanes], self.z[rows, lanes])

    def above(self, rows, lanes):
        return pick(self.pg, self.z[rows, lanes], self.y[rows, lanes])


def fine_walk(m_of, v_of, mb, ma, vb, va, emit):
    a, g = position()
    sub = iota((NH, NR), 0)
    lane = iota((NH, NR), 1)
    ca, ri, ro = radial_consts((NH, NR), NR, 2.0 * math.pi / (NA * N_AZ), lane)
    zlo = jnp.where((sub == 0) & (g == 0), 0.0, 0.5)
    zhi = jnp.where((sub == NH - 1) & (g == N_GZ - 1), 0.0, 0.5)
    first, final = sub == 0, sub == NH - 1
    mp, mc = m_of(-1), m_of(0)
    vp, vc = v_of(-1), v_of(0)
    wa = ca * (mp + mc)
    for i in range(NA):
        mn, vn = m_of(i + 1), v_of(i + 1)
        wan = ca * (mc + mn)
        m_lo = jnp.where(first, mb(i), pltpu.roll(mc, 1, 0))
        m_hi = jnp.where(final, ma(i), pltpu.roll(mc, NH - 1, 0))
        v_lo = jnp.where(first, vb(i), pltpu.roll(vc, 1, 0))
        v_hi = jnp.where(final, va(i), pltpu.roll(vc, NH - 1, 0))
        wl, wh = zlo * (mc + m_lo), zhi * (mc + m_hi)
        wi = ri * (mc + pltpu.roll(mc, 1, 1))
        wo = ro * (mc + pltpu.roll(mc, NR - 1, 1))
        diagonal = (wa + wan) + (wl + wh) + (wi + wo) + SIGMA
        around = (wa * vp + wan * vn) + (wl * v_lo + wh * v_hi)
        around = around + (wi * pltpu.roll(vc, 1, 1) + wo * pltpu.roll(vc, NR - 1, 1))
        emit(i, diagonal, around, vc)
        mp, mc, vp, vc, wa = mc, mn, vc, vn, wan


def level1_weights(m, prev, nxt, below, above, buf):
    a, g = position()
    rows = A1 * H1
    sub = iota((rows, R1), 0)
    lane = iota((rows, R1), 1)
    ht = sub % H1
    ca, ri, ro = radial_consts((rows, R1), R1, 2.0 * math.pi / (A1 * N_AZ), lane)
    zlo = jnp.where((ht == 0) & (g == 0), 0.0, 0.5)
    zhi = jnp.where((ht == H1 - 1) & (g == N_GZ - 1), 0.0, 0.5)
    mp, mn, ml, mh, mi, mo = level1_around(m, prev, nxt, below, above, buf)
    w = (ca * (m + mp), ca * (m + mn), zlo * (m + ml), zhi * (m + mh), ri * (m + mi), ro * (m + mo))
    diagonal = (w[0] + w[1]) + (w[2] + w[3]) + (w[4] + w[5]) + SIGMA * 4.0
    return w, diagonal


def level1_around(x, prev, nxt, below, above, buf):
    rows = A1 * H1
    ht = iota((rows, R1), 0) % H1
    spread = (iota((rows, A1), 0) // H1 == iota((rows, A1), 1)).astype(F32)
    buf[8 : 8 + rows, :] = x
    buf[8 - H1 : 8, :] = prev
    buf[8 + rows : 8 + rows + H1, :] = nxt
    xp = buf[8 - H1 : 8 - H1 + rows, :]
    xn = buf[8 + H1 : 8 + H1 + rows, :]
    xl = jnp.where(ht == 0, dot(spread, below), pltpu.roll(x, 1, 0))
    xh = jnp.where(ht == H1 - 1, dot(spread, above), pltpu.roll(x, rows - 1, 0))
    return xp, xn, xl, xh, pltpu.roll(x, 1, 1), pltpu.roll(x, R1 - 1, 1)


def weighted(w, n):
    return (w[0] * n[0] + w[1] * n[1]) + (w[2] * n[2] + w[3] * n[3]) + (w[4] * n[4] + w[5] * n[5])


ALL = slice(None)


def store_faces(ref, x_ref, c_ref, z_ref, y_ref, planes_at=0, rows_at=0):
    a, g = position()
    pa, pg = a % 2, g % 2
    c_plane = jnp.where(pa == 0, NA - 1, 0)
    x_plane = NA - 1 - c_plane
    c_ref[planes_at : planes_at + NH, :] = ref[c_plane]
    x_ref[planes_at : planes_at + NH, :] = ref[x_plane]
    z_row = jnp.where(pg == 0, NH - 1, 0)
    y_row = NH - 1 - z_row
    for i in range(NA):
        z_ref[rows_at + i : rows_at + i + 1, :] = ref[i, pl.ds(z_row, 1), :]
        y_ref[rows_at + i : rows_at + i + 1, :] = ref[i, pl.ds(y_row, 1), :]


def store_faces1(ref, x_ref, c_ref, z_ref, y_ref, planes_at=0, rows_at=0):
    a, g = position()
    pa, pg = a % 2, g % 2
    rows = A1 * H1
    lo, hi = ref[0:H1, :], ref[rows - H1 : rows, :]
    c_ref[planes_at : planes_at + H1, 0:R1] = pick(pa, hi, lo)
    x_ref[planes_at : planes_at + H1, 0:R1] = pick(pa, lo, hi)
    for i in range(A1):
        low, high = ref[H1 * i : H1 * i + 1, :], ref[H1 * i + H1 - 1 : H1 * i + H1, :]
        z_ref[rows_at + i : rows_at + i + 1, 0:R1] = pick(pg, high, low)
        y_ref[rows_at + i : rows_at + i + 1, 0:R1] = pick(pg, low, high)


def prepare(p_ref, void_ref, vol_ref, cnt_ref, m0_ref, m1_ref, m2_ref, sx, sc, sz, sy, pairs):
    for i in range(0, NA, 2):
        u = 1.0 / (1.0 - void_ref[i])
        v = 1.0 / (1.0 - void_ref[i + 1])
        m0_ref[i] = u
        m0_ref[i + 1] = v
        pairs[(i // 2) * NH : (i // 2 + 1) * NH, :] = u + v
    m1 = 0.125 * dot(pair_rows_h(A1 * NH), dot(pairs[...], pair_cols(NR)))
    m1_ref[...] = m1
    m2_ref[...] = 0.125 * dot(block_rows(A1, H1), dot(m1, pair_cols(R1)))
    store_faces(p_ref, sx, sc, sz, sy, 0, 0)
    store_faces(m0_ref, sx, sc, sz, sy, NH, NA)
    zero = jnp.zeros((NH, NR), F32)
    sx[2 * NH : 3 * NH, :] = zero
    sc[2 * NH : 3 * NH, :] = zero
    for ref in (sz, sy):
        ref[2 * NA : 2 * NA + A1, R1:NR] = jnp.zeros((A1, NR - R1), F32)
    store_faces1(m1_ref, sx, sc, sz, sy, 2 * NH, 2 * NA)
    live = jnp.where(iota((1, SLOTS), 1) < cnt_ref[0], vol_ref[...], 0.0)
    sx[2 * NH + H1 : 2 * NH + H1 + 1, 0:SLOTS] = live
    sc[2 * NH + H1 : 2 * NH + H1 + 1, 0:SLOTS] = live


def fine_mobility(m_ref, ah):
    def m_of(i):
        if i < 0:
            return ah.prev(slice(NH, 2 * NH), ALL)
        if i >= NA:
            return ah.next(slice(NH, 2 * NH), ALL)
        return m_ref[i]

    return (
        m_of,
        lambda i: ah.below(slice(NA + i, NA + i + 1), ALL),
        lambda i: ah.above(slice(NA + i, NA + i + 1), ALL),
    )


def fine_values(v_ref, vh):
    def v_of(i):
        if i < 0:
            return vh.prev(slice(0, NH), ALL)
        if i >= NA:
            return vh.next(slice(0, NH), ALL)
        return v_ref[i]

    return (
        v_of,
        lambda i: vh.below(slice(i, i + 1), ALL),
        lambda i: vh.above(slice(i, i + 1), ALL),
    )


def presmooth(p_ref, div_ref, m_ref, cell_ref, ax, ac, az, ay, rhs_ref, v_ref, sx, sc, sz, sy):
    ah = Halo(ax, ac, az, ay)
    arrived = ah.prev(slice(2 * NH + H1, 2 * NH + H1 + 1), slice(0, SLOTS))
    cell = cell_ref[...]
    plane_hot = (iota((NA * NH, SLOTS), 0) == lax.shift_right_logical(cell, 9)).astype(F32)
    radius_hot = jnp.where(iota((NR, SLOTS), 0) == (cell & (NR - 1)), arrived, 0.0)
    deposit = lax.dot_general(
        plane_hot,
        radius_hot,
        (((1,), (1,)), ((), ())),
        precision=lax.Precision.HIGHEST,
        preferred_element_type=F32,
    )
    rhs_ref[...] = div_ref[...] + deposit.reshape(NA, NH, NR)
    m_of, mb, ma = fine_mobility(m_ref, ah)
    v_of, vb, va = fine_values(p_ref, ah)

    def emit(i, diagonal, around, centre):
        v_ref[i] = centre + OMEGA * (rhs_ref[i] - diagonal * centre + around) / diagonal

    fine_walk(m_of, v_of, mb, ma, vb, va, emit)
    store_faces(v_ref, sx, sc, sz, sy)


def mobility1(m1_ref, ah):
    return (
        m1_ref[...],
        ah.prev(slice(2 * NH, 2 * NH + H1), slice(0, R1)),
        ah.next(slice(2 * NH, 2 * NH + H1), slice(0, R1)),
        ah.below(slice(2 * NA, 2 * NA + A1), slice(0, R1)),
        ah.above(slice(2 * NA, 2 * NA + A1), slice(0, R1)),
    )


def restrict(
    rhs_ref, v_ref, m_ref, m1_ref, ax, ac, az, ay, bx, bc, bz, by, b1_ref, v1_ref, sx, sc, sz, sy, pairs, buf
):
    ah, bh = Halo(ax, ac, az, ay), Halo(bx, bc, bz, by)
    m_of, mb, ma = fine_mobility(m_ref, ah)
    v_of, vb, va = fine_values(v_ref, bh)
    kept = []

    def emit(i, diagonal, around, centre):
        r = rhs_ref[i] - diagonal * centre + around
        if i % 2 == 0:
            kept.append(r)
        else:
            pairs[(i // 2) * NH : (i // 2 + 1) * NH, :] = kept.pop() + r

    fine_walk(m_of, v_of, mb, ma, vb, va, emit)
    b1 = 0.5 * dot(pair_rows_h(A1 * NH), dot(pairs[...], pair_cols(NR)))
    b1_ref[...] = b1
    _, diagonal = level1_weights(*mobility1(m1_ref, ah), buf)
    v1_ref[...] = OMEGA * b1 / diagonal
    store_faces1(v1_ref, sx, sc, sz, sy)


def halo1(h):
    return (
        h.prev(slice(0, H1), ALL),
        h.next(slice(0, H1), ALL),
        h.below(slice(0, A1), ALL),
        h.above(slice(0, A1), ALL),
    )


def restrict1(b1_ref, v1_ref, m1_ref, m2_ref, ax, ac, az, ay, cx, cc, cz, cy, out_ref, buf):
    ah, ch = Halo(ax, ac, az, ay), Halo(cx, cc, cz, cy)
    w, diagonal = level1_weights(*mobility1(m1_ref, ah), buf)
    v1 = v1_ref[...]
    n = level1_around(v1, *halo1(ch), buf)
    r1 = b1_ref[...] - diagonal * v1 + weighted(w, n)
    b2 = 0.5 * dot(block_rows(A1, H1), dot(r1, pair_cols(R1)))
    m2 = m2_ref[...]
    rows = A2 * H2
    for k in range(out_ref.shape[0]):
        out_ref[k, 0:rows, :] = b2
        out_ref[k, rows : 2 * rows, :] = m2


def level2_plane(ca, ri, ro, zlo, zhi, mp, mc, mn):
    mid = 0.5 * (mc[0] + mc[1])
    lows = (zlo * (mc[0] + pltpu.roll(mc[1], 1, 0)), mid)
    highs = (mid, zhi * (mc[1] + pltpu.roll(mc[0], G2 - 1, 0)))
    out = []
    for p in range(2):
        m = mc[p]
        w = (
            ca * (m + mp[p]),
            ca * (m + mn[p]),
            lows[p],
            highs[p],
            ri * (m + pltpu.roll(m, 1, 1)),
            ro * (m + pltpu.roll(m, R2 - 1, 1)),
        )
        out.append((w, (w[0] + w[1]) + (w[2] + w[3]) + (w[4] + w[5]) + SIGMA * 16.0))
    return out


def level2_around(vp, vc, vn):
    lows = (pltpu.roll(vc[1], 1, 0), vc[0])
    highs = (vc[1], pltpu.roll(vc[0], G2 - 1, 0))
    return [
        (vp[p], vn[p], lows[p], highs[p], pltpu.roll(vc[p], 1, 1), pltpu.roll(vc[p], R2 - 1, 1))
        for p in range(2)
    ]


def coarse(
    own, oth, b1_ref, v1_ref, m1_ref, ax, ac, az, ay, cx, cc, cz, cy,
    v1_out, sx, sc, sz, sy,
    m2, b2, v2, sum_m, sum_r, m3, w3, va, vb, e2, v2f, src, buf,
):
    a, g = position()
    pa = a % 2
    rows = A2 * H2

    for k in range(N_AZ):
        base = (k // 2) * N_GZ * 2 * rows
        for i in range(A2):
            total = None
            for p in range(2):
                at_b = pl.ds(base + i * 2 + p, G2, stride=2 * rows)
                at_m = pl.ds(base + rows + i * 2 + p, G2, stride=2 * rows)
                first, second = (own, oth) if k % 2 == 0 else (oth, own)
                b2[k * A2 + i + 2, p] = pick(pa, first[at_b, :], second[at_b, :])
                m2[k * A2 + i + 2, p] = pick(pa, first[at_m, :], second[at_m, :])
    for ref in (m2, b2):
        ref[0:2] = ref[AZ2 : AZ2 + 2]
        ref[AZ2 + 2 : AZ2 + 4] = ref[2:4]

    sub = iota((G2, R2), 0)
    lane = iota((G2, R2), 1)
    ca, ri, ro = radial_consts((G2, R2), R2, 2.0 * math.pi / AZ2, lane)
    zlo = jnp.where(sub == 0, 0.0, 0.5)
    zhi = jnp.where(sub == G2 - 1, 0.0, 0.5)
    plane = functools.partial(level2_plane, ca, ri, ro, zlo, zhi)

    def both(ref, s):
        return (ref[s, 0], ref[s, 1])

    def first_sweep(j, carry):
        s = 2 * j + 2
        planes = [both(m2, s + d) for d in (-1, 0, 1, 2)]
        for d in range(2):
            for p, (_, diagonal) in enumerate(plane(*planes[d : d + 3])):
                v2[s + d, p] = OMEGA * b2[s + d, p] / diagonal
        sum_m[j] = (planes[1][0] + planes[1][1]) + (planes[2][0] + planes[2][1])
        return carry

    lax.fori_loop(0, AZ3, first_sweep, 0)
    v2[0:2] = v2[AZ2 : AZ2 + 2]
    v2[AZ2 + 2 : AZ2 + 4] = v2[2:4]

    def residuals(j, carry):
        s = 2 * j + 2
        planes = [both(m2, s + d) for d in (-1, 0, 1, 2)]
        values = [both(v2, s + d) for d in (-1, 0, 1, 2)]
        total = None
        for d in range(2):
            around = level2_around(*values[d : d + 3])
            for p, (w, diagonal) in enumerate(plane(*planes[d : d + 3])):
                r = b2[s + d, p] - diagonal * values[d + 1][p] + weighted(w, around[p])
                total = r if total is None else total + r
        sum_r[j] = total
        return carry

    lax.fori_loop(0, AZ3, residuals, 0)

    half = AZ3 // 2
    row_i, col_i = iota((R2, R2), 0), iota((R2, R2), 1)
    left = (row_i // 2 == col_i).astype(F32)
    right = (row_i // 2 + R2 // 2 == col_i).astype(F32)

    def packed(ref):
        lower = ref[0:half].reshape(half * G2, R2)
        upper = ref[half:AZ3].reshape(half * G2, R2)
        return (dot(lower, left) + dot(upper, right)).reshape(half, G2, R2)

    def wrap(ref):
        ref[0] = pltpu.roll(ref[half], R2 // 2, 1)
        ref[half + 1] = pltpu.roll(ref[1], R2 // 2, 1)

    m3[1 : half + 1] = 0.125 * packed(sum_m)
    wrap(m3)
    b3 = 0.5 * packed(sum_r)
    va[1 : half + 1] = b3
    ca, ri, ro = radial_consts((G2, R2), R2 // 2, 2.0 * math.pi / AZ3, lane % (R2 // 2))
    mp, mc = m3[0], m3[1]
    for i in range(half):
        mn = m3[i + 2]
        w = (
            ca * (mc + mp),
            ca * (mc + mn),
            zlo * (mc + pltpu.roll(mc, 1, 0)),
            zhi * (mc + pltpu.roll(mc, G2 - 1, 0)),
            ri * (mc + pltpu.roll(mc, 1, 1)),
            ro * (mc + pltpu.roll(mc, R2 - 1, 1)),
        )
        diagonal = (w[0] + w[1]) + (w[2] + w[3]) + (w[4] + w[5]) + SIGMA * 64.0
        scale = OMEGA / diagonal
        for f in range(6):
            w3[f, i] = w[f] * scale
        start = va[i + 1] * scale
        w3[6, i] = start
        va[i + 1] = start
        mp, mc = mc, mn
    wrap(va)

    def sweep(src_ref, dst_ref):
        vp, vc = src_ref[0], src_ref[1]
        for i in range(half):
            vn = src_ref[i + 2]
            n = (
                vp,
                vn,
                pltpu.roll(vc, 1, 0),
                pltpu.roll(vc, G2 - 1, 0),
                pltpu.roll(vc, 1, 1),
                pltpu.roll(vc, R2 - 1, 1),
            )
            w = [w3[f, i] for f in range(6)]
            dst_ref[i + 1] = ((1.0 - OMEGA) * vc + w3[6, i]) + weighted(w, n)
            vp, vc = vc, vn
        wrap(dst_ref)

    def two(k, carry):
        sweep(va, vb)
        sweep(vb, va)
        return carry

    lax.fori_loop(0, (COARSE_SWEEPS - 2) // 2, two, 0)
    sweep(va, vb)

    solved = vb[1 : half + 1].reshape(half * G2, R2)
    e2[0:half] = dot(solved, (row_i == col_i // 2).astype(F32)).reshape(half, G2, R2)
    e2[half:AZ3] = dot(solved, (row_i == col_i // 2 + R2 // 2).astype(F32)).reshape(half, G2, R2)

    at = a * A2
    ca, ri, ro = radial_consts((G2, R2), R2, 2.0 * math.pi / AZ2, lane)
    plane = functools.partial(level2_plane, ca, ri, ro, zlo, zhi)
    values = []
    for k in range(A2 + 4):
        e = e2[(a * (A2 // 2) - 1 + k // 2 + AZ3) % AZ3]
        values.append((v2[at + k, 0] + e, v2[at + k, 1] + e))
    for k in range(1, A2 + 3):
        around = level2_around(*values[k - 1 : k + 2])
        for p, (w, diagonal) in enumerate(plane(both(m2, at + k - 1), both(m2, at + k), both(m2, at + k + 1))):
            v = values[k][p]
            r = b2[at + k, p] - diagonal * v + weighted(w, around[p])
            v2f[k - 1, p] = v + OMEGA * r / diagonal

    low, high = jnp.maximum(g - 1, 0), jnp.minimum(g + 1, N_GZ - 1)
    for j in range(A2):
        src[2 * j : 2 * j + 1, :] = v2f[j + 1, 0, pl.ds(g, 1), :]
        src[2 * j + 1 : 2 * j + 2, :] = v2f[j + 1, 1, pl.ds(g, 1), :]
        src[16 + j : 17 + j, :] = v2f[j + 1, 1, pl.ds(low, 1), :]
        src[24 + j : 25 + j, :] = v2f[j + 1, 0, pl.ds(high, 1), :]
    for p in range(2):
        src[32 + p : 33 + p, :] = v2f[0, p, pl.ds(g, 1), :]
        src[34 + p : 35 + p, :] = v2f[A2 + 1, p, pl.ds(g, 1), :]
    src[36:40, :] = jnp.zeros((4, R2), F32)
    o, c = iota((112, 40), 0), iota((112, 40), 1)
    target = jnp.where(
        o < 64,
        (o // 8) * 2 + (o % 4) // 2,
        jnp.where(
            o < 96,
            16 + (o - 64) // 2,
            jnp.where(o < 100, 32 + (o - 96) // 2, 34 + (o - 104) // 2),
        ),
    )
    e1 = dot((target == c).astype(F32), dot(src[...], dup_cols(R2)))

    ah, ch = Halo(ax, ac, az, ay), Halo(cx, cc, cz, cy)
    w, diagonal = level1_weights(*mobility1(m1_ref, ah), buf)
    prev, nxt, below, above = halo1(ch)
    v1 = v1_ref[...] + e1[0:64]
    n = level1_around(
        v1, prev + e1[96:100], nxt + e1[104:108], below + e1[64:80], above + e1[80:96], buf
    )
    v1_out[...] = v1 + OMEGA * (b1_ref[...] - diagonal * v1 + weighted(w, n)) / diagonal
    store_faces1(v1_out, sx, sc, sz, sy)


def postsmooth(
    rhs_ref, v_ref, m_ref, v1_ref, ax, ac, az, ay, bx, bc, bz, by, fx, fc, fz, fy, out_ref, sx, sc, sz, sy, e_ref, er
):
    ah, bh, fh = Halo(ax, ac, az, ay), Halo(bx, bc, bz, by), Halo(fx, fc, fz, fy)
    dup = dup_cols(R1)
    rows = A1 * NH
    tall = (iota((rows, A1 * H1), 0) // 2 == iota((rows, A1 * H1), 1)).astype(F32)
    e_ref[...] = dot(tall, dot(v1_ref[...], dup)).reshape(A1, NH, NR)
    prev, nxt, below, above = halo1(fh)
    er[0:A1, :] = dot(below, dup)
    er[A1 : 2 * A1, :] = dot(above, dup)
    tall = (iota((NH, H1), 0) // 2 == iota((NH, H1), 1)).astype(F32)
    er[2 * A1 : 2 * A1 + NH, :] = dot(tall, dot(prev, dup))
    er[2 * A1 + NH : 2 * A1 + 2 * NH, :] = dot(tall, dot(nxt, dup))
    m_of, mb, ma = fine_mobility(m_ref, ah)
    old, ob, oa = fine_values(v_ref, bh)

    def v_of(i):
        if i < 0:
            return old(i) + er[2 * A1 : 2 * A1 + NH, :]
        if i >= NA:
            return old(i) + er[2 * A1 + NH : 2 * A1 + 2 * NH, :]
        return old(i) + e_ref[i // 2]

    def emit(i, diagonal, around, centre):
        out_ref[i] = centre + OMEGA * (rhs_ref[i] - diagonal * centre + around) / diagonal

    fine_walk(
        m_of,
        v_of,
        mb,
        ma,
        lambda i: ob(i) + er[i // 2 : i // 2 + 1, :],
        lambda i: oa(i) + er[A1 + i // 2 : A1 + i // 2 + 1, :],
        emit,
    )
    store_faces(out_ref, sx, sc, sz, sy)


def final(rhs_ref, v_ref, m_ref, ax, ac, az, ay, gx, gc, gz, gy, out_ref):
    ah, gh = Halo(ax, ac, az, ay), Halo(gx, gc, gz, gy)
    m_of, mb, ma = fine_mobility(m_ref, ah)
    v_of, vb, va = fine_values(v_ref, gh)

    def emit(i, diagonal, around, centre):
        out_ref[i] = (rhs_ref[i] - diagonal * centre + around) / diagonal

    fine_walk(m_of, v_of, mb, ma, vb, va, emit)


def swap(x, axis, odd):
    n = lax.axis_size(axis)
    pairs = []
    for i in range(n):
        partner = i ^ 1 if odd == 0 else ((i + 1) % n if i % 2 else (i - 1) % n)
        pairs.append((i, partner))
    return lax.ppermute(x, axis, pairs)


def exchange(sx, sc, sz, sy):
    return swap(sx, "az", 1), swap(sc, "az", 0), swap(sz, "gz", 0), swap(sy, "gz", 1)


def gathered(x):
    groups = [[a * N_GZ + g for a in range(c, N_AZ, 2) for g in range(N_GZ)] for c in range(2)]
    own = lax.all_to_all(x, ("az", "gz"), 0, 0, tiled=True, axis_index_groups=groups)
    own = own.reshape(own.shape[0] * own.shape[1], own.shape[2])
    return own, swap(own, "az", 0)


def faces(planes, rows, width):
    return [struct(planes, width)] * 2 + [struct(rows, width)] * 2


def vmem(*shape):
    return pltpu.VMEM(shape, F32)


def body(pressure, divergence, void_fraction, bubble_volume, bubble_count, bubble_cell):
    block = struct(NA, NH, NR)
    flat1 = struct(A1 * H1, R1)
    cell = bubble_cell.reshape(1, SLOTS)
    volume = bubble_volume.reshape(1, SLOTS)
    pairs = vmem(A1 * NH, NR)
    buf = vmem(A1 * H1 + 16, R1)

    m0, m1, m2, *send = call(
        prepare,
        [block, flat1, struct(A2 * H2, R2)] + faces(3 * NH, 2 * NA + A1, NR),
        (pressure, void_fraction, volume, bubble_count),
        [pairs],
        smem=(3,),
    )
    ha = exchange(*send)
    rhs, v0, *send = call(
        presmooth, [block, block] + faces(NH, NA, NR), (pressure, divergence, m0, cell, *ha)
    )
    hb = exchange(*send)
    b1, v1, *send = call(
        restrict, [flat1, flat1] + faces(H1, A1, R1), (rhs, v0, m0, m1, *ha, *hb), [pairs, buf]
    )
    hc = exchange(*send)
    (copies,) = call(
        restrict1, [struct(64, 2 * A2 * H2, R2)], (b1, v1, m1, m2, *ha, *hc), [buf]
    )
    own, oth = gathered(copies)
    ring = vmem(AZ2 + 4, 2, G2, R2)
    half = AZ3 // 2
    v1, *send = call(
        coarse,
        [flat1] + faces(H1, A1, R1),
        (own, oth, b1, v1, m1, *ha, *hc),
        [
            ring,
            ring,
            ring,
            vmem(AZ3, G2, R2),
            vmem(AZ3, G2, R2),
            vmem(half + 2, G2, R2),
            vmem(7, half, G2, R2),
            vmem(half + 2, G2, R2),
            vmem(half + 2, G2, R2),
            vmem(AZ3, G2, R2),
            vmem(A2 + 2, 2, G2, R2),
            vmem(40, R2),
            buf,
        ],
    )
    hf = exchange(*send)
    out, *send = call(
        postsmooth,
        [block] + faces(NH, NA, NR),
        (rhs, v0, m0, v1, *ha, *hb, *hf),
        [vmem(A1, NH, NR), vmem(2 * A1 + 2 * NH, NR)],
    )
    hg = exchange(*send)
    (scaled,) = call(final, [block], (rhs, out, m0, *ha, *hg))
    return out, scaled


def solution(mesh):
    return jax.shard_map(
        body,
        mesh=mesh,
        in_specs=(
            P("az", "gz", None),
            P("az", "gz", None),
            P("az", "gz", None),
            P(("az", "gz")),
            P(("az", "gz")),
            P(("az", "gz")),
        ),
        out_specs=(P("az", "gz", None), P("az", "gz", None)),
        check_vma=False,
    )
```

```python
import functools
import math

import jax
import jax.numpy as jnp
from jax import lax
from jax.experimental import pallas as pl
from jax.experimental.pallas import tpu as pltpu
from jax.sharding import PartitionSpec as P

SIGMA = 0.02
OMEGA = 0.8
COARSE_SWEEPS = 32
F32 = jnp.float32

NA, NH, NR = 32, 8, 512
A1, H1, R1 = 16, 4, 256
A2, H2, R2 = 8, 2, 128
AZ2, G2 = 128, 8
AZ3 = 64
N_AZ, N_GZ = 16, 8
SLOTS = 128


def struct(*shape):
    return jax.ShapeDtypeStruct(shape, F32)


def call(kernel, outs, ins, scratch=(), smem=(), hbm=(), hbm_out=(), limit=48):
    def space(i, far):
        return pltpu.HBM if i in far else pltpu.SMEM if i in smem else pltpu.VMEM

    specs = [pl.BlockSpec(memory_space=space(i, hbm)) for i in range(len(ins))]
    return pl.pallas_call(
        kernel,
        out_shape=outs,
        in_specs=specs,
        out_specs=[
            pl.BlockSpec(memory_space=pltpu.HBM if i in hbm_out else pltpu.VMEM)
            for i in range(len(outs))
        ],
        scratch_shapes=list(scratch),
        compiler_params=pltpu.CompilerParams(vmem_limit_bytes=limit * 1024 * 1024),
    )(*ins)


def iota(shape, dim):
    return lax.broadcasted_iota(jnp.int32, shape, dim)


def dot(a, b):
    return jnp.dot(a, b, precision=lax.Precision.HIGHEST, preferred_element_type=F32)


def radial_consts(shape, size, step, rad):
    i = rad.astype(F32)
    metric = ((i + 0.5) * step) ** 2
    ca = 0.5 / metric
    ri = jnp.where(rad > 0, 0.5 * i / (i + 0.5), 0.0)
    ro = jnp.where(rad < size - 1, 0.5 * (i + 1.0) / (i + 0.5), 0.0)
    return ca, ri, ro


def pair_cols(n):
    return (iota((n, n // 2), 0) // 2 == iota((n, n // 2), 1)).astype(F32)


def dup_cols(n):
    return (iota((n, 2 * n), 0) == iota((n, 2 * n), 1) // 2).astype(F32)


def pair_rows_h(rows):
    return (iota((rows // 2, rows), 1) // 2 == iota((rows // 2, rows), 0)).astype(F32)


def block_rows(az, ht):
    out = (az // 2) * (ht // 2)
    r = iota((out, az * ht), 1)
    o = iota((out, az * ht), 0)
    target = (r // (2 * ht)) * (ht // 2) + (r % ht) // 2
    return (target == o).astype(F32)


def position():
    return lax.axis_index("az"), lax.axis_index("gz")


def pick(par, even, odd):
    return jnp.where(par == 0, even, odd)


class Halo:
    def __init__(self, x_ref, c_ref, z_ref, y_ref):
        a, g = position()
        self.pa, self.pg = a % 2, g % 2
        self.x, self.c, self.z, self.y = x_ref, c_ref, z_ref, y_ref

    def prev(self, rows, lanes):
        return pick(self.pa, self.x[rows, lanes], self.c[rows, lanes])

    def next(self, rows, lanes):
        return pick(self.pa, self.c[rows, lanes], self.x[rows, lanes])

    def below(self, rows, lanes):
        return pick(self.pg, self.y[rows, lanes], self.z[rows, lanes])

    def above(self, rows, lanes):
        return pick(self.pg, self.z[rows, lanes], self.y[rows, lanes])


def fine_walk(m_of, v_of, mb, ma, vb, va, emit):
    a, g = position()
    sub = iota((NH, NR), 0)
    lane = iota((NH, NR), 1)
    ca, ri, ro = radial_consts((NH, NR), NR, 2.0 * math.pi / (NA * N_AZ), lane)
    zlo = jnp.where((sub == 0) & (g == 0), 0.0, 0.5)
    zhi = jnp.where((sub == NH - 1) & (g == N_GZ - 1), 0.0, 0.5)
    first, final = sub == 0, sub == NH - 1
    mp, mc = m_of(-1), m_of(0)
    vp, vc = v_of(-1), v_of(0)
    wa = ca * (mp + mc)
    for i in range(NA):
        mn, vn = m_of(i + 1), v_of(i + 1)
        wan = ca * (mc + mn)
        m_lo = jnp.where(first, mb(i), pltpu.roll(mc, 1, 0))
        m_hi = jnp.where(final, ma(i), pltpu.roll(mc, NH - 1, 0))
        v_lo = jnp.where(first, vb(i), pltpu.roll(vc, 1, 0))
        v_hi = jnp.where(final, va(i), pltpu.roll(vc, NH - 1, 0))
        wl, wh = zlo * (mc + m_lo), zhi * (mc + m_hi)
        wi = ri * (mc + pltpu.roll(mc, 1, 1))
        wo = ro * (mc + pltpu.roll(mc, NR - 1, 1))
        diagonal = (wa + wan) + (wl + wh) + (wi + wo) + SIGMA
        around = (wa * vp + wan * vn) + (wl * v_lo + wh * v_hi)
        around = around + (wi * pltpu.roll(vc, 1, 1) + wo * pltpu.roll(vc, NR - 1, 1))
        emit(i, diagonal, around, vc)
        mp, mc, vp, vc, wa = mc, mn, vc, vn, wan


def level1_weights(m, prev, nxt, below, above, buf):
    a, g = position()
    rows = A1 * H1
    sub = iota((rows, R1), 0)
    lane = iota((rows, R1), 1)
    ht = sub % H1
    ca, ri, ro = radial_consts((rows, R1), R1, 2.0 * math.pi / (A1 * N_AZ), lane)
    zlo = jnp.where((ht == 0) & (g == 0), 0.0, 0.5)
    zhi = jnp.where((ht == H1 - 1) & (g == N_GZ - 1), 0.0, 0.5)
    mp, mn, ml, mh, mi, mo = level1_around(m, prev, nxt, below, above, buf)
    w = (ca * (m + mp), ca * (m + mn), zlo * (m + ml), zhi * (m + mh), ri * (m + mi), ro * (m + mo))
    diagonal = (w[0] + w[1]) + (w[2] + w[3]) + (w[4] + w[5]) + SIGMA * 4.0
    return w, diagonal


def level1_around(x, prev, nxt, below, above, buf):
    rows = A1 * H1
    ht = iota((rows, R1), 0) % H1
    spread = (iota((rows, A1), 0) // H1 == iota((rows, A1), 1)).astype(F32)
    buf[8 : 8 + rows, :] = x
    buf[8 - H1 : 8, :] = prev
    buf[8 + rows : 8 + rows + H1, :] = nxt
    xp = buf[8 - H1 : 8 - H1 + rows, :]
    xn = buf[8 + H1 : 8 + H1 + rows, :]
    xl = jnp.where(ht == 0, dot(spread, below), pltpu.roll(x, 1, 0))
    xh = jnp.where(ht == H1 - 1, dot(spread, above), pltpu.roll(x, rows - 1, 0))
    return xp, xn, xl, xh, pltpu.roll(x, 1, 1), pltpu.roll(x, R1 - 1, 1)


def weighted(w, n):
    return (w[0] * n[0] + w[1] * n[1]) + (w[2] * n[2] + w[3] * n[3]) + (w[4] * n[4] + w[5] * n[5])


ALL = slice(None)


def store_faces(ref, x_ref, c_ref, z_ref, y_ref, planes_at=0, rows_at=0):
    a, g = position()
    pa, pg = a % 2, g % 2
    c_plane = jnp.where(pa == 0, NA - 1, 0)
    x_plane = NA - 1 - c_plane
    c_ref[planes_at : planes_at + NH, :] = ref[c_plane]
    x_ref[planes_at : planes_at + NH, :] = ref[x_plane]
    z_row = jnp.where(pg == 0, NH - 1, 0)
    y_row = NH - 1 - z_row
    for i in range(NA):
        z_ref[rows_at + i : rows_at + i + 1, :] = ref[i, pl.ds(z_row, 1), :]
        y_ref[rows_at + i : rows_at + i + 1, :] = ref[i, pl.ds(y_row, 1), :]


def store_faces1(ref, x_ref, c_ref, z_ref, y_ref, planes_at=0, rows_at=0):
    a, g = position()
    pa, pg = a % 2, g % 2
    rows = A1 * H1
    lo, hi = ref[0:H1, :], ref[rows - H1 : rows, :]
    c_ref[planes_at : planes_at + H1, 0:R1] = pick(pa, hi, lo)
    x_ref[planes_at : planes_at + H1, 0:R1] = pick(pa, lo, hi)
    for i in range(A1):
        low, high = ref[H1 * i : H1 * i + 1, :], ref[H1 * i + H1 - 1 : H1 * i + H1, :]
        z_ref[rows_at + i : rows_at + i + 1, 0:R1] = pick(pg, high, low)
        y_ref[rows_at + i : rows_at + i + 1, 0:R1] = pick(pg, low, high)


def prepare(
    p_hbm, void_hbm, vol_hbm, cell_hbm, cnt_ref,
    m0_ref, m1_ref, m2_ref, cell_ref, sx, sc, sz, sy,
    p_ref, void_ref, vol_ref, pairs, sems,
):
    part = NA // 4
    copies = [
        pltpu.make_async_copy(
            src.at[pl.ds(k * part, part)], dst.at[pl.ds(k * part, part)], sems.at[4 * n + k]
        )
        for n, (src, dst) in enumerate(((void_hbm, void_ref), (p_hbm, p_ref)))
        for k in range(4)
    ]
    copies.append(pltpu.make_async_copy(vol_hbm, vol_ref, sems.at[8]))
    copies.append(pltpu.make_async_copy(cell_hbm, cell_ref, sems.at[9]))
    for copy in copies:
        copy.start()
    zero = jnp.zeros((NH, NR), F32)
    sx[2 * NH : 3 * NH, :] = zero
    sc[2 * NH : 3 * NH, :] = zero
    for ref in (sz, sy):
        ref[2 * NA : 2 * NA + A1, R1:NR] = jnp.zeros((A1, NR - R1), F32)
    for i in range(0, NA, 2):
        if i % part == 0:
            copies[i // part].wait()
        u = 1.0 / (1.0 - void_ref[i])
        v = 1.0 / (1.0 - void_ref[i + 1])
        m0_ref[i] = u
        m0_ref[i + 1] = v
        pairs[(i // 2) * NH : (i // 2 + 1) * NH, :] = u + v
    m1 = 0.125 * dot(pair_rows_h(A1 * NH), dot(pairs[...], pair_cols(NR)))
    m1_ref[...] = m1
    m2 = 0.125 * dot(block_rows(A1, H1), dot(m1, pair_cols(R1)))
    for k in range(m2_ref.shape[0]):
        m2_ref[k] = m2
    for copy in copies[4:]:
        copy.wait()
    store_faces(p_ref, sx, sc, sz, sy, 0, 0)
    store_faces(m0_ref, sx, sc, sz, sy, NH, NA)
    store_faces1(m1_ref, sx, sc, sz, sy, 2 * NH, 2 * NA)
    live = jnp.where(iota((1, SLOTS), 1) < cnt_ref[0], vol_ref[...], 0.0)
    sx[2 * NH + H1 : 2 * NH + H1 + 1, 0:SLOTS] = live
    sc[2 * NH + H1 : 2 * NH + H1 + 1, 0:SLOTS] = live


def fine_mobility(m_ref, ah):
    def m_of(i):
        if i < 0:
            return ah.prev(slice(NH, 2 * NH), ALL)
        if i >= NA:
            return ah.next(slice(NH, 2 * NH), ALL)
        return m_ref[i]

    return (
        m_of,
        lambda i: ah.below(slice(NA + i, NA + i + 1), ALL),
        lambda i: ah.above(slice(NA + i, NA + i + 1), ALL),
    )


def fine_values(v_ref, vh):
    def v_of(i):
        if i < 0:
            return vh.prev(slice(0, NH), ALL)
        if i >= NA:
            return vh.next(slice(0, NH), ALL)
        return v_ref[i]

    return (
        v_of,
        lambda i: vh.below(slice(i, i + 1), ALL),
        lambda i: vh.above(slice(i, i + 1), ALL),
    )


def presmooth(p_ref, div_ref, m_ref, cell_ref, ax, ac, az, ay, rhs_ref, v_ref, sx, sc, sz, sy):
    ah = Halo(ax, ac, az, ay)
    arrived = ah.prev(slice(2 * NH + H1, 2 * NH + H1 + 1), slice(0, SLOTS))
    cell = cell_ref[...]
    plane_hot = (iota((NA * NH, SLOTS), 0) == lax.shift_right_logical(cell, 9)).astype(F32)
    radius_hot = jnp.where(iota((NR, SLOTS), 0) == (cell & (NR - 1)), arrived, 0.0)
    deposit = lax.dot_general(
        plane_hot,
        radius_hot,
        (((1,), (1,)), ((), ())),
        precision=lax.Precision.HIGHEST,
        preferred_element_type=F32,
    )
    rhs_ref[...] = div_ref[...] + deposit.reshape(NA, NH, NR)
    m_of, mb, ma = fine_mobility(m_ref, ah)
    v_of, vb, va = fine_values(p_ref, ah)

    def emit(i, diagonal, around, centre):
        v_ref[i] = (1.0 - OMEGA) * centre + OMEGA * (rhs_ref[i] + around) / diagonal

    fine_walk(m_of, v_of, mb, ma, vb, va, emit)
    store_faces(v_ref, sx, sc, sz, sy)


def mobility1(m1_ref, ah):
    return (
        m1_ref[...],
        ah.prev(slice(2 * NH, 2 * NH + H1), slice(0, R1)),
        ah.next(slice(2 * NH, 2 * NH + H1), slice(0, R1)),
        ah.below(slice(2 * NA, 2 * NA + A1), slice(0, R1)),
        ah.above(slice(2 * NA, 2 * NA + A1), slice(0, R1)),
    )


def restrict(
    rhs_ref, v_ref, m_ref, m1_ref, ax, ac, az, ay, bx, bc, bz, by, b1_ref, v1_ref, sx, sc, sz, sy, pairs, buf
):
    ah, bh = Halo(ax, ac, az, ay), Halo(bx, bc, bz, by)
    m_of, mb, ma = fine_mobility(m_ref, ah)
    v_of, vb, va = fine_values(v_ref, bh)
    kept = []

    def emit(i, diagonal, around, centre):
        r = rhs_ref[i] - diagonal * centre + around
        if i % 2 == 0:
            kept.append(r)
        else:
            pairs[(i // 2) * NH : (i // 2 + 1) * NH, :] = kept.pop() + r

    fine_walk(m_of, v_of, mb, ma, vb, va, emit)
    b1 = 0.5 * dot(pair_rows_h(A1 * NH), dot(pairs[...], pair_cols(NR)))
    b1_ref[...] = b1
    _, diagonal = level1_weights(*mobility1(m1_ref, ah), buf)
    v1_ref[...] = OMEGA * b1 / diagonal
    store_faces1(v1_ref, sx, sc, sz, sy)


def halo1(h):
    return (
        h.prev(slice(0, H1), ALL),
        h.next(slice(0, H1), ALL),
        h.below(slice(0, A1), ALL),
        h.above(slice(0, A1), ALL),
    )


def restrict1(b1_ref, v1_ref, m1_ref, ax, ac, az, ay, cx, cc, cz, cy, out_ref, buf):
    ah, ch = Halo(ax, ac, az, ay), Halo(cx, cc, cz, cy)
    w, _ = level1_weights(*mobility1(m1_ref, ah), buf)
    n = level1_around(v1_ref[...], *halo1(ch), buf)
    r1 = (1.0 - OMEGA) * b1_ref[...] + weighted(w, n)
    b2 = 0.5 * dot(block_rows(A1, H1), dot(r1, pair_cols(R1)))
    for k in range(out_ref.shape[0]):
        out_ref[k] = b2


def level2_plane(consts, face, mc, mn):
    ca, ri, ro, zlo, zhi = consts
    mid = 0.5 * (mc[0] + mc[1])
    lows = (zlo * (mc[0] + pltpu.roll(mc[1], 1, 0)), mid)
    highs = (mid, zhi * (mc[1] + pltpu.roll(mc[0], G2 - 1, 0)))
    nxt = level2_face(consts, mc, mn)
    out = []
    for p in range(2):
        m = mc[p]
        wi, wo = ri * (m + pltpu.roll(m, 1, 1)), ro * (m + pltpu.roll(m, R2 - 1, 1))
        out.append((face[p], nxt[p], lows[p], highs[p], wi, wo))
    return out, nxt


def level2_face(consts, mp, mc):
    return (consts[0] * (mp[0] + mc[0]), consts[0] * (mp[1] + mc[1]))


def level2_around(vp, vc, vn):
    lows = (pltpu.roll(vc[1], 1, 0), vc[0])
    highs = (vc[1], pltpu.roll(vc[0], G2 - 1, 0))
    return [
        (vp[p], vn[p], lows[p], highs[p], pltpu.roll(vc[p], 1, 1), pltpu.roll(vc[p], R2 - 1, 1))
        for p in range(2)
    ]


def total_weight(w):
    return (w[0] + w[1]) + (w[2] + w[3]) + (w[4] + w[5])


def height_walls():
    sub = iota((G2, R2), 0)
    return jnp.where(sub == 0, 0.0, 0.5), jnp.where(sub == G2 - 1, 0.0, 0.5)


def level2_consts():
    lane = iota((G2, R2), 1)
    return radial_consts((G2, R2), R2, 2.0 * math.pi / AZ2, lane) + height_walls()


def both(ref, s):
    return (ref[s, 0], ref[s, 1])


def close_ring(ref):
    ref[0:2] = ref[AZ2 : AZ2 + 2]
    ref[AZ2 + 2 : AZ2 + 4] = ref[2:4]


HALF = AZ3 // 2


def packed(ref):
    row_i, col_i = iota((R2, R2), 0), iota((R2, R2), 1)
    left = (row_i // 2 == col_i).astype(F32)
    right = (row_i // 2 + R2 // 2 == col_i).astype(F32)
    lower = ref[0:HALF].reshape(HALF * G2, R2)
    upper = ref[HALF:AZ3].reshape(HALF * G2, R2)
    return (dot(lower, left) + dot(upper, right)).reshape(HALF, G2, R2)


def wrap(ref):
    ref[0] = pltpu.roll(ref[HALF], R2 // 2, 1)
    ref[HALF + 1] = pltpu.roll(ref[1], R2 // 2, 1)


STEP = 8


def coarse_weights(own, oth, m2, d2, w3, sum_m, m3):
    a, g = position()
    pa = a % 2
    rows = A2 * H2
    for k in range(N_AZ):
        base = (k // 2) * N_GZ * rows
        first, second = (own, oth) if k % 2 == 0 else (oth, own)
        for i in range(A2):
            for p in range(2):
                at = pl.ds(base + i * 2 + p, G2, stride=rows)
                m2[k * A2 + i + 2, p] = pick(pa, first[at, :], second[at, :])
    close_ring(m2)
    consts = level2_consts()

    def diagonals(k, carry):
        s = STEP * k + 2
        mp, mc = both(m2, s - 1), both(m2, s)
        face = level2_face(consts, mp, mc)
        for d in range(STEP):
            mn = both(m2, s + d + 1)
            w, face = level2_plane(consts, face, mc, mn)
            for p in range(2):
                d2[s + d, p] = OMEGA / (total_weight(w[p]) + SIGMA * 16.0)
            if d % 2:
                sum_m[(STEP // 2) * k + d // 2] = (mp[0] + mp[1]) + (mc[0] + mc[1])
            mp, mc = mc, mn
        return carry

    lax.fori_loop(0, AZ2 // STEP, diagonals, 0)
    close_ring(d2)
    m3[1 : HALF + 1] = 0.125 * packed(sum_m)
    wrap(m3)
    lane = iota((G2, R2), 1) % (R2 // 2)
    ca, ri, ro = radial_consts((G2, R2), R2 // 2, 2.0 * math.pi / AZ3, lane)
    zlo, zhi = height_walls()
    mp, mc = m3[0], m3[1]
    for i in range(HALF):
        mn = m3[i + 2]
        w = (
            ca * (mc + mp),
            ca * (mc + mn),
            zlo * (mc + pltpu.roll(mc, 1, 0)),
            zhi * (mc + pltpu.roll(mc, G2 - 1, 0)),
            ri * (mc + pltpu.roll(mc, 1, 1)),
            ro * (mc + pltpu.roll(mc, R2 - 1, 1)),
        )
        scale = OMEGA / (total_weight(w) + SIGMA * 64.0)
        for f in range(6):
            w3[f, i] = w[f] * scale
        w3[6, i] = scale
        mp, mc = mc, mn


def coarse(
    own, oth, m2, d2, w3, b1_ref, v1_ref, m1_ref, ax, ac, az, ay, cx, cc, cz, cy,
    v1_out, sx, sc, sz, sy,
    b2, v2, sum_r, add, va, vb, e2, v2f, src, buf,
):
    a, g = position()
    pa = a % 2
    rows = A2 * H2

    for k in range(N_AZ):
        base = (k // 2) * N_GZ * rows
        first, second = (own, oth) if k % 2 == 0 else (oth, own)
        for i in range(A2):
            for p in range(2):
                at = pl.ds(base + i * 2 + p, G2, stride=rows)
                b = pick(pa, first[at, :], second[at, :])
                b2[k * A2 + i + 2, p] = b
                v2[k * A2 + i + 2, p] = b * d2[k * A2 + i + 2, p]
    close_ring(b2)
    close_ring(v2)
    consts = level2_consts()

    def residuals(k, carry):
        s = STEP * k + 2
        mc = both(m2, s)
        vp, vc = both(v2, s - 1), both(v2, s)
        face = level2_face(consts, both(m2, s - 1), mc)
        total = None
        for d in range(STEP):
            mn, vn = both(m2, s + d + 1), both(v2, s + d + 1)
            w, face = level2_plane(consts, face, mc, mn)
            n = level2_around(vp, vc, vn)
            b = both(b2, s + d)
            r = ((1.0 - OMEGA) * (b[0] + b[1]) + weighted(w[0], n[0])) + weighted(w[1], n[1])
            if d % 2:
                sum_r[(STEP // 2) * k + d // 2] = total + r
            total, mc, vp, vc = r, mn, vc, vn
        return carry

    lax.fori_loop(0, AZ2 // STEP, residuals, 0)

    b3 = 0.5 * packed(sum_r)
    for i in range(HALF):
        start = b3[i] * w3[6, i]
        add[i] = start
        va[i + 1] = start
    wrap(va)

    def sweep(src_ref, dst_ref):
        vp, vc = src_ref[0], src_ref[1]
        for i in range(HALF):
            vn = src_ref[i + 2]
            n = (
                vp,
                vn,
                pltpu.roll(vc, 1, 0),
                pltpu.roll(vc, G2 - 1, 0),
                pltpu.roll(vc, 1, 1),
                pltpu.roll(vc, R2 - 1, 1),
            )
            w = [w3[f, i] for f in range(6)]
            dst_ref[i + 1] = ((1.0 - OMEGA) * vc + add[i]) + weighted(w, n)
            vp, vc = vc, vn
        wrap(dst_ref)

    def two(k, carry):
        sweep(va, vb)
        sweep(vb, va)
        return carry

    lax.fori_loop(0, (COARSE_SWEEPS - 2) // 2, two, 0)
    sweep(va, vb)

    row_i, col_i = iota((R2, R2), 0), iota((R2, R2), 1)
    solved = vb[1 : HALF + 1].reshape(HALF * G2, R2)
    e2[0:HALF] = dot(solved, (row_i == col_i // 2).astype(F32)).reshape(HALF, G2, R2)
    e2[HALF:AZ3] = dot(solved, (row_i == col_i // 2 + R2 // 2).astype(F32)).reshape(HALF, G2, R2)

    at = a * A2
    values = []
    for k in range(A2 + 4):
        e = e2[(a * (A2 // 2) - 1 + k // 2 + AZ3) % AZ3]
        values.append((v2[at + k, 0] + e, v2[at + k, 1] + e))
    mc = both(m2, at + 1)
    face = level2_face(consts, both(m2, at), mc)
    for k in range(1, A2 + 3):
        mn = both(m2, at + k + 1)
        w, face = level2_plane(consts, face, mc, mn)
        n = level2_around(*values[k - 1 : k + 2])
        for p in range(2):
            gain = b2[at + k, p] + weighted(w[p], n[p])
            v2f[k - 1, p] = (1.0 - OMEGA) * values[k][p] + d2[at + k, p] * gain
        mc = mn

    low, high = jnp.maximum(g - 1, 0), jnp.minimum(g + 1, N_GZ - 1)
    for j in range(A2):
        src[2 * j : 2 * j + 1, :] = v2f[j + 1, 0, pl.ds(g, 1), :]
        src[2 * j + 1 : 2 * j + 2, :] = v2f[j + 1, 1, pl.ds(g, 1), :]
        src[16 + j : 17 + j, :] = v2f[j + 1, 1, pl.ds(low, 1), :]
        src[24 + j : 25 + j, :] = v2f[j + 1, 0, pl.ds(high, 1), :]
    for p in range(2):
        src[32 + p : 33 + p, :] = v2f[0, p, pl.ds(g, 1), :]
        src[34 + p : 35 + p, :] = v2f[A2 + 1, p, pl.ds(g, 1), :]
    src[36:40, :] = jnp.zeros((4, R2), F32)
    o, c = iota((112, 40), 0), iota((112, 40), 1)
    target = jnp.where(
        o < 64,
        (o // 8) * 2 + (o % 4) // 2,
        jnp.where(
            o < 96,
            16 + (o - 64) // 2,
            jnp.where(o < 100, 32 + (o - 96) // 2, 34 + (o - 104) // 2),
        ),
    )
    e1 = dot((target == c).astype(F32), dot(src[...], dup_cols(R2)))

    ah, ch = Halo(ax, ac, az, ay), Halo(cx, cc, cz, cy)
    w, diagonal = level1_weights(*mobility1(m1_ref, ah), buf)
    prev, nxt, below, above = halo1(ch)
    v1 = v1_ref[...] + e1[0:64]
    n = level1_around(
        v1, prev + e1[96:100], nxt + e1[104:108], below + e1[64:80], above + e1[80:96], buf
    )
    v1_out[...] = (1.0 - OMEGA) * v1 + OMEGA * (b1_ref[...] + weighted(w, n)) / diagonal
    store_faces1(v1_out, sx, sc, sz, sy)


def postsmooth(
    rhs_ref, v_ref, m_ref, v1_ref, ax, ac, az, ay, bx, bc, bz, by, fx, fc, fz, fy, out_ref, sx, sc, sz, sy, e_ref, er
):
    ah, bh, fh = Halo(ax, ac, az, ay), Halo(bx, bc, bz, by), Halo(fx, fc, fz, fy)
    dup = dup_cols(R1)
    rows = A1 * NH
    tall = (iota((rows, A1 * H1), 0) // 2 == iota((rows, A1 * H1), 1)).astype(F32)
    e_ref[...] = dot(tall, dot(v1_ref[...], dup)).reshape(A1, NH, NR)
    prev, nxt, below, above = halo1(fh)
    er[0:A1, :] = dot(below, dup)
    er[A1 : 2 * A1, :] = dot(above, dup)
    tall = (iota((NH, H1), 0) // 2 == iota((NH, H1), 1)).astype(F32)
    er[2 * A1 : 2 * A1 + NH, :] = dot(tall, dot(prev, dup))
    er[2 * A1 + NH : 2 * A1 + 2 * NH, :] = dot(tall, dot(nxt, dup))
    m_of, mb, ma = fine_mobility(m_ref, ah)
    old, ob, oa = fine_values(v_ref, bh)

    def v_of(i):
        if i < 0:
            return old(i) + er[2 * A1 : 2 * A1 + NH, :]
        if i >= NA:
            return old(i) + er[2 * A1 + NH : 2 * A1 + 2 * NH, :]
        return old(i) + e_ref[i // 2]

    def emit(i, diagonal, around, centre):
        out_ref[i] = (1.0 - OMEGA) * centre + OMEGA * (rhs_ref[i] + around) / diagonal

    fine_walk(
        m_of,
        v_of,
        mb,
        ma,
        lambda i: ob(i) + er[i // 2 : i // 2 + 1, :],
        lambda i: oa(i) + er[A1 + i // 2 : A1 + i // 2 + 1, :],
        emit,
    )
    store_faces(out_ref, sx, sc, sz, sy)


def final(rhs_ref, v_ref, m_ref, ax, ac, az, ay, gx, gc, gz, gy, p_hbm, out_hbm, out_ref, sems):
    part = NA // 4
    copies = [
        pltpu.make_async_copy(
            src.at[pl.ds(k * part, part)], dst.at[pl.ds(k * part, part)], sems.at[4 * n + k]
        )
        for n, (src, dst) in enumerate(((v_ref, p_hbm), (out_ref, out_hbm)))
        for k in range(4)
    ]
    for copy in copies[:4]:
        copy.start()
    ah, gh = Halo(ax, ac, az, ay), Halo(gx, gc, gz, gy)
    m_of, mb, ma = fine_mobility(m_ref, ah)
    v_of, vb, va = fine_values(v_ref, gh)

    def emit(i, diagonal, around, centre):
        out_ref[i] = (rhs_ref[i] - diagonal * centre + around) / diagonal
        if i % part == part - 1:
            copies[4 + i // part].start()

    fine_walk(m_of, v_of, mb, ma, vb, va, emit)
    for copy in copies:
        copy.wait()


def swap(x, axis, odd):
    n = lax.axis_size(axis)
    pairs = []
    for i in range(n):
        partner = i ^ 1 if odd == 0 else ((i + 1) % n if i % 2 else (i - 1) % n)
        pairs.append((i, partner))
    return lax.ppermute(x, axis, pairs)


def exchange(sx, sc, sz, sy):
    return swap(sx, "az", 1), swap(sc, "az", 0), swap(sz, "gz", 0), swap(sy, "gz", 1)


def gathered(x):
    groups = [[a * N_GZ + g for a in range(c, N_AZ, 2) for g in range(N_GZ)] for c in range(2)]
    own = lax.all_to_all(x, ("az", "gz"), 0, 0, tiled=True, axis_index_groups=groups)
    own = own.reshape(own.shape[0] * own.shape[1], own.shape[2])
    return own, swap(own, "az", 0)


def faces(planes, rows, width):
    return [struct(planes, width)] * 2 + [struct(rows, width)] * 2


def vmem(*shape):
    return pltpu.VMEM(shape, F32)


def body(pressure, divergence, void_fraction, bubble_volume, bubble_count, bubble_cell):
    block = struct(NA, NH, NR)
    flat1 = struct(A1 * H1, R1)
    cell = bubble_cell.reshape(1, SLOTS)
    volume = bubble_volume.reshape(1, SLOTS)
    pairs = vmem(A1 * NH, NR)
    buf = vmem(A1 * H1 + 16, R1)

    spread = struct(64, A2 * H2, R2)
    m0, m1, m2, cell, *send = call(
        prepare,
        [block, flat1, spread, jax.ShapeDtypeStruct((1, SLOTS), jnp.int32)]
        + faces(3 * NH, 2 * NA + A1, NR),
        (pressure, void_fraction, volume, cell, bubble_count),
        [
            vmem(NA, NH, NR),
            vmem(NA, NH, NR),
            vmem(1, SLOTS),
            pairs,
            pltpu.SemaphoreType.DMA((10,)),
        ],
        smem=(4,),
        hbm=(0, 1, 2, 3),
    )
    ha = exchange(*send)
    ring = (AZ2 + 4, 2, G2, R2)
    m2, d2, w3 = call(
        coarse_weights,
        [struct(*ring), struct(*ring), struct(7, HALF, G2, R2)],
        gathered(m2),
        [vmem(AZ3, G2, R2), vmem(HALF + 2, G2, R2)],
    )
    rhs, v0, *send = call(
        presmooth, [block, block] + faces(NH, NA, NR), (pressure, divergence, m0, cell, *ha)
    )
    hb = exchange(*send)
    b1, v1, *send = call(
        restrict, [flat1, flat1] + faces(H1, A1, R1), (rhs, v0, m0, m1, *ha, *hb), [pairs, buf]
    )
    hc = exchange(*send)
    (copies,) = call(restrict1, [spread], (b1, v1, m1, *ha, *hc), [buf])
    v1, *send = call(
        coarse,
        [flat1] + faces(H1, A1, R1),
        (*gathered(copies), m2, d2, w3, b1, v1, m1, *ha, *hc),
        [
            vmem(*ring),
            vmem(*ring),
            vmem(AZ3, G2, R2),
            vmem(HALF, G2, R2),
            vmem(HALF + 2, G2, R2),
            vmem(HALF + 2, G2, R2),
            vmem(AZ3, G2, R2),
            vmem(A2 + 2, 2, G2, R2),
            vmem(40, R2),
            buf,
        ],
    )
    hf = exchange(*send)
    out, *send = call(
        postsmooth,
        [block] + faces(NH, NA, NR),
        (rhs, v0, m0, v1, *ha, *hb, *hf),
        [vmem(A1, NH, NR), vmem(2 * A1 + 2 * NH, NR)],
    )
    hg = exchange(*send)
    return tuple(
        call(
            final,
            [block, block],
            (rhs, out, m0, *ha, *hg),
            [vmem(NA, NH, NR), pltpu.SemaphoreType.DMA((8,))],
            hbm_out=(0, 1),
        )
    )


def solution(mesh):
    return jax.shard_map(
        body,
        mesh=mesh,
        in_specs=(
            P("az", "gz", None),
            P("az", "gz", None),
            P("az", "gz", None),
            P(("az", "gz")),
            P(("az", "gz")),
            P(("az", "gz")),
        ),
        out_specs=(P("az", "gz", None), P("az", "gz", None)),
        check_vma=False,
    )
```

```python
import functools
import math

import jax
import jax.numpy as jnp
from jax import lax
from jax.experimental import pallas as pl
from jax.experimental.pallas import tpu as pltpu
from jax.sharding import PartitionSpec as P

SIGMA = 0.02
OMEGA = 0.8
COARSE_SWEEPS = 32
F32 = jnp.float32

NA, NH, NR = 32, 8, 512
A1, H1, R1 = 16, 4, 256
A2, H2, R2 = 8, 2, 128
AZ2, G2 = 128, 8
AZ3 = 64
N_AZ, N_GZ = 16, 8
SLOTS = 128


def struct(*shape):
    return jax.ShapeDtypeStruct(shape, F32)


def call(kernel, outs, ins, scratch=(), smem=(), hbm=(), hbm_out=(), limit=48):
    def space(i, far):
        return pltpu.HBM if i in far else pltpu.SMEM if i in smem else pltpu.VMEM

    specs = [pl.BlockSpec(memory_space=space(i, hbm)) for i in range(len(ins))]
    return pl.pallas_call(
        kernel,
        out_shape=outs,
        in_specs=specs,
        out_specs=[
            pl.BlockSpec(memory_space=pltpu.HBM if i in hbm_out else pltpu.VMEM)
            for i in range(len(outs))
        ],
        scratch_shapes=list(scratch),
        compiler_params=pltpu.CompilerParams(vmem_limit_bytes=limit * 1024 * 1024),
    )(*ins)


def iota(shape, dim):
    return lax.broadcasted_iota(jnp.int32, shape, dim)


def dot(a, b):
    return jnp.dot(a, b, precision=lax.Precision.HIGHEST, preferred_element_type=F32)


def radial_consts(shape, size, step, rad):
    i = rad.astype(F32)
    metric = ((i + 0.5) * step) ** 2
    ca = 0.5 / metric
    ri = jnp.where(rad > 0, 0.5 * i / (i + 0.5), 0.0)
    ro = jnp.where(rad < size - 1, 0.5 * (i + 1.0) / (i + 0.5), 0.0)
    return ca, ri, ro


def pair_cols(n):
    return (iota((n, n // 2), 0) // 2 == iota((n, n // 2), 1)).astype(F32)


def dup_cols(n):
    return (iota((n, 2 * n), 0) == iota((n, 2 * n), 1) // 2).astype(F32)


def row_sums(planes, out, first, per):
    o, r = iota((planes * out, planes * per), 0), iota((planes * out, planes * per), 1)
    h = r % per - first
    return ((o // out == r // per) & (h >= 0) & (h // 2 == o % out)).astype(F32)


def widened(planes):
    o, r = iota((planes * 8, planes * 8), 0), iota((planes * 8, planes * 8), 1)
    return ((o // 8 == r // 8) & (o % 8 == (r % 8) // 2 + 2)).astype(F32)


def position():
    return lax.axis_index("az"), lax.axis_index("gz")


def pick(par, even, odd):
    return jnp.where(par == 0, even, odd)


class Halo:
    def __init__(self, x_ref, c_ref, z_ref, y_ref):
        a, g = position()
        self.pa, self.pg = a % 2, g % 2
        self.x, self.c, self.z, self.y = x_ref, c_ref, z_ref, y_ref

    def prev(self, rows, lanes):
        return pick(self.pa, self.x[rows, lanes], self.c[rows, lanes])

    def next(self, rows, lanes):
        return pick(self.pa, self.c[rows, lanes], self.x[rows, lanes])

    def below(self, rows, lanes):
        return pick(self.pg, self.y[rows, lanes], self.z[rows, lanes])

    def above(self, rows, lanes):
        return pick(self.pg, self.z[rows, lanes], self.y[rows, lanes])


def fine_walk(m_of, v_of, mb, ma, vb, va, emit):
    a, g = position()
    sub = iota((NH, NR), 0)
    lane = iota((NH, NR), 1)
    ca, ri, ro = radial_consts((NH, NR), NR, 2.0 * math.pi / (NA * N_AZ), lane)
    zlo = jnp.where((sub == 0) & (g == 0), 0.0, 0.5)
    zhi = jnp.where((sub == NH - 1) & (g == N_GZ - 1), 0.0, 0.5)
    first, final = sub == 0, sub == NH - 1
    mp, mc = m_of(-1), m_of(0)
    vp, vc = v_of(-1), v_of(0)
    wa = ca * (mp + mc)
    for i in range(NA):
        mn, vn = m_of(i + 1), v_of(i + 1)
        wan = ca * (mc + mn)
        m_lo = jnp.where(first, mb(i), pltpu.roll(mc, 1, 0))
        m_hi = jnp.where(final, ma(i), pltpu.roll(mc, NH - 1, 0))
        v_lo = jnp.where(first, vb(i), pltpu.roll(vc, 1, 0))
        v_hi = jnp.where(final, va(i), pltpu.roll(vc, NH - 1, 0))
        wl, wh = zlo * (mc + m_lo), zhi * (mc + m_hi)
        wi = ri * (mc + pltpu.roll(mc, 1, 1))
        wo = ro * (mc + pltpu.roll(mc, NR - 1, 1))
        diagonal = (wa + wan) + (wl + wh) + (wi + wo) + SIGMA
        around = (wa * vp + wan * vn) + (wl * v_lo + wh * v_hi)
        around = around + (wi * pltpu.roll(vc, 1, 1) + wo * pltpu.roll(vc, NR - 1, 1))
        emit(i, diagonal, around, vc)
        mp, mc, vp, vc, wa = mc, mn, vc, vn, wan


T1 = 8


def level1_walk(m_of, v_of, first, count, emit):
    a, g = position()
    sub = iota((T1, R1), 0)
    lane = iota((T1, R1), 1)
    height = g * H1 + sub - 2
    ca, ri, ro = radial_consts((T1, R1), R1, 2.0 * math.pi / (A1 * N_AZ), lane)
    zlo = jnp.where(height <= 0, 0.0, 0.5)
    zhi = jnp.where(height >= H1 * N_GZ - 1, 0.0, 0.5)
    mp, mc = m_of(first - 1), m_of(first)
    if v_of is not None:
        vp, vc = v_of(first - 1), v_of(first)
    wa = ca * (mp + mc)
    for i in range(first, first + count):
        mn = m_of(i + 1)
        wan = ca * (mc + mn)
        w = (
            wa,
            wan,
            zlo * (mc + pltpu.roll(mc, 1, 0)),
            zhi * (mc + pltpu.roll(mc, T1 - 1, 0)),
            ri * (mc + pltpu.roll(mc, 1, 1)),
            ro * (mc + pltpu.roll(mc, R1 - 1, 1)),
        )
        diagonal = total_weight(w) + SIGMA * 4.0
        if v_of is None:
            emit(i, diagonal, None, None)
        else:
            vn = v_of(i + 1)
            n = (
                vp,
                vn,
                pltpu.roll(vc, 1, 0),
                pltpu.roll(vc, T1 - 1, 0),
                pltpu.roll(vc, 1, 1),
                pltpu.roll(vc, R1 - 1, 1),
            )
            emit(i, diagonal, weighted(w, n), vc)
            vp, vc = vc, vn
        mp, mc, wa = mc, mn, wan


def weighted(w, n):
    return (w[0] * n[0] + w[1] * n[1]) + (w[2] * n[2] + w[3] * n[3]) + (w[4] * n[4] + w[5] * n[5])


ALL = slice(None)


def store_faces(ref, x_ref, c_ref, z_ref, y_ref, planes_at=0, rows_at=0):
    a, g = position()
    pa, pg = a % 2, g % 2
    c_plane = jnp.where(pa == 0, NA - 1, 0)
    x_plane = NA - 1 - c_plane
    c_ref[planes_at : planes_at + NH, :] = ref[c_plane]
    x_ref[planes_at : planes_at + NH, :] = ref[x_plane]
    z_row = jnp.where(pg == 0, NH - 1, 0)
    y_row = NH - 1 - z_row
    for i in range(NA):
        z_ref[rows_at + i : rows_at + i + 1, :] = ref[i, pl.ds(z_row, 1), :]
        y_ref[rows_at + i : rows_at + i + 1, :] = ref[i, pl.ds(y_row, 1), :]


def prepare(
    p_ref, void_ref, vol_ref, cnt_ref, m0_ref, m1_ref, m2_ref, sx, sc, sz, sy, pairs, halves
):
    a, g = position()
    pa, pg = a % 2, g % 2
    for i in range(0, NA, 2):
        u = 1.0 / (1.0 - void_ref[i])
        v = 1.0 / (1.0 - void_ref[i + 1])
        m0_ref[i] = u
        m0_ref[i + 1] = v
        pairs[(i // 2) * NH : (i // 2 + 1) * NH, :] = u + v
    m1_ref[...] = 0.125 * dot(widened(A1), dot(pairs[...], pair_cols(NR))).reshape(A1, T1, R1)
    for i in range(A2):
        halves[i * T1 : (i + 1) * T1, :] = m1_ref[2 * i] + m1_ref[2 * i + 1]
    m2_ref[...] = 0.125 * dot(row_sums(A2, H2, 2, T1), dot(halves[...], pair_cols(R1)))
    store_faces(p_ref, sx, sc, sz, sy, 0, 0)
    store_faces(m0_ref, sx, sc, sz, sy, NH, NA)
    rest = slice(2 * NH, 3 * NH)
    sx[rest, R1:NR] = jnp.zeros((NH, NR - R1), F32)
    sc[rest, R1:NR] = jnp.zeros((NH, NR - R1), F32)
    c_plane = jnp.where(pa == 0, A1 - 1, 0)
    sc[rest, 0:R1] = m1_ref[c_plane]
    sx[rest, 0:R1] = m1_ref[A1 - 1 - c_plane]
    for ref in (sz, sy):
        ref[2 * NA : 2 * NA + A1, R1:NR] = jnp.zeros((A1, NR - R1), F32)
    z_row = jnp.where(pg == 0, H1 + 1, 2)
    for i in range(A1):
        at = slice(2 * NA + i, 2 * NA + i + 1)
        sz[at, 0:R1] = m1_ref[i, pl.ds(z_row, 1), :]
        sy[at, 0:R1] = m1_ref[i, pl.ds(H1 + 3 - z_row, 1), :]
    live = jnp.where(iota((1, SLOTS), 1) < cnt_ref[0], vol_ref[...], 0.0)
    for ref in (sx, sc):
        ref[2 * NH : 2 * NH + 1, R1 : R1 + SLOTS] = live


def fine_mobility(m_ref, ah):
    def m_of(i):
        if i < 0:
            return ah.prev(slice(NH, 2 * NH), ALL)
        if i >= NA:
            return ah.next(slice(NH, 2 * NH), ALL)
        return m_ref[i]

    return (
        m_of,
        lambda i: ah.below(slice(NA + i, NA + i + 1), ALL),
        lambda i: ah.above(slice(NA + i, NA + i + 1), ALL),
    )


def fine_values(v_ref, vh):
    def v_of(i):
        if i < 0:
            return vh.prev(slice(0, NH), ALL)
        if i >= NA:
            return vh.next(slice(0, NH), ALL)
        return v_ref[i]

    return (
        v_of,
        lambda i: vh.below(slice(i, i + 1), ALL),
        lambda i: vh.above(slice(i, i + 1), ALL),
    )


def presmooth(p_ref, div_ref, m_ref, cell_ref, ax, ac, az, ay, rhs_ref, v_ref, sx, sc, sz, sy):
    ah = Halo(ax, ac, az, ay)
    arrived = ah.prev(slice(2 * NH, 2 * NH + 1), slice(R1, R1 + SLOTS))
    cell = cell_ref[...]
    plane_hot = (iota((NA * NH, SLOTS), 0) == lax.shift_right_logical(cell, 9)).astype(F32)
    radius_hot = jnp.where(iota((NR, SLOTS), 0) == (cell & (NR - 1)), arrived, 0.0)
    deposit = lax.dot_general(
        plane_hot,
        radius_hot,
        (((1,), (1,)), ((), ())),
        precision=lax.Precision.HIGHEST,
        preferred_element_type=F32,
    )
    rhs_ref[...] = div_ref[...] + deposit.reshape(NA, NH, NR)
    m_of, mb, ma = fine_mobility(m_ref, ah)
    v_of, vb, va = fine_values(p_ref, ah)

    def emit(i, diagonal, around, centre):
        v_ref[i] = (1.0 - OMEGA) * centre + OMEGA * (rhs_ref[i] + around) / diagonal

    fine_walk(m_of, v_of, mb, ma, vb, va, emit)
    store_faces(v_ref, sx, sc, sz, sy)


def restrict(
    rhs_ref, v_ref, m_ref, m1_ref, ax, ac, az, ay, bx, bc, bz, by, b1_ref, v1_ref, sz, sy, pairs
):
    ah, bh = Halo(ax, ac, az, ay), Halo(bx, bc, bz, by)
    m_of, mb, ma = fine_mobility(m_ref, ah)
    v_of, vb, va = fine_values(v_ref, bh)
    kept = []

    def emit(i, diagonal, around, centre):
        r = rhs_ref[i] - diagonal * centre + around
        if i % 2 == 0:
            kept.append(r)
        else:
            pairs[(i // 2) * NH : (i // 2 + 1) * NH, :] = kept.pop() + r

    fine_walk(m_of, v_of, mb, ma, vb, va, emit)
    b1_ref[...] = 0.5 * dot(widened(A1), dot(pairs[...], pair_cols(NR))).reshape(A1, T1, R1)

    sub = iota((T1, R1), 0)

    def m1_of(i):
        if i < 0:
            return ah.prev(slice(2 * NH, 3 * NH), slice(0, R1))
        if i >= A1:
            return ah.next(slice(2 * NH, 3 * NH), slice(0, R1))
        at = slice(2 * NA + i, 2 * NA + i + 1)
        below, above = ah.below(at, slice(0, R1)), ah.above(at, slice(0, R1))
        return jnp.where(sub == 1, below, jnp.where(sub == H1 + 2, above, m1_ref[i]))

    def emit1(i, diagonal, around, centre):
        v1_ref[i] = OMEGA * b1_ref[i] / diagonal

    level1_walk(m1_of, None, 0, A1, emit1)
    g = lax.axis_index("gz")
    for layer in range(2):
        z_row = jnp.where(g % 2 == 0, H1 + 1 - layer, 2 + layer)
        y_row = H1 + 3 - z_row
        sources = (v1_ref, m1_ref) if layer else (v1_ref, m1_ref, b1_ref)
        for n, ref in enumerate(sources):
            for i in range(A1):
                at = (2 * n + layer) * A1 + i
                sz[at : at + 1, :] = ref[i, pl.ds(z_row, 1), :]
                sy[at : at + 1, :] = ref[i, pl.ds(y_row, 1), :]


def widen(b1_ref, v1_ref, m1_ref, z_ref, y_ref, vw, mw, bw, sx, sc):
    a, g = position()
    sub = iota((T1, R1), 0)
    halo = Halo(None, None, z_ref, y_ref)
    for n, (src, dst) in enumerate(((v1_ref, vw), (m1_ref, mw), (b1_ref, bw))):
        for i in range(A1):
            tile = src[i]
            for layer in range(2 if n < 2 else 1):
                at = (2 * n + layer) * A1 + i
                at = slice(at, at + 1)
                tile = jnp.where(sub == 1 - layer, halo.below(at, ALL), tile)
                tile = jnp.where(sub == H1 + 2 + layer, halo.above(at, ALL), tile)
            dst[i] = tile
    for layer in range(2):
        c_plane = jnp.where(a % 2 == 0, A1 - 1 - layer, layer)
        x_plane = A1 - 1 - c_plane
        for n, ref in enumerate((vw, mw) if layer else (vw, mw, bw)):
            at = (2 * n + layer) * T1
            sc[at : at + T1, :] = ref[c_plane]
            sx[at : at + T1, :] = ref[x_plane]


def wide_planes(ref, halo, n, i):
    if i < 0:
        at = (2 * n - 1 - i) * T1
        return halo.prev(slice(at, at + T1), ALL)
    if i >= A1:
        at = (2 * n + i - A1) * T1
        return halo.next(slice(at, at + T1), ALL)
    return ref[i]


def restrict1(bw, vw, mw, m2_ref, cx, cc, out_ref, halves):
    halo = Halo(cx, cc, None, None)
    kept = []

    def emit(i, diagonal, around, centre):
        r = (1.0 - OMEGA) * bw[i] + around
        if i % 2 == 0:
            kept.append(r)
        else:
            halves[(i // 2) * T1 : (i // 2 + 1) * T1, :] = kept.pop() + r

    level1_walk(
        lambda i: wide_planes(mw, halo, 1, i), lambda i: wide_planes(vw, halo, 0, i), 0, A1, emit
    )
    b2 = 0.5 * dot(row_sums(A2, H2, 2, T1), dot(halves[...], pair_cols(R1)))
    m2 = m2_ref[...]
    rows = A2 * H2
    for k in range(out_ref.shape[0]):
        out_ref[k, 0:rows, :] = b2
        out_ref[k, rows : 2 * rows, :] = m2


def level2_plane(consts, face, mc, mn):
    ca, ri, ro, zlo, zhi = consts
    mid = 0.5 * (mc[0] + mc[1])
    lows = (zlo * (mc[0] + pltpu.roll(mc[1], 1, 0)), mid)
    highs = (mid, zhi * (mc[1] + pltpu.roll(mc[0], G2 - 1, 0)))
    nxt = level2_face(consts, mc, mn)
    out = []
    for p in range(2):
        m = mc[p]
        wi, wo = ri * (m + pltpu.roll(m, 1, 1)), ro * (m + pltpu.roll(m, R2 - 1, 1))
        out.append((face[p], nxt[p], lows[p], highs[p], wi, wo))
    return out, nxt


def level2_face(consts, mp, mc):
    return (consts[0] * (mp[0] + mc[0]), consts[0] * (mp[1] + mc[1]))


def level2_around(vp, vc, vn):
    lows = (pltpu.roll(vc[1], 1, 0), vc[0])
    highs = (vc[1], pltpu.roll(vc[0], G2 - 1, 0))
    return [
        (vp[p], vn[p], lows[p], highs[p], pltpu.roll(vc[p], 1, 1), pltpu.roll(vc[p], R2 - 1, 1))
        for p in range(2)
    ]


def total_weight(w):
    return (w[0] + w[1]) + (w[2] + w[3]) + (w[4] + w[5])


def height_walls():
    sub = iota((G2, R2), 0)
    return jnp.where(sub == 0, 0.0, 0.5), jnp.where(sub == G2 - 1, 0.0, 0.5)


def level2_consts():
    lane = iota((G2, R2), 1)
    return radial_consts((G2, R2), R2, 2.0 * math.pi / AZ2, lane) + height_walls()


def both(ref, s):
    return (ref[s, 0], ref[s, 1])


def close_ring(ref):
    ref[0:2] = ref[AZ2 : AZ2 + 2]
    ref[AZ2 + 2 : AZ2 + 4] = ref[2:4]


HALF = AZ3 // 2


def packed(ref):
    row_i, col_i = iota((R2, R2), 0), iota((R2, R2), 1)
    left = (row_i // 2 == col_i).astype(F32)
    right = (row_i // 2 + R2 // 2 == col_i).astype(F32)
    lower = ref[0:HALF].reshape(HALF * G2, R2)
    upper = ref[HALF:AZ3].reshape(HALF * G2, R2)
    return (dot(lower, left) + dot(upper, right)).reshape(HALF, G2, R2)


def wrap(ref):
    ref[0] = pltpu.roll(ref[HALF], R2 // 2, 1)
    ref[HALF + 1] = pltpu.roll(ref[1], R2 // 2, 1)


STEP = 8


def coarse_weights(own, oth, m2, d2, w3, sum_m, m3):
    a, g = position()
    pa = a % 2
    rows = A2 * H2
    for k in range(N_AZ):
        base = (k // 2) * N_GZ * 2 * rows + rows
        first, second = (own, oth) if k % 2 == 0 else (oth, own)
        for i in range(A2):
            for p in range(2):
                at = pl.ds(base + i * 2 + p, G2, stride=2 * rows)
                m2[k * A2 + i + 2, p] = pick(pa, first[at, :], second[at, :])
    close_ring(m2)
    consts = level2_consts()

    def diagonals(k, carry):
        s = STEP * k + 2
        mp, mc = both(m2, s - 1), both(m2, s)
        face = level2_face(consts, mp, mc)
        for d in range(STEP):
            mn = both(m2, s + d + 1)
            w, face = level2_plane(consts, face, mc, mn)
            for p in range(2):
                d2[s + d, p] = OMEGA / (total_weight(w[p]) + SIGMA * 16.0)
            if d % 2:
                sum_m[(STEP // 2) * k + d // 2] = (mp[0] + mp[1]) + (mc[0] + mc[1])
            mp, mc = mc, mn
        return carry

    lax.fori_loop(0, AZ2 // STEP, diagonals, 0)
    close_ring(d2)
    m3[1 : HALF + 1] = 0.125 * packed(sum_m)
    wrap(m3)
    lane = iota((G2, R2), 1) % (R2 // 2)
    ca, ri, ro = radial_consts((G2, R2), R2 // 2, 2.0 * math.pi / AZ3, lane)
    zlo, zhi = height_walls()
    mp, mc = m3[0], m3[1]
    for i in range(HALF):
        mn = m3[i + 2]
        w = (
            ca * (mc + mp),
            ca * (mc + mn),
            zlo * (mc + pltpu.roll(mc, 1, 0)),
            zhi * (mc + pltpu.roll(mc, G2 - 1, 0)),
            ri * (mc + pltpu.roll(mc, 1, 1)),
            ro * (mc + pltpu.roll(mc, R2 - 1, 1)),
        )
        scale = OMEGA / (total_weight(w) + SIGMA * 64.0)
        for f in range(6):
            w3[f, i] = w[f] * scale
        w3[6, i] = scale
        mp, mc = mc, mn


def coarse(
    own, oth, bw, vw, mw, cx, cc, rhs_ref, v_ref, m_ref, ax, ac, az, ay, bx, bc, bz, by,
    out_ref, sx, sc, sz, sy,
    m2, d2, w3, sum_m, m3, b2, v2, sum_r, add, va, vb, e2, v2f, src, v1f, e_ref,
):
    coarse_weights(own, oth, m2, d2, w3, sum_m, m3)
    a, g = position()
    pa = a % 2
    rows = A2 * H2

    for k in range(N_AZ):
        base = (k // 2) * N_GZ * 2 * rows
        first, second = (own, oth) if k % 2 == 0 else (oth, own)
        for i in range(A2):
            for p in range(2):
                at = pl.ds(base + i * 2 + p, G2, stride=2 * rows)
                b = pick(pa, first[at, :], second[at, :])
                b2[k * A2 + i + 2, p] = b
                v2[k * A2 + i + 2, p] = b * d2[k * A2 + i + 2, p]
    close_ring(b2)
    close_ring(v2)
    consts = level2_consts()

    def residuals(k, carry):
        s = STEP * k + 2
        mc = both(m2, s)
        vp, vc = both(v2, s - 1), both(v2, s)
        face = level2_face(consts, both(m2, s - 1), mc)
        total = None
        for d in range(STEP):
            mn, vn = both(m2, s + d + 1), both(v2, s + d + 1)
            w, face = level2_plane(consts, face, mc, mn)
            n = level2_around(vp, vc, vn)
            b = both(b2, s + d)
            r = ((1.0 - OMEGA) * (b[0] + b[1]) + weighted(w[0], n[0])) + weighted(w[1], n[1])
            if d % 2:
                sum_r[(STEP // 2) * k + d // 2] = total + r
            total, mc, vp, vc = r, mn, vc, vn
        return carry

    lax.fori_loop(0, AZ2 // STEP, residuals, 0)

    b3 = 0.5 * packed(sum_r)
    for i in range(HALF):
        start = b3[i] * w3[6, i]
        add[i] = start
        va[i + 1] = start
    wrap(va)

    def sweep(src_ref, dst_ref):
        vp, vc = src_ref[0], src_ref[1]
        for i in range(HALF):
            vn = src_ref[i + 2]
            n = (
                vp,
                vn,
                pltpu.roll(vc, 1, 0),
                pltpu.roll(vc, G2 - 1, 0),
                pltpu.roll(vc, 1, 1),
                pltpu.roll(vc, R2 - 1, 1),
            )
            w = [w3[f, i] for f in range(6)]
            dst_ref[i + 1] = ((1.0 - OMEGA) * vc + add[i]) + weighted(w, n)
            vp, vc = vc, vn
        wrap(dst_ref)

    def two(k, carry):
        sweep(va, vb)
        sweep(vb, va)
        return carry

    lax.fori_loop(0, (COARSE_SWEEPS - 2) // 2, two, 0)
    sweep(va, vb)

    row_i, col_i = iota((R2, R2), 0), iota((R2, R2), 1)
    solved = vb[1 : HALF + 1].reshape(HALF * G2, R2)
    e2[0:HALF] = dot(solved, (row_i == col_i // 2).astype(F32)).reshape(HALF, G2, R2)
    e2[HALF:AZ3] = dot(solved, (row_i == col_i // 2 + R2 // 2).astype(F32)).reshape(HALF, G2, R2)

    at = a * A2
    values = []
    for k in range(A2 + 4):
        e = e2[(a * (A2 // 2) - 1 + k // 2 + AZ3) % AZ3]
        values.append((v2[at + k, 0] + e, v2[at + k, 1] + e))
    mc = both(m2, at + 1)
    face = level2_face(consts, both(m2, at), mc)
    for k in range(1, A2 + 3):
        mn = both(m2, at + k + 1)
        w, face = level2_plane(consts, face, mc, mn)
        n = level2_around(*values[k - 1 : k + 2])
        for p in range(2):
            gain = b2[at + k, p] + weighted(w[p], n[p])
            v2f[k - 1, p] = (1.0 - OMEGA) * values[k][p] + d2[at + k, p] * gain
        mc = mn

    low, high = jnp.maximum(g - 1, 0), jnp.minimum(g + 1, N_GZ - 1)
    for j in range(A2 + 2):
        for q, (p, row) in enumerate(((1, low), (0, g), (1, g), (0, high))):
            src[4 * j + q : 4 * j + q + 1, :] = v2f[j, p, pl.ds(row, 1), :]
    o, c = iota((8 * (A2 + 2), 4 * (A2 + 2)), 0), iota((8 * (A2 + 2), 4 * (A2 + 2)), 1)
    e1 = dot((o // 2 == c).astype(F32), dot(src[...], dup_cols(R2)))
    halo = Halo(cx, cc, None, None)

    def v1_of(i):
        j = (i + 2) // 2
        return wide_planes(vw, halo, 0, i) + e1[T1 * j : T1 * (j + 1)]

    def emit1(i, diagonal, around, centre):
        b = wide_planes(bw, halo, 2, i)
        at = (i + 1) * T1
        v1f[at : at + T1, :] = (1.0 - OMEGA) * centre + OMEGA * (b + around) / diagonal

    level1_walk(lambda i: wide_planes(mw, halo, 1, i), v1_of, -1, A1 + 2, emit1)

    own_rows = (A1 + 2) * NH
    shape = (own_rows + 2 * A1, (A1 + 2) * T1)
    o, c = iota(shape, 0), iota(shape, 1)
    j = jnp.where(o < own_rows, o // NH, (o - own_rows) % A1 + 1)
    h = jnp.where(o < own_rows, (o % NH) // 2 + 2, jnp.where(o < own_rows + A1, 1, H1 + 2))
    e_ref[...] = dot(dot((c == j * T1 + h).astype(F32), v1f[...]), dup_cols(R1))
    ah, bh = Halo(ax, ac, az, ay), Halo(bx, bc, bz, by)
    m_of, mb, ma = fine_mobility(m_ref, ah)
    old, ob, oa = fine_values(v_ref, bh)

    def v_of(i):
        at = (i // 2 + 1) * NH
        return old(i) + e_ref[at : at + NH, :]

    def around_row(value, start):
        def row(i):
            at = start + i // 2
            return value(i) + e_ref[at : at + 1, :]

        return row

    def emit(i, diagonal, around, centre):
        out_ref[i] = (1.0 - OMEGA) * centre + OMEGA * (rhs_ref[i] + around) / diagonal

    fine_walk(
        m_of, v_of, mb, ma, around_row(ob, own_rows), around_row(oa, own_rows + A1), emit
    )
    store_faces(out_ref, sx, sc, sz, sy)


def final(rhs_ref, v_ref, m_ref, ax, ac, az, ay, gx, gc, gz, gy, p_hbm, out_hbm, out_ref, sems):
    part = NA // 4
    copies = [
        pltpu.make_async_copy(
            src.at[pl.ds(k * part, part)], dst.at[pl.ds(k * part, part)], sems.at[4 * n + k]
        )
        for n, (src, dst) in enumerate(((v_ref, p_hbm), (out_ref, out_hbm)))
        for k in range(4)
    ]
    for copy in copies[:4]:
        copy.start()
    ah, gh = Halo(ax, ac, az, ay), Halo(gx, gc, gz, gy)
    m_of, mb, ma = fine_mobility(m_ref, ah)
    v_of, vb, va = fine_values(v_ref, gh)

    def emit(i, diagonal, around, centre):
        out_ref[i] = (rhs_ref[i] - diagonal * centre + around) / diagonal
        if i % part == part - 1:
            copies[4 + i // part].start()

    fine_walk(m_of, v_of, mb, ma, vb, va, emit)
    for copy in copies:
        copy.wait()


def swap(x, axis, odd):
    n = lax.axis_size(axis)
    pairs = []
    for i in range(n):
        partner = i ^ 1 if odd == 0 else ((i + 1) % n if i % 2 else (i - 1) % n)
        pairs.append((i, partner))
    return lax.ppermute(x, axis, pairs)


def exchange(sx, sc, sz, sy):
    return swap(sx, "az", 1), swap(sc, "az", 0), swap(sz, "gz", 0), swap(sy, "gz", 1)


def gathered(x):
    groups = [[a * N_GZ + g for a in range(c, N_AZ, 2) for g in range(N_GZ)] for c in range(2)]
    own = lax.all_to_all(x, ("az", "gz"), 0, 0, tiled=True, axis_index_groups=groups)
    own = own.reshape(own.shape[0] * own.shape[1], own.shape[2])
    return own, swap(own, "az", 0)


def faces(planes, rows, width):
    return [struct(planes, width)] * 2 + [struct(rows, width)] * 2


def vmem(*shape):
    return pltpu.VMEM(shape, F32)


def body(pressure, divergence, void_fraction, bubble_volume, bubble_count, bubble_cell):
    block = struct(NA, NH, NR)
    wide = struct(A1, T1, R1)
    cell = bubble_cell.reshape(1, SLOTS)
    volume = bubble_volume.reshape(1, SLOTS)
    pairs = vmem(A1 * NH, NR)
    halves = vmem(A2 * T1, R1)

    m0, m1, m2, *send = call(
        prepare,
        [block, wide, struct(A2 * H2, R2)] + faces(3 * NH, 2 * NA + A1, NR),
        (pressure, void_fraction, volume, bubble_count),
        [pairs, halves],
        smem=(3,),
    )
    ha = exchange(*send)
    rhs, v0, *send = call(
        presmooth, [block, block] + faces(NH, NA, NR), (pressure, divergence, m0, cell, *ha)
    )
    hb = exchange(*send)
    b1, v1, sz, sy = call(
        restrict,
        [wide, wide] + [struct(5 * A1, R1)] * 2,
        (rhs, v0, m0, m1, *ha, *hb),
        [pairs],
    )
    v1, m1, b1, sx, sc = call(
        widen,
        [wide, wide, wide] + [struct(5 * T1, R1)] * 2,
        (b1, v1, m1, swap(sz, "gz", 0), swap(sy, "gz", 1)),
    )
    hc = swap(sx, "az", 1), swap(sc, "az", 0)
    (copies,) = call(restrict1, [struct(64, 2 * A2 * H2, R2)], (b1, v1, m1, m2, *hc), [halves])
    ring = vmem(AZ2 + 4, 2, G2, R2)
    ends = vmem(HALF + 2, G2, R2)
    third = vmem(AZ3, G2, R2)
    out, *send = call(
        coarse,
        [block] + faces(NH, NA, NR),
        (*gathered(copies), b1, v1, m1, *hc, rhs, v0, m0, *ha, *hb),
        [
            ring,
            ring,
            vmem(7, HALF, G2, R2),
            third,
            ends,
            ring,
            ring,
            third,
            vmem(HALF, G2, R2),
            ends,
            ends,
            third,
            vmem(A2 + 2, 2, G2, R2),
            vmem(4 * (A2 + 2), R2),
            vmem((A1 + 2) * T1, R1),
            vmem((A1 + 2) * NH + 2 * A1, NR),
        ],
    )
    hg = exchange(*send)
    return tuple(
        call(
            final,
            [block, block],
            (rhs, out, m0, *ha, *hg),
            [vmem(NA, NH, NR), pltpu.SemaphoreType.DMA((8,))],
            hbm_out=(0, 1),
        )
    )


def solution(mesh):
    return jax.shard_map(
        body,
        mesh=mesh,
        in_specs=(
            P("az", "gz", None),
            P("az", "gz", None),
            P("az", "gz", None),
            P(("az", "gz")),
            P(("az", "gz")),
            P(("az", "gz")),
        ),
        out_specs=(P("az", "gz", None), P("az", "gz", None)),
        check_vma=False,
    )
```

```python
import functools
import math

import jax
import jax.numpy as jnp
from jax import lax
from jax.experimental import pallas as pl
from jax.experimental.pallas import tpu as pltpu
from jax.sharding import PartitionSpec as P

SIGMA = 0.02
OMEGA = 0.8
COARSE_SWEEPS = 32
F32 = jnp.float32
BF16 = jnp.bfloat16

NA, NH, NR = 32, 8, 512
A1, H1, R1 = 16, 4, 256
A2, H2, R2 = 8, 2, 128
AZ2, G2 = 128, 8
AZ3 = 64
N_AZ, N_GZ = 16, 8
SLOTS = 128


def struct(*shape):
    return jax.ShapeDtypeStruct(shape, F32)


def call(kernel, outs, ins, scratch=(), smem=(), hbm=(), hbm_out=(), limit=48):
    def space(i, far):
        return pltpu.HBM if i in far else pltpu.SMEM if i in smem else pltpu.VMEM

    specs = [pl.BlockSpec(memory_space=space(i, hbm)) for i in range(len(ins))]
    return pl.pallas_call(
        kernel,
        out_shape=outs,
        in_specs=specs,
        out_specs=[
            pl.BlockSpec(memory_space=pltpu.HBM if i in hbm_out else pltpu.VMEM)
            for i in range(len(outs))
        ],
        scratch_shapes=list(scratch),
        compiler_params=pltpu.CompilerParams(vmem_limit_bytes=limit * 1024 * 1024),
    )(*ins)


def iota(shape, dim):
    return lax.broadcasted_iota(jnp.int32, shape, dim)


def parts(x):
    high = x.astype(BF16)
    rest = x - high.astype(F32)
    mid = rest.astype(BF16)
    return high, mid, (rest - mid.astype(F32)).astype(BF16)


def dot(a, b):
    if b.dtype == BF16:
        p = [jnp.dot(x, b, preferred_element_type=F32) for x in parts(a)]
    else:
        p = [jnp.dot(a, x, preferred_element_type=F32) for x in parts(b)]
    return (p[2] + p[1]) + p[0]


def radial_consts(shape, size, step, rad):
    i = rad.astype(F32)
    metric = ((i + 0.5) * step) ** 2
    ca = 0.5 / metric
    ri = jnp.where(rad > 0, 0.5 * i / (i + 0.5), 0.0)
    ro = jnp.where(rad < size - 1, 0.5 * (i + 1.0) / (i + 0.5), 0.0)
    return ca, ri, ro


def hot(mask):
    return mask.astype(F32).astype(BF16)


def pair_cols(n):
    return hot(iota((n, n // 2), 0) // 2 == iota((n, n // 2), 1))


def dup_cols(n):
    return hot(iota((n, 2 * n), 0) == iota((n, 2 * n), 1) // 2)


def row_sums(planes, out, first, per):
    o, r = iota((planes * out, planes * per), 0), iota((planes * out, planes * per), 1)
    h = r % per - first
    return hot((o // out == r // per) & (h >= 0) & (h // 2 == o % out))


def widened(planes):
    o, r = iota((planes * 8, planes * 8), 0), iota((planes * 8, planes * 8), 1)
    return hot((o // 8 == r // 8) & (o % 8 == (r % 8) // 2 + 2))


def position():
    return lax.axis_index("az"), lax.axis_index("gz")


def pick(par, even, odd):
    return jnp.where(par == 0, even, odd)


class Halo:
    def __init__(self, x_ref, c_ref, z_ref, y_ref):
        a, g = position()
        self.pa, self.pg = a % 2, g % 2
        self.x, self.c, self.z, self.y = x_ref, c_ref, z_ref, y_ref

    def prev(self, rows, lanes):
        return pick(self.pa, self.x[rows, lanes], self.c[rows, lanes])

    def next(self, rows, lanes):
        return pick(self.pa, self.c[rows, lanes], self.x[rows, lanes])

    def below(self, rows, lanes):
        return pick(self.pg, self.y[rows, lanes], self.z[rows, lanes])

    def above(self, rows, lanes):
        return pick(self.pg, self.z[rows, lanes], self.y[rows, lanes])


def fine_walk(m_of, v_of, mb, ma, vb, va, emit):
    a, g = position()
    sub = iota((NH, NR), 0)
    lane = iota((NH, NR), 1)
    ca, ri, ro = radial_consts((NH, NR), NR, 2.0 * math.pi / (NA * N_AZ), lane)
    zlo = jnp.where((sub == 0) & (g == 0), 0.0, 0.5)
    zhi = jnp.where((sub == NH - 1) & (g == N_GZ - 1), 0.0, 0.5)
    first, final = sub == 0, sub == NH - 1
    mp, mc = m_of(-1), m_of(0)
    vp, vc = v_of(-1), v_of(0)
    wa = ca * (mp + mc)
    for i in range(NA):
        mn, vn = m_of(i + 1), v_of(i + 1)
        wan = ca * (mc + mn)
        m_lo = jnp.where(first, mb(i), pltpu.roll(mc, 1, 0))
        m_hi = jnp.where(final, ma(i), pltpu.roll(mc, NH - 1, 0))
        v_lo = jnp.where(first, vb(i), pltpu.roll(vc, 1, 0))
        v_hi = jnp.where(final, va(i), pltpu.roll(vc, NH - 1, 0))
        wl, wh = zlo * (mc + m_lo), zhi * (mc + m_hi)
        wi = ri * (mc + pltpu.roll(mc, 1, 1))
        wo = ro * (mc + pltpu.roll(mc, NR - 1, 1))
        diagonal = (wa + wan) + (wl + wh) + (wi + wo) + SIGMA
        around = (wa * vp + wan * vn) + (wl * v_lo + wh * v_hi)
        around = around + (wi * pltpu.roll(vc, 1, 1) + wo * pltpu.roll(vc, NR - 1, 1))
        emit(i, diagonal, around, vc)
        mp, mc, vp, vc, wa = mc, mn, vc, vn, wan


T1 = 8


def level1_walk(m_of, v_of, first, count, emit):
    a, g = position()
    sub = iota((T1, R1), 0)
    lane = iota((T1, R1), 1)
    height = g * H1 + sub - 2
    ca, ri, ro = radial_consts((T1, R1), R1, 2.0 * math.pi / (A1 * N_AZ), lane)
    zlo = jnp.where(height <= 0, 0.0, 0.5)
    zhi = jnp.where(height >= H1 * N_GZ - 1, 0.0, 0.5)
    mp, mc = m_of(first - 1), m_of(first)
    if v_of is not None:
        vp, vc = v_of(first - 1), v_of(first)
    wa = ca * (mp + mc)
    for i in range(first, first + count):
        mn = m_of(i + 1)
        wan = ca * (mc + mn)
        w = (
            wa,
            wan,
            zlo * (mc + pltpu.roll(mc, 1, 0)),
            zhi * (mc + pltpu.roll(mc, T1 - 1, 0)),
            ri * (mc + pltpu.roll(mc, 1, 1)),
            ro * (mc + pltpu.roll(mc, R1 - 1, 1)),
        )
        diagonal = total_weight(w) + SIGMA * 4.0
        if v_of is None:
            emit(i, diagonal, None, None)
        else:
            vn = v_of(i + 1)
            n = (
                vp,
                vn,
                pltpu.roll(vc, 1, 0),
                pltpu.roll(vc, T1 - 1, 0),
                pltpu.roll(vc, 1, 1),
                pltpu.roll(vc, R1 - 1, 1),
            )
            emit(i, diagonal, weighted(w, n), vc)
            vp, vc = vc, vn
        mp, mc, wa = mc, mn, wan


def weighted(w, n):
    return (w[0] * n[0] + w[1] * n[1]) + (w[2] * n[2] + w[3] * n[3]) + (w[4] * n[4] + w[5] * n[5])


ALL = slice(None)


def store_faces(ref, x_ref, c_ref, z_ref, y_ref, planes_at=0, rows_at=0):
    a, g = position()
    pa, pg = a % 2, g % 2
    c_plane = jnp.where(pa == 0, NA - 1, 0)
    x_plane = NA - 1 - c_plane
    c_ref[planes_at : planes_at + NH, :] = ref[c_plane]
    x_ref[planes_at : planes_at + NH, :] = ref[x_plane]
    z_row = jnp.where(pg == 0, NH - 1, 0)
    y_row = NH - 1 - z_row
    for i in range(NA):
        z_ref[rows_at + i : rows_at + i + 1, :] = ref[i, pl.ds(z_row, 1), :]
        y_ref[rows_at + i : rows_at + i + 1, :] = ref[i, pl.ds(y_row, 1), :]


def mobilities(void_ref, m0_ref, m1_ref, m2_ref, pairs, halves):
    for i in range(0, NA, 2):
        u = 1.0 / (1.0 - void_ref[i])
        v = 1.0 / (1.0 - void_ref[i + 1])
        m0_ref[i] = u
        m0_ref[i + 1] = v
        pairs[(i // 2) * NH : (i // 2 + 1) * NH, :] = u + v
    m1_ref[...] = 0.125 * dot(widened(A1), dot(pairs[...], pair_cols(NR))).reshape(A1, T1, R1)
    for i in range(A2):
        halves[i * T1 : (i + 1) * T1, :] = m1_ref[2 * i] + m1_ref[2 * i + 1]
    m2_ref[...] = 0.125 * dot(row_sums(A2, H2, 2, T1), dot(halves[...], pair_cols(R1)))


def first_faces(p_ref, m0_ref, m1_ref, vol_ref, cnt_ref, sx, sc, sz, sy):
    a, g = position()
    pa, pg = a % 2, g % 2
    store_faces(p_ref, sx, sc, sz, sy, 0, 0)
    store_faces(m0_ref, sx, sc, sz, sy, NH, NA)
    rest = slice(2 * NH, 3 * NH)
    sx[rest, R1:NR] = jnp.zeros((NH, NR - R1), F32)
    sc[rest, R1:NR] = jnp.zeros((NH, NR - R1), F32)
    c_plane = jnp.where(pa == 0, A1 - 1, 0)
    sc[rest, 0:R1] = m1_ref[c_plane]
    sx[rest, 0:R1] = m1_ref[A1 - 1 - c_plane]
    for ref in (sz, sy):
        ref[2 * NA : 2 * NA + A1, R1:NR] = jnp.zeros((A1, NR - R1), F32)
    z_row = jnp.where(pg == 0, H1 + 1, 2)
    for i in range(A1):
        at = slice(2 * NA + i, 2 * NA + i + 1)
        sz[at, 0:R1] = m1_ref[i, pl.ds(z_row, 1), :]
        sy[at, 0:R1] = m1_ref[i, pl.ds(H1 + 3 - z_row, 1), :]
    live = jnp.where(iota((1, SLOTS), 1) < cnt_ref[0], vol_ref[...], 0.0)
    for ref in (sx, sc):
        ref[2 * NH : 2 * NH + 1, R1 : R1 + SLOTS] = live


def fine_mobility(m_ref, ah):
    def m_of(i):
        if i < 0:
            return ah.prev(slice(NH, 2 * NH), ALL)
        if i >= NA:
            return ah.next(slice(NH, 2 * NH), ALL)
        return m_ref[i]

    return (
        m_of,
        lambda i: ah.below(slice(NA + i, NA + i + 1), ALL),
        lambda i: ah.above(slice(NA + i, NA + i + 1), ALL),
    )


def fine_values(v_ref, vh):
    def v_of(i):
        if i < 0:
            return vh.prev(slice(0, NH), ALL)
        if i >= NA:
            return vh.next(slice(0, NH), ALL)
        return v_ref[i]

    return (
        v_of,
        lambda i: vh.below(slice(i, i + 1), ALL),
        lambda i: vh.above(slice(i, i + 1), ALL),
    )


def presmooth(p_ref, div_ref, m_ref, cell_ref, ax, ac, az, ay, rhs_ref, v_ref, sx, sc, sz, sy):
    ah = Halo(ax, ac, az, ay)
    arrived = ah.prev(slice(2 * NH, 2 * NH + 1), slice(R1, R1 + SLOTS))
    cell = cell_ref[...]
    plane_hot = hot(iota((NA * NH, SLOTS), 0) == lax.shift_right_logical(cell, 9))
    radius_hot = jnp.where(iota((NR, SLOTS), 0) == (cell & (NR - 1)), arrived, 0.0)
    deposit = [
        lax.dot_general(plane_hot, x, (((1,), (1,)), ((), ())), preferred_element_type=F32)
        for x in parts(radius_hot)
    ]
    deposit = (deposit[2] + deposit[1]) + deposit[0]
    rhs_ref[...] = div_ref[...] + deposit.reshape(NA, NH, NR)
    m_of, mb, ma = fine_mobility(m_ref, ah)
    v_of, vb, va = fine_values(p_ref, ah)

    def emit(i, diagonal, around, centre):
        v_ref[i] = (1.0 - OMEGA) * centre + OMEGA * (rhs_ref[i] + around) / diagonal

    fine_walk(m_of, v_of, mb, ma, vb, va, emit)
    store_faces(v_ref, sx, sc, sz, sy)


def restrict(
    rhs_ref, v_ref, m_ref, m1_ref, ax, ac, az, ay, bx, bc, bz, by, b1_ref, v1_ref, sz, sy, pairs
):
    ah, bh = Halo(ax, ac, az, ay), Halo(bx, bc, bz, by)
    m_of, mb, ma = fine_mobility(m_ref, ah)
    v_of, vb, va = fine_values(v_ref, bh)
    kept = []

    def emit(i, diagonal, around, centre):
        r = rhs_ref[i] - diagonal * centre + around
        if i % 2 == 0:
            kept.append(r)
        else:
            pairs[(i // 2) * NH : (i // 2 + 1) * NH, :] = kept.pop() + r

    fine_walk(m_of, v_of, mb, ma, vb, va, emit)
    b1_ref[...] = 0.5 * dot(widened(A1), dot(pairs[...], pair_cols(NR))).reshape(A1, T1, R1)

    sub = iota((T1, R1), 0)

    def m1_of(i):
        if i < 0:
            return ah.prev(slice(2 * NH, 3 * NH), slice(0, R1))
        if i >= A1:
            return ah.next(slice(2 * NH, 3 * NH), slice(0, R1))
        at = slice(2 * NA + i, 2 * NA + i + 1)
        below, above = ah.below(at, slice(0, R1)), ah.above(at, slice(0, R1))
        return jnp.where(sub == 1, below, jnp.where(sub == H1 + 2, above, m1_ref[i]))

    def emit1(i, diagonal, around, centre):
        v1_ref[i] = OMEGA * b1_ref[i] / diagonal

    level1_walk(m1_of, None, 0, A1, emit1)
    g = lax.axis_index("gz")
    for layer in range(2):
        z_row = jnp.where(g % 2 == 0, H1 + 1 - layer, 2 + layer)
        y_row = H1 + 3 - z_row
        sources = (v1_ref, m1_ref) if layer else (v1_ref, m1_ref, b1_ref)
        for n, ref in enumerate(sources):
            for i in range(A1):
                at = (2 * n + layer) * A1 + i
                sz[at : at + 1, :] = ref[i, pl.ds(z_row, 1), :]
                sy[at : at + 1, :] = ref[i, pl.ds(y_row, 1), :]


def widen(b1_ref, v1_ref, m1_ref, z_ref, y_ref, vw, mw, bw, sx, sc):
    a, g = position()
    sub = iota((T1, R1), 0)
    halo = Halo(None, None, z_ref, y_ref)
    for n, (src, dst) in enumerate(((v1_ref, vw), (m1_ref, mw), (b1_ref, bw))):
        for i in range(A1):
            tile = src[i]
            for layer in range(2 if n < 2 else 1):
                at = (2 * n + layer) * A1 + i
                at = slice(at, at + 1)
                tile = jnp.where(sub == 1 - layer, halo.below(at, ALL), tile)
                tile = jnp.where(sub == H1 + 2 + layer, halo.above(at, ALL), tile)
            dst[i] = tile
    for layer in range(2):
        c_plane = jnp.where(a % 2 == 0, A1 - 1 - layer, layer)
        x_plane = A1 - 1 - c_plane
        for n, ref in enumerate((vw, mw) if layer else (vw, mw, bw)):
            at = (2 * n + layer) * T1
            sc[at : at + T1, :] = ref[c_plane]
            sx[at : at + T1, :] = ref[x_plane]


def wide_planes(ref, halo, n, i):
    if i < 0:
        at = (2 * n - 1 - i) * T1
        return halo.prev(slice(at, at + T1), ALL)
    if i >= A1:
        at = (2 * n + i - A1) * T1
        return halo.next(slice(at, at + T1), ALL)
    return ref[i]


def restrict1(bw, vw, mw, m2_ref, cx, cc, out_ref, halves):
    halo = Halo(cx, cc, None, None)
    kept = []

    def emit(i, diagonal, around, centre):
        r = (1.0 - OMEGA) * bw[i] + around
        if i % 2 == 0:
            kept.append(r)
        else:
            halves[(i // 2) * T1 : (i // 2 + 1) * T1, :] = kept.pop() + r

    level1_walk(
        lambda i: wide_planes(mw, halo, 1, i), lambda i: wide_planes(vw, halo, 0, i), 0, A1, emit
    )
    b2 = 0.5 * dot(row_sums(A2, H2, 2, T1), dot(halves[...], pair_cols(R1)))
    m2 = m2_ref[...]
    rows = A2 * H2
    for k in range(out_ref.shape[0]):
        out_ref[k, 0:rows, :] = b2
        out_ref[k, rows : 2 * rows, :] = m2


def level2_plane(consts, face, mc, mn):
    ca, ri, ro, zlo, zhi = consts
    mid = 0.5 * (mc[0] + mc[1])
    lows = (zlo * (mc[0] + pltpu.roll(mc[1], 1, 0)), mid)
    highs = (mid, zhi * (mc[1] + pltpu.roll(mc[0], G2 - 1, 0)))
    nxt = level2_face(consts, mc, mn)
    out = []
    for p in range(2):
        m = mc[p]
        wi, wo = ri * (m + pltpu.roll(m, 1, 1)), ro * (m + pltpu.roll(m, R2 - 1, 1))
        out.append((face[p], nxt[p], lows[p], highs[p], wi, wo))
    return out, nxt


def level2_face(consts, mp, mc):
    return (consts[0] * (mp[0] + mc[0]), consts[0] * (mp[1] + mc[1]))


def level2_around(vp, vc, vn):
    lows = (pltpu.roll(vc[1], 1, 0), vc[0])
    highs = (vc[1], pltpu.roll(vc[0], G2 - 1, 0))
    return [
        (vp[p], vn[p], lows[p], highs[p], pltpu.roll(vc[p], 1, 1), pltpu.roll(vc[p], R2 - 1, 1))
        for p in range(2)
    ]


def total_weight(w):
    return (w[0] + w[1]) + (w[2] + w[3]) + (w[4] + w[5])


def height_walls():
    sub = iota((G2, R2), 0)
    return jnp.where(sub == 0, 0.0, 0.5), jnp.where(sub == G2 - 1, 0.0, 0.5)


def level2_consts():
    lane = iota((G2, R2), 1)
    return radial_consts((G2, R2), R2, 2.0 * math.pi / AZ2, lane) + height_walls()


def both(ref, s):
    return (ref[s, 0], ref[s, 1])


def close_ring(ref):
    ref[0:2] = ref[AZ2 : AZ2 + 2]
    ref[AZ2 + 2 : AZ2 + 4] = ref[2:4]


HALF = AZ3 // 2


def packed(ref):
    row_i, col_i = iota((R2, R2), 0), iota((R2, R2), 1)
    left = hot(row_i // 2 == col_i)
    right = hot(row_i // 2 + R2 // 2 == col_i)
    lower = ref[0:HALF].reshape(HALF * G2, R2)
    upper = ref[HALF:AZ3].reshape(HALF * G2, R2)
    return (dot(lower, left) + dot(upper, right)).reshape(HALF, G2, R2)


def wrap(ref):
    ref[0] = pltpu.roll(ref[HALF], R2 // 2, 1)
    ref[HALF + 1] = pltpu.roll(ref[1], R2 // 2, 1)


STEP = 8


def coarse_weights(own, oth, m2, d2, w3, sum_m, m3):
    a, g = position()
    pa = a % 2
    rows = A2 * H2
    def lay(own, oth):
        for k in range(N_AZ):
            base = (k // 2) * N_GZ * 2 * rows + rows
            ref = oth if k % 2 else own
            for i in range(A2):
                for p in range(2):
                    at = pl.ds(base + i * 2 + p, G2, stride=2 * rows)
                    m2[k * A2 + i + 2, p] = ref[at, :]

    pl.when(pa == 0)(lambda: lay(own, oth))
    pl.when(pa == 1)(lambda: lay(oth, own))
    close_ring(m2)
    consts = level2_consts()

    def diagonals(k, carry):
        s = STEP * k + 2
        mp, mc = both(m2, s - 1), both(m2, s)
        face = level2_face(consts, mp, mc)
        for d in range(STEP):
            mn = both(m2, s + d + 1)
            w, face = level2_plane(consts, face, mc, mn)
            for p in range(2):
                d2[s + d, p] = OMEGA / (total_weight(w[p]) + SIGMA * 16.0)
            if d % 2:
                sum_m[(STEP // 2) * k + d // 2] = (mp[0] + mp[1]) + (mc[0] + mc[1])
            mp, mc = mc, mn
        return carry

    lax.fori_loop(0, AZ2 // STEP, diagonals, 0)
    close_ring(d2)
    m3[1 : HALF + 1] = 0.125 * packed(sum_m)
    wrap(m3)
    lane = iota((G2, R2), 1) % (R2 // 2)
    ca, ri, ro = radial_consts((G2, R2), R2 // 2, 2.0 * math.pi / AZ3, lane)
    zlo, zhi = height_walls()
    mp, mc = m3[0], m3[1]
    for i in range(HALF):
        mn = m3[i + 2]
        w = (
            ca * (mc + mp),
            ca * (mc + mn),
            zlo * (mc + pltpu.roll(mc, 1, 0)),
            zhi * (mc + pltpu.roll(mc, G2 - 1, 0)),
            ri * (mc + pltpu.roll(mc, 1, 1)),
            ro * (mc + pltpu.roll(mc, R2 - 1, 1)),
        )
        scale = OMEGA / (total_weight(w) + SIGMA * 64.0)
        for f in range(6):
            w3[f, i] = w[f] * scale
        w3[6, i] = scale
        mp, mc = mc, mn


def coarse(
    own, oth, bw, vw, mw, cx, cc, rhs_ref, v_ref, m_ref, ax, ac, az, ay, bx, bc, bz, by,
    out_ref, sx, sc, sz, sy,
    m2, d2, w3, sum_m, m3, b2, v2, sum_r, add, va, vb, e2, v2f, src, v1f, e_ref,
):
    coarse_weights(own, oth, m2, d2, w3, sum_m, m3)
    a, g = position()
    pa = a % 2
    rows = A2 * H2

    def lay(own, oth):
        for k in range(N_AZ):
            base = (k // 2) * N_GZ * 2 * rows
            ref = oth if k % 2 else own
            for i in range(A2):
                s = k * A2 + i + 2
                for p in range(2):
                    b = ref[pl.ds(base + i * 2 + p, G2, stride=2 * rows), :]
                    b2[s, p] = b
                    v2[s, p] = b * d2[s, p]

    pl.when(pa == 0)(lambda: lay(own, oth))
    pl.when(pa == 1)(lambda: lay(oth, own))
    close_ring(b2)
    close_ring(v2)
    consts = level2_consts()

    def residuals(k, carry):
        s = STEP * k + 2
        mc = both(m2, s)
        vp, vc = both(v2, s - 1), both(v2, s)
        face = level2_face(consts, both(m2, s - 1), mc)
        total = None
        for d in range(STEP):
            mn, vn = both(m2, s + d + 1), both(v2, s + d + 1)
            w, face = level2_plane(consts, face, mc, mn)
            n = level2_around(vp, vc, vn)
            b = both(b2, s + d)
            r = ((1.0 - OMEGA) * (b[0] + b[1]) + weighted(w[0], n[0])) + weighted(w[1], n[1])
            if d % 2:
                sum_r[(STEP // 2) * k + d // 2] = total + r
            total, mc, vp, vc = r, mn, vc, vn
        return carry

    lax.fori_loop(0, AZ2 // STEP, residuals, 0)

    b3 = 0.5 * packed(sum_r)
    for i in range(HALF):
        start = b3[i] * w3[6, i]
        add[i] = start
        va[i + 1] = start
    wrap(va)

    def sweep(src_ref, dst_ref):
        vp, vc = src_ref[0], src_ref[1]
        for i in range(HALF):
            vn = src_ref[i + 2]
            n = (
                vp,
                vn,
                pltpu.roll(vc, 1, 0),
                pltpu.roll(vc, G2 - 1, 0),
                pltpu.roll(vc, 1, 1),
                pltpu.roll(vc, R2 - 1, 1),
            )
            w = [w3[f, i] for f in range(6)]
            dst_ref[i + 1] = ((1.0 - OMEGA) * vc + add[i]) + weighted(w, n)
            vp, vc = vc, vn
        wrap(dst_ref)

    def two(k, carry):
        sweep(va, vb)
        sweep(vb, va)
        return carry

    lax.fori_loop(0, (COARSE_SWEEPS - 2) // 2, two, 0)
    sweep(va, vb)

    row_i, col_i = iota((R2, R2), 0), iota((R2, R2), 1)
    solved = vb[1 : HALF + 1].reshape(HALF * G2, R2)
    e2[0:HALF] = dot(solved, hot(row_i == col_i // 2)).reshape(HALF, G2, R2)
    e2[HALF:AZ3] = dot(solved, hot(row_i == col_i // 2 + R2 // 2)).reshape(HALF, G2, R2)

    at = a * A2
    values = []
    for k in range(A2 + 4):
        e = e2[(a * (A2 // 2) - 1 + k // 2 + AZ3) % AZ3]
        values.append((v2[at + k, 0] + e, v2[at + k, 1] + e))
    mc = both(m2, at + 1)
    face = level2_face(consts, both(m2, at), mc)
    for k in range(1, A2 + 3):
        mn = both(m2, at + k + 1)
        w, face = level2_plane(consts, face, mc, mn)
        n = level2_around(*values[k - 1 : k + 2])
        for p in range(2):
            gain = b2[at + k, p] + weighted(w[p], n[p])
            v2f[k - 1, p] = (1.0 - OMEGA) * values[k][p] + d2[at + k, p] * gain
        mc = mn

    low, high = jnp.maximum(g - 1, 0), jnp.minimum(g + 1, N_GZ - 1)
    for j in range(A2 + 2):
        for q, (p, row) in enumerate(((1, low), (0, g), (1, g), (0, high))):
            src[4 * j + q : 4 * j + q + 1, :] = v2f[j, p, pl.ds(row, 1), :]
    o, c = iota((8 * (A2 + 2), 4 * (A2 + 2)), 0), iota((8 * (A2 + 2), 4 * (A2 + 2)), 1)
    e1 = dot(hot(o // 2 == c), dot(src[...], dup_cols(R2)))
    halo = Halo(cx, cc, None, None)

    def v1_of(i):
        j = (i + 2) // 2
        return wide_planes(vw, halo, 0, i) + e1[T1 * j : T1 * (j + 1)]

    def emit1(i, diagonal, around, centre):
        b = wide_planes(bw, halo, 2, i)
        at = (i + 1) * T1
        v1f[at : at + T1, :] = (1.0 - OMEGA) * centre + OMEGA * (b + around) / diagonal

    level1_walk(lambda i: wide_planes(mw, halo, 1, i), v1_of, -1, A1 + 2, emit1)

    own_rows = (A1 + 2) * NH
    shape = (own_rows + 2 * A1, (A1 + 2) * T1)
    o, c = iota(shape, 0), iota(shape, 1)
    j = jnp.where(o < own_rows, o // NH, (o - own_rows) % A1 + 1)
    h = jnp.where(o < own_rows, (o % NH) // 2 + 2, jnp.where(o < own_rows + A1, 1, H1 + 2))
    e_ref[...] = dot(dot(hot(c == j * T1 + h), v1f[...]), dup_cols(R1))
    ah, bh = Halo(ax, ac, az, ay), Halo(bx, bc, bz, by)
    m_of, mb, ma = fine_mobility(m_ref, ah)
    old, ob, oa = fine_values(v_ref, bh)

    def v_of(i):
        at = (i // 2 + 1) * NH
        return old(i) + e_ref[at : at + NH, :]

    def around_row(value, start):
        def row(i):
            at = start + i // 2
            return value(i) + e_ref[at : at + 1, :]

        return row

    def emit(i, diagonal, around, centre):
        out_ref[i] = (1.0 - OMEGA) * centre + OMEGA * (rhs_ref[i] + around) / diagonal

    fine_walk(
        m_of, v_of, mb, ma, around_row(ob, own_rows), around_row(oa, own_rows + A1), emit
    )
    store_faces(out_ref, sx, sc, sz, sy)


def final(rhs_ref, v_ref, m_ref, ax, ac, az, ay, gx, gc, gz, gy, p_hbm, out_hbm, out_ref, sems):
    part = NA // 4
    copies = [
        pltpu.make_async_copy(
            src.at[pl.ds(k * part, part)], dst.at[pl.ds(k * part, part)], sems.at[4 * n + k]
        )
        for n, (src, dst) in enumerate(((v_ref, p_hbm), (out_ref, out_hbm)))
        for k in range(4)
    ]
    for copy in copies[:4]:
        copy.start()
    ah, gh = Halo(ax, ac, az, ay), Halo(gx, gc, gz, gy)
    m_of, mb, ma = fine_mobility(m_ref, ah)
    v_of, vb, va = fine_values(v_ref, gh)

    def emit(i, diagonal, around, centre):
        out_ref[i] = (rhs_ref[i] - diagonal * centre + around) / diagonal
        if i % part == part - 1:
            copies[4 + i // part].start()

    fine_walk(m_of, v_of, mb, ma, vb, va, emit)
    for copy in copies:
        copy.wait()


def swap(x, axis, odd):
    n = lax.axis_size(axis)
    pairs = []
    for i in range(n):
        partner = i ^ 1 if odd == 0 else ((i + 1) % n if i % 2 else (i - 1) % n)
        pairs.append((i, partner))
    return lax.ppermute(x, axis, pairs)


def exchange(sx, sc, sz, sy):
    return swap(sx, "az", 1), swap(sc, "az", 0), swap(sz, "gz", 0), swap(sy, "gz", 1)


def gathered(x):
    groups = [[a * N_GZ + g for a in range(c, N_AZ, 2) for g in range(N_GZ)] for c in range(2)]
    own = lax.all_to_all(x, ("az", "gz"), 0, 0, tiled=True, axis_index_groups=groups)
    own = own.reshape(own.shape[0] * own.shape[1], own.shape[2])
    return own, swap(own, "az", 0)


def faces(planes, rows, width):
    return [struct(planes, width)] * 2 + [struct(rows, width)] * 2


def vmem(*shape):
    return pltpu.VMEM(shape, F32)


def body(pressure, divergence, void_fraction, bubble_volume, bubble_count, bubble_cell):
    block = struct(NA, NH, NR)
    wide = struct(A1, T1, R1)
    cell = bubble_cell.reshape(1, SLOTS)
    volume = bubble_volume.reshape(1, SLOTS)
    pairs = vmem(A1 * NH, NR)
    halves = vmem(A2 * T1, R1)

    m0, m1, m2 = call(
        mobilities, [block, wide, struct(A2 * H2, R2)], (void_fraction,), [pairs, halves]
    )
    send = call(
        first_faces,
        faces(3 * NH, 2 * NA + A1, NR),
        (pressure, m0, m1, volume, bubble_count),
        smem=(4,),
    )
    ha = exchange(*send)
    rhs, v0, *send = call(
        presmooth, [block, block] + faces(NH, NA, NR), (pressure, divergence, m0, cell, *ha)
    )
    hb = exchange(*send)
    b1, v1, sz, sy = call(
        restrict,
        [wide, wide] + [struct(5 * A1, R1)] * 2,
        (rhs, v0, m0, m1, *ha, *hb),
        [pairs],
    )
    v1, m1, b1, sx, sc = call(
        widen,
        [wide, wide, wide] + [struct(5 * T1, R1)] * 2,
        (b1, v1, m1, swap(sz, "gz", 0), swap(sy, "gz", 1)),
    )
    hc = swap(sx, "az", 1), swap(sc, "az", 0)
    (copies,) = call(restrict1, [struct(64, 2 * A2 * H2, R2)], (b1, v1, m1, m2, *hc), [halves])
    ring = vmem(AZ2 + 4, 2, G2, R2)
    ends = vmem(HALF + 2, G2, R2)
    third = vmem(AZ3, G2, R2)
    out, *send = call(
        coarse,
        [block] + faces(NH, NA, NR),
        (*gathered(copies), b1, v1, m1, *hc, rhs, v0, m0, *ha, *hb),
        [
            ring,
            ring,
            vmem(7, HALF, G2, R2),
            third,
            ends,
            ring,
            ring,
            third,
            vmem(HALF, G2, R2),
            ends,
            ends,
            third,
            vmem(A2 + 2, 2, G2, R2),
            vmem(4 * (A2 + 2), R2),
            vmem((A1 + 2) * T1, R1),
            vmem((A1 + 2) * NH + 2 * A1, NR),
        ],
    )
    hg = exchange(*send)
    return tuple(
        call(
            final,
            [block, block],
            (rhs, out, m0, *ha, *hg),
            [vmem(NA, NH, NR), pltpu.SemaphoreType.DMA((8,))],
            hbm_out=(0, 1),
        )
    )


def solution(mesh):
    return jax.shard_map(
        body,
        mesh=mesh,
        in_specs=(
            P("az", "gz", None),
            P("az", "gz", None),
            P("az", "gz", None),
            P(("az", "gz")),
            P(("az", "gz")),
            P(("az", "gz")),
        ),
        out_specs=(P("az", "gz", None), P("az", "gz", None)),
        check_vma=False,
    )
```

```python
import functools
import math

import jax
import jax.numpy as jnp
from jax import lax
from jax.experimental import pallas as pl
from jax.experimental.pallas import tpu as pltpu
from jax.sharding import PartitionSpec as P

SIGMA = 0.02
OMEGA = 0.8
COARSE_SWEEPS = 32
F32 = jnp.float32
BF16 = jnp.bfloat16

NA, NH, NR = 32, 8, 512
A1, H1, R1 = 16, 4, 256
A2, H2, R2 = 8, 2, 128
AZ2, G2 = 128, 8
AZ3 = 64
N_AZ, N_GZ = 16, 8
SLOTS = 128


def struct(*shape):
    return jax.ShapeDtypeStruct(shape, F32)


def call(kernel, outs, ins, scratch=(), smem=(), hbm=(), hbm_out=(), limit=48):
    def space(i, far):
        return pltpu.HBM if i in far else pltpu.SMEM if i in smem else pltpu.VMEM

    specs = [pl.BlockSpec(memory_space=space(i, hbm)) for i in range(len(ins))]
    return pl.pallas_call(
        kernel,
        out_shape=outs,
        in_specs=specs,
        out_specs=[
            pl.BlockSpec(memory_space=pltpu.HBM if i in hbm_out else pltpu.VMEM)
            for i in range(len(outs))
        ],
        scratch_shapes=list(scratch),
        compiler_params=pltpu.CompilerParams(vmem_limit_bytes=limit * 1024 * 1024),
    )(*ins)


def iota(shape, dim):
    return lax.broadcasted_iota(jnp.int32, shape, dim)


def parts(x):
    high = x.astype(BF16)
    rest = x - high.astype(F32)
    mid = rest.astype(BF16)
    return high, mid, (rest - mid.astype(F32)).astype(BF16)


def dot(a, b):
    if b.dtype == BF16:
        p = [jnp.dot(x, b, preferred_element_type=F32) for x in parts(a)]
    else:
        p = [jnp.dot(a, x, preferred_element_type=F32) for x in parts(b)]
    return (p[2] + p[1]) + p[0]


def radial_consts(shape, size, step, rad):
    i = rad.astype(F32)
    metric = ((i + 0.5) * step) ** 2
    ca = 0.5 / metric
    ri = jnp.where(rad > 0, 0.5 * i / (i + 0.5), 0.0)
    ro = jnp.where(rad < size - 1, 0.5 * (i + 1.0) / (i + 0.5), 0.0)
    return ca, ri, ro


def hot(mask):
    return mask.astype(F32).astype(BF16)


def pair_cols(n):
    return hot(iota((n, n // 2), 0) // 2 == iota((n, n // 2), 1))


def dup_cols(n):
    return hot(iota((n, 2 * n), 0) == iota((n, 2 * n), 1) // 2)


def row_sums(planes, out, first, per):
    o, r = iota((planes * out, planes * per), 0), iota((planes * out, planes * per), 1)
    h = r % per - first
    return hot((o // out == r // per) & (h >= 0) & (h // 2 == o % out))


def widened(planes):
    o, r = iota((planes * 8, planes * 8), 0), iota((planes * 8, planes * 8), 1)
    return hot((o // 8 == r // 8) & (o % 8 == (r % 8) // 2 + 2))


def position():
    return lax.axis_index("az"), lax.axis_index("gz")


def pick(par, even, odd):
    return jnp.where(par == 0, even, odd)


class Halo:
    def __init__(self, x_ref, c_ref, z_ref, y_ref):
        a, g = position()
        self.pa, self.pg = a % 2, g % 2
        self.x, self.c, self.z, self.y = x_ref, c_ref, z_ref, y_ref

    def prev(self, rows, lanes):
        return pick(self.pa, self.x[rows, lanes], self.c[rows, lanes])

    def next(self, rows, lanes):
        return pick(self.pa, self.c[rows, lanes], self.x[rows, lanes])

    def below(self, rows, lanes):
        return pick(self.pg, self.y[rows, lanes], self.z[rows, lanes])

    def above(self, rows, lanes):
        return pick(self.pg, self.z[rows, lanes], self.y[rows, lanes])


def fine_walk(m_of, v_of, mb, ma, vb, va, emit):
    a, g = position()
    sub = iota((NH, NR), 0)
    lane = iota((NH, NR), 1)
    ca, ri, ro = radial_consts((NH, NR), NR, 2.0 * math.pi / (NA * N_AZ), lane)
    zlo = jnp.where((sub == 0) & (g == 0), 0.0, 0.5)
    zhi = jnp.where((sub == NH - 1) & (g == N_GZ - 1), 0.0, 0.5)
    first, final = sub == 0, sub == NH - 1
    mp, mc = m_of(-1), m_of(0)
    vp, vc = v_of(-1), v_of(0)
    wa = ca * (mp + mc)
    for i in range(NA):
        mn, vn = m_of(i + 1), v_of(i + 1)
        wan = ca * (mc + mn)
        m_lo = jnp.where(first, mb(i), pltpu.roll(mc, 1, 0))
        m_hi = jnp.where(final, ma(i), pltpu.roll(mc, NH - 1, 0))
        v_lo = jnp.where(first, vb(i), pltpu.roll(vc, 1, 0))
        v_hi = jnp.where(final, va(i), pltpu.roll(vc, NH - 1, 0))
        wl, wh = zlo * (mc + m_lo), zhi * (mc + m_hi)
        wi = ri * (mc + pltpu.roll(mc, 1, 1))
        wo = ro * (mc + pltpu.roll(mc, NR - 1, 1))
        diagonal = (wa + wan) + (wl + wh) + (wi + wo) + SIGMA
        around = (wa * vp + wan * vn) + (wl * v_lo + wh * v_hi)
        around = around + (wi * pltpu.roll(vc, 1, 1) + wo * pltpu.roll(vc, NR - 1, 1))
        emit(i, diagonal, around, vc)
        mp, mc, vp, vc, wa = mc, mn, vc, vn, wan


T1 = 8


def level1_walk(m_of, v_of, first, count, emit):
    a, g = position()
    sub = iota((T1, R1), 0)
    lane = iota((T1, R1), 1)
    height = g * H1 + sub - 2
    ca, ri, ro = radial_consts((T1, R1), R1, 2.0 * math.pi / (A1 * N_AZ), lane)
    zlo = jnp.where(height <= 0, 0.0, 0.5)
    zhi = jnp.where(height >= H1 * N_GZ - 1, 0.0, 0.5)
    mp, mc = m_of(first - 1), m_of(first)
    if v_of is not None:
        vp, vc = v_of(first - 1), v_of(first)
    wa = ca * (mp + mc)
    for i in range(first, first + count):
        mn = m_of(i + 1)
        wan = ca * (mc + mn)
        w = (
            wa,
            wan,
            zlo * (mc + pltpu.roll(mc, 1, 0)),
            zhi * (mc + pltpu.roll(mc, T1 - 1, 0)),
            ri * (mc + pltpu.roll(mc, 1, 1)),
            ro * (mc + pltpu.roll(mc, R1 - 1, 1)),
        )
        diagonal = total_weight(w) + SIGMA * 4.0
        if v_of is None:
            emit(i, diagonal, None, None)
        else:
            vn = v_of(i + 1)
            n = (
                vp,
                vn,
                pltpu.roll(vc, 1, 0),
                pltpu.roll(vc, T1 - 1, 0),
                pltpu.roll(vc, 1, 1),
                pltpu.roll(vc, R1 - 1, 1),
            )
            emit(i, diagonal, weighted(w, n), vc)
            vp, vc = vc, vn
        mp, mc, wa = mc, mn, wan


def weighted(w, n):
    return (w[0] * n[0] + w[1] * n[1]) + (w[2] * n[2] + w[3] * n[3]) + (w[4] * n[4] + w[5] * n[5])


ALL = slice(None)


def store_faces(ref, x_ref, c_ref, z_ref, y_ref, planes_at=0, rows_at=0):
    a, g = position()
    pa, pg = a % 2, g % 2
    c_plane = jnp.where(pa == 0, NA - 1, 0)
    x_plane = NA - 1 - c_plane
    c_ref[planes_at : planes_at + NH, :] = ref[c_plane]
    x_ref[planes_at : planes_at + NH, :] = ref[x_plane]
    z_row = jnp.where(pg == 0, NH - 1, 0)
    y_row = NH - 1 - z_row
    for i in range(NA):
        z_ref[rows_at + i : rows_at + i + 1, :] = ref[i, pl.ds(z_row, 1), :]
        y_ref[rows_at + i : rows_at + i + 1, :] = ref[i, pl.ds(y_row, 1), :]


def mobilities(void_ref, m0_ref, m1_ref, m2_ref, pairs, halves):
    for i in range(0, NA, 2):
        u = 1.0 / (1.0 - void_ref[i])
        v = 1.0 / (1.0 - void_ref[i + 1])
        m0_ref[i] = u
        m0_ref[i + 1] = v
        pairs[(i // 2) * NH : (i // 2 + 1) * NH, :] = u + v
    m1_ref[...] = 0.125 * dot(widened(A1), dot(pairs[...], pair_cols(NR))).reshape(A1, T1, R1)
    for i in range(A2):
        halves[i * T1 : (i + 1) * T1, :] = m1_ref[2 * i] + m1_ref[2 * i + 1]
    m2_ref[...] = 0.125 * dot(row_sums(A2, H2, 2, T1), dot(halves[...], pair_cols(R1)))


def first_faces(p_ref, m0_ref, m1_ref, vol_ref, cnt_ref, sx, sc, sz, sy):
    a, g = position()
    pa, pg = a % 2, g % 2
    store_faces(p_ref, sx, sc, sz, sy, 0, 0)
    store_faces(m0_ref, sx, sc, sz, sy, NH, NA)
    rest = slice(2 * NH, 3 * NH)
    sx[rest, R1:NR] = jnp.zeros((NH, NR - R1), F32)
    sc[rest, R1:NR] = jnp.zeros((NH, NR - R1), F32)
    c_plane = jnp.where(pa == 0, A1 - 1, 0)
    sc[rest, 0:R1] = m1_ref[c_plane]
    sx[rest, 0:R1] = m1_ref[A1 - 1 - c_plane]
    for ref in (sz, sy):
        ref[2 * NA : 2 * NA + A1, R1:NR] = jnp.zeros((A1, NR - R1), F32)
    z_row = jnp.where(pg == 0, H1 + 1, 2)
    for i in range(A1):
        at = slice(2 * NA + i, 2 * NA + i + 1)
        sz[at, 0:R1] = m1_ref[i, pl.ds(z_row, 1), :]
        sy[at, 0:R1] = m1_ref[i, pl.ds(H1 + 3 - z_row, 1), :]
    live = jnp.where(iota((1, SLOTS), 1) < cnt_ref[0], vol_ref[...], 0.0)
    for ref in (sx, sc):
        ref[2 * NH : 2 * NH + 1, R1 : R1 + SLOTS] = live


def fine_mobility(m_ref, ah):
    def m_of(i):
        if i < 0:
            return ah.prev(slice(NH, 2 * NH), ALL)
        if i >= NA:
            return ah.next(slice(NH, 2 * NH), ALL)
        return m_ref[i]

    return (
        m_of,
        lambda i: ah.below(slice(NA + i, NA + i + 1), ALL),
        lambda i: ah.above(slice(NA + i, NA + i + 1), ALL),
    )


def fine_values(v_ref, vh):
    def v_of(i):
        if i < 0:
            return vh.prev(slice(0, NH), ALL)
        if i >= NA:
            return vh.next(slice(0, NH), ALL)
        return v_ref[i]

    return (
        v_of,
        lambda i: vh.below(slice(i, i + 1), ALL),
        lambda i: vh.above(slice(i, i + 1), ALL),
    )


def presmooth(p_ref, div_ref, m_ref, cell_ref, ax, ac, az, ay, rhs_ref, v_ref, sx, sc, sz, sy):
    ah = Halo(ax, ac, az, ay)
    arrived = ah.prev(slice(2 * NH, 2 * NH + 1), slice(R1, R1 + SLOTS))
    cell = cell_ref[...]
    plane_hot = hot(iota((NA * NH, SLOTS), 0) == lax.shift_right_logical(cell, 9))
    radius_hot = jnp.where(iota((NR, SLOTS), 0) == (cell & (NR - 1)), arrived, 0.0)
    deposit = [
        lax.dot_general(plane_hot, x, (((1,), (1,)), ((), ())), preferred_element_type=F32)
        for x in parts(radius_hot)
    ]
    deposit = (deposit[2] + deposit[1]) + deposit[0]
    rhs_ref[...] = div_ref[...] + deposit.reshape(NA, NH, NR)
    m_of, mb, ma = fine_mobility(m_ref, ah)
    v_of, vb, va = fine_values(p_ref, ah)

    def emit(i, diagonal, around, centre):
        v_ref[i] = (1.0 - OMEGA) * centre + OMEGA * (rhs_ref[i] + around) / diagonal

    fine_walk(m_of, v_of, mb, ma, vb, va, emit)
    store_faces(v_ref, sx, sc, sz, sy)


def restrict(
    rhs_ref, v_ref, m_ref, m1_ref, ax, ac, az, ay, bx, bc, bz, by, b1_ref, v1_ref, sx, sc, sz, sy, pairs
):
    ah, bh = Halo(ax, ac, az, ay), Halo(bx, bc, bz, by)
    m_of, mb, ma = fine_mobility(m_ref, ah)
    v_of, vb, va = fine_values(v_ref, bh)
    kept = []

    def emit(i, diagonal, around, centre):
        r = rhs_ref[i] - diagonal * centre + around
        if i % 2 == 0:
            kept.append(r)
        else:
            pairs[(i // 2) * NH : (i // 2 + 1) * NH, :] = kept.pop() + r

    fine_walk(m_of, v_of, mb, ma, vb, va, emit)
    b1_ref[...] = 0.5 * dot(widened(A1), dot(pairs[...], pair_cols(NR))).reshape(A1, T1, R1)

    sub = iota((T1, R1), 0)

    def m1_of(i):
        if i < 0:
            return ah.prev(slice(2 * NH, 3 * NH), slice(0, R1))
        if i >= A1:
            return ah.next(slice(2 * NH, 3 * NH), slice(0, R1))
        at = slice(2 * NA + i, 2 * NA + i + 1)
        below, above = ah.below(at, slice(0, R1)), ah.above(at, slice(0, R1))
        return jnp.where(sub == 1, below, jnp.where(sub == H1 + 2, above, m1_ref[i]))

    def emit1(i, diagonal, around, centre):
        v1_ref[i] = OMEGA * b1_ref[i] / diagonal

    level1_walk(m1_of, None, 0, A1, emit1)
    a, g = position()
    for layer in range(2):
        c_plane = jnp.where(a % 2 == 0, A1 - 1 - layer, layer)
        z_row = jnp.where(g % 2 == 0, H1 + 1 - layer, 2 + layer)
        y_row = H1 + 3 - z_row
        sources = (v1_ref, m1_ref) if layer else (v1_ref, m1_ref, b1_ref)
        for n, ref in enumerate(sources):
            for i in range(A1):
                at = (2 * n + layer) * A1 + i
                sz[at : at + 1, :] = ref[i, pl.ds(z_row, 1), :]
                sy[at : at + 1, :] = ref[i, pl.ds(y_row, 1), :]
            at = (2 * n + layer) * T1
            sc[at : at + T1, :] = ref[c_plane]
            sx[at : at + T1, :] = ref[A1 - 1 - c_plane]


def widen(pairs, halo):
    sub = iota((T1, R1), 0)
    for n, (src, dst) in enumerate(pairs):
        for i in range(A1):
            tile = src[i]
            for layer in range(2 if n < 2 else 1):
                at = (2 * n + layer) * A1 + i
                at = slice(at, at + 1)
                tile = jnp.where(sub == 1 - layer, halo.below(at, ALL), tile)
                tile = jnp.where(sub == H1 + 2 + layer, halo.above(at, ALL), tile)
            dst[i] = tile


def wide_planes(ref, halo, n, i, corners=None):
    if corners is not None and i == -1:
        return corners.prev(slice(n * T1, (n + 1) * T1), ALL)
    if corners is not None and i == A1:
        return corners.next(slice(n * T1, (n + 1) * T1), ALL)
    if i < 0:
        at = (2 * n - 1 - i) * T1
        return halo.prev(slice(at, at + T1), ALL)
    if i >= A1:
        at = (2 * n + i - A1) * T1
        return halo.next(slice(at, at + T1), ALL)
    return ref[i]


def restrict1(
    b1_ref, v1_ref, m1_ref, m2_ref, cx, cc, cz, cy, out_ref, bw, vw, mw, sx, sc, halves
):
    halo = Halo(cx, cc, cz, cy)
    widen(((v1_ref, vw), (m1_ref, mw), (b1_ref, bw)), halo)
    c_plane = jnp.where(lax.axis_index("az") % 2 == 0, A1 - 1, 0)
    for n, ref in enumerate((vw, mw)):
        sc[n * T1 : (n + 1) * T1, :] = ref[c_plane]
        sx[n * T1 : (n + 1) * T1, :] = ref[A1 - 1 - c_plane]
    kept = []

    def emit(i, diagonal, around, centre):
        r = (1.0 - OMEGA) * bw[i] + around
        if i % 2 == 0:
            kept.append(r)
        else:
            halves[(i // 2) * T1 : (i // 2 + 1) * T1, :] = kept.pop() + r

    level1_walk(
        lambda i: wide_planes(mw, halo, 1, i), lambda i: wide_planes(vw, halo, 0, i), 0, A1, emit
    )
    b2 = 0.5 * dot(row_sums(A2, H2, 2, T1), dot(halves[...], pair_cols(R1)))
    m2 = m2_ref[...]
    rows = A2 * H2
    for k in range(out_ref.shape[0]):
        out_ref[k, 0:rows, :] = b2
        out_ref[k, rows : 2 * rows, :] = m2


def level2_plane(consts, face, mc, mn):
    ca, ri, ro, zlo, zhi = consts
    mid = 0.5 * (mc[0] + mc[1])
    lows = (zlo * (mc[0] + pltpu.roll(mc[1], 1, 0)), mid)
    highs = (mid, zhi * (mc[1] + pltpu.roll(mc[0], G2 - 1, 0)))
    nxt = level2_face(consts, mc, mn)
    out = []
    for p in range(2):
        m = mc[p]
        wi, wo = ri * (m + pltpu.roll(m, 1, 1)), ro * (m + pltpu.roll(m, R2 - 1, 1))
        out.append((face[p], nxt[p], lows[p], highs[p], wi, wo))
    return out, nxt


def level2_face(consts, mp, mc):
    return (consts[0] * (mp[0] + mc[0]), consts[0] * (mp[1] + mc[1]))


def level2_around(vp, vc, vn):
    lows = (pltpu.roll(vc[1], 1, 0), vc[0])
    highs = (vc[1], pltpu.roll(vc[0], G2 - 1, 0))
    return [
        (vp[p], vn[p], lows[p], highs[p], pltpu.roll(vc[p], 1, 1), pltpu.roll(vc[p], R2 - 1, 1))
        for p in range(2)
    ]


def total_weight(w):
    return (w[0] + w[1]) + (w[2] + w[3]) + (w[4] + w[5])


def height_walls():
    sub = iota((G2, R2), 0)
    return jnp.where(sub == 0, 0.0, 0.5), jnp.where(sub == G2 - 1, 0.0, 0.5)


def level2_consts():
    lane = iota((G2, R2), 1)
    return radial_consts((G2, R2), R2, 2.0 * math.pi / AZ2, lane) + height_walls()


def both(ref, s):
    return (ref[s, 0], ref[s, 1])


def close_ring(ref):
    ref[0:2] = ref[AZ2 : AZ2 + 2]
    ref[AZ2 + 2 : AZ2 + 4] = ref[2:4]


HALF = AZ3 // 2


def packed(ref):
    row_i, col_i = iota((R2, R2), 0), iota((R2, R2), 1)
    left = hot(row_i // 2 == col_i)
    right = hot(row_i // 2 + R2 // 2 == col_i)
    lower = ref[0:HALF].reshape(HALF * G2, R2)
    upper = ref[HALF:AZ3].reshape(HALF * G2, R2)
    return (dot(lower, left) + dot(upper, right)).reshape(HALF, G2, R2)


def wrap(ref):
    ref[0] = pltpu.roll(ref[HALF], R2 // 2, 1)
    ref[HALF + 1] = pltpu.roll(ref[1], R2 // 2, 1)


STEP = 8


def coarse_weights(own, oth, m2, d2, w3, sum_m, m3):
    a, g = position()
    pa = a % 2
    rows = A2 * H2
    def lay(own, oth):
        for k in range(N_AZ):
            base = (k // 2) * N_GZ * 2 * rows + rows
            ref = oth if k % 2 else own
            for i in range(A2):
                for p in range(2):
                    at = pl.ds(base + i * 2 + p, G2, stride=2 * rows)
                    m2[k * A2 + i + 2, p] = ref[at, :]

    pl.when(pa == 0)(lambda: lay(own, oth))
    pl.when(pa == 1)(lambda: lay(oth, own))
    close_ring(m2)
    consts = level2_consts()

    def diagonals(k, carry):
        s = STEP * k + 2
        mp, mc = both(m2, s - 1), both(m2, s)
        face = level2_face(consts, mp, mc)
        for d in range(STEP):
            mn = both(m2, s + d + 1)
            w, face = level2_plane(consts, face, mc, mn)
            for p in range(2):
                d2[s + d, p] = OMEGA / (total_weight(w[p]) + SIGMA * 16.0)
            if d % 2:
                sum_m[(STEP // 2) * k + d // 2] = (mp[0] + mp[1]) + (mc[0] + mc[1])
            mp, mc = mc, mn
        return carry

    lax.fori_loop(0, AZ2 // STEP, diagonals, 0)
    close_ring(d2)
    m3[1 : HALF + 1] = 0.125 * packed(sum_m)
    wrap(m3)
    lane = iota((G2, R2), 1) % (R2 // 2)
    ca, ri, ro = radial_consts((G2, R2), R2 // 2, 2.0 * math.pi / AZ3, lane)
    zlo, zhi = height_walls()
    mp, mc = m3[0], m3[1]
    for i in range(HALF):
        mn = m3[i + 2]
        w = (
            ca * (mc + mp),
            ca * (mc + mn),
            zlo * (mc + pltpu.roll(mc, 1, 0)),
            zhi * (mc + pltpu.roll(mc, G2 - 1, 0)),
            ri * (mc + pltpu.roll(mc, 1, 1)),
            ro * (mc + pltpu.roll(mc, R2 - 1, 1)),
        )
        scale = OMEGA / (total_weight(w) + SIGMA * 64.0)
        for f in range(6):
            w3[f, i] = w[f] * scale
        w3[6, i] = scale
        mp, mc = mc, mn


def coarse(
    own, oth, bw, vw, mw, cx, cc, kx, kc, rhs_ref, v_ref, m_ref, ax, ac, az, ay, bx, bc, bz, by,
    out_ref, sx, sc, sz, sy,
    m2, d2, w3, sum_m, m3, b2, v2, sum_r, add, va, vb, e2, v2f, src, v1f, e_ref,
):
    coarse_weights(own, oth, m2, d2, w3, sum_m, m3)
    a, g = position()
    pa = a % 2
    rows = A2 * H2

    def lay(own, oth):
        for k in range(N_AZ):
            base = (k // 2) * N_GZ * 2 * rows
            ref = oth if k % 2 else own
            for i in range(A2):
                s = k * A2 + i + 2
                for p in range(2):
                    b = ref[pl.ds(base + i * 2 + p, G2, stride=2 * rows), :]
                    b2[s, p] = b
                    v2[s, p] = b * d2[s, p]

    pl.when(pa == 0)(lambda: lay(own, oth))
    pl.when(pa == 1)(lambda: lay(oth, own))
    close_ring(b2)
    close_ring(v2)
    consts = level2_consts()

    def residuals(k, carry):
        s = STEP * k + 2
        mc = both(m2, s)
        vp, vc = both(v2, s - 1), both(v2, s)
        face = level2_face(consts, both(m2, s - 1), mc)
        total = None
        for d in range(STEP):
            mn, vn = both(m2, s + d + 1), both(v2, s + d + 1)
            w, face = level2_plane(consts, face, mc, mn)
            n = level2_around(vp, vc, vn)
            b = both(b2, s + d)
            r = ((1.0 - OMEGA) * (b[0] + b[1]) + weighted(w[0], n[0])) + weighted(w[1], n[1])
            if d % 2:
                sum_r[(STEP // 2) * k + d // 2] = total + r
            total, mc, vp, vc = r, mn, vc, vn
        return carry

    lax.fori_loop(0, AZ2 // STEP, residuals, 0)

    b3 = 0.5 * packed(sum_r)
    for i in range(HALF):
        start = b3[i] * w3[6, i]
        add[i] = start
        va[i + 1] = start
    wrap(va)

    def sweep(src_ref, dst_ref):
        vp, vc = src_ref[0], src_ref[1]
        for i in range(HALF):
            vn = src_ref[i + 2]
            n = (
                vp,
                vn,
                pltpu.roll(vc, 1, 0),
                pltpu.roll(vc, G2 - 1, 0),
                pltpu.roll(vc, 1, 1),
                pltpu.roll(vc, R2 - 1, 1),
            )
            w = [w3[f, i] for f in range(6)]
            dst_ref[i + 1] = ((1.0 - OMEGA) * vc + add[i]) + weighted(w, n)
            vp, vc = vc, vn
        wrap(dst_ref)

    def two(k, carry):
        sweep(va, vb)
        sweep(vb, va)
        return carry

    lax.fori_loop(0, (COARSE_SWEEPS - 2) // 2, two, 0)
    sweep(va, vb)

    row_i, col_i = iota((R2, R2), 0), iota((R2, R2), 1)
    solved = vb[1 : HALF + 1].reshape(HALF * G2, R2)
    e2[0:HALF] = dot(solved, hot(row_i == col_i // 2)).reshape(HALF, G2, R2)
    e2[HALF:AZ3] = dot(solved, hot(row_i == col_i // 2 + R2 // 2)).reshape(HALF, G2, R2)

    at = a * A2
    values = []
    for k in range(A2 + 4):
        e = e2[(a * (A2 // 2) - 1 + k // 2 + AZ3) % AZ3]
        values.append((v2[at + k, 0] + e, v2[at + k, 1] + e))
    mc = both(m2, at + 1)
    face = level2_face(consts, both(m2, at), mc)
    for k in range(1, A2 + 3):
        mn = both(m2, at + k + 1)
        w, face = level2_plane(consts, face, mc, mn)
        n = level2_around(*values[k - 1 : k + 2])
        for p in range(2):
            gain = b2[at + k, p] + weighted(w[p], n[p])
            v2f[k - 1, p] = (1.0 - OMEGA) * values[k][p] + d2[at + k, p] * gain
        mc = mn

    low, high = jnp.maximum(g - 1, 0), jnp.minimum(g + 1, N_GZ - 1)
    for j in range(A2 + 2):
        for q, (p, row) in enumerate(((1, low), (0, g), (1, g), (0, high))):
            src[4 * j + q : 4 * j + q + 1, :] = v2f[j, p, pl.ds(row, 1), :]
    o, c = iota((8 * (A2 + 2), 4 * (A2 + 2)), 0), iota((8 * (A2 + 2), 4 * (A2 + 2)), 1)
    e1 = dot(hot(o // 2 == c), dot(src[...], dup_cols(R2)))
    halo, corners = Halo(cx, cc, None, None), Halo(kx, kc, None, None)

    def v1_of(i):
        j = (i + 2) // 2
        return wide_planes(vw, halo, 0, i, corners) + e1[T1 * j : T1 * (j + 1)]

    def emit1(i, diagonal, around, centre):
        b = wide_planes(bw, halo, 2, i)
        at = (i + 1) * T1
        v1f[at : at + T1, :] = (1.0 - OMEGA) * centre + OMEGA * (b + around) / diagonal

    level1_walk(lambda i: wide_planes(mw, halo, 1, i, corners), v1_of, -1, A1 + 2, emit1)

    own_rows = (A1 + 2) * NH
    shape = (own_rows + 2 * A1, (A1 + 2) * T1)
    o, c = iota(shape, 0), iota(shape, 1)
    j = jnp.where(o < own_rows, o // NH, (o - own_rows) % A1 + 1)
    h = jnp.where(o < own_rows, (o % NH) // 2 + 2, jnp.where(o < own_rows + A1, 1, H1 + 2))
    e_ref[...] = dot(dot(hot(c == j * T1 + h), v1f[...]), dup_cols(R1))
    ah, bh = Halo(ax, ac, az, ay), Halo(bx, bc, bz, by)
    m_of, mb, ma = fine_mobility(m_ref, ah)
    old, ob, oa = fine_values(v_ref, bh)

    def v_of(i):
        at = (i // 2 + 1) * NH
        return old(i) + e_ref[at : at + NH, :]

    def around_row(value, start):
        def row(i):
            at = start + i // 2
            return value(i) + e_ref[at : at + 1, :]

        return row

    def emit(i, diagonal, around, centre):
        out_ref[i] = (1.0 - OMEGA) * centre + OMEGA * (rhs_ref[i] + around) / diagonal

    fine_walk(
        m_of, v_of, mb, ma, around_row(ob, own_rows), around_row(oa, own_rows + A1), emit
    )
    store_faces(out_ref, sx, sc, sz, sy)


def final(rhs_ref, v_ref, m_ref, ax, ac, az, ay, gx, gc, gz, gy, p_hbm, out_hbm, out_ref, sems):
    part = NA // 4
    copies = [
        pltpu.make_async_copy(
            src.at[pl.ds(k * part, part)], dst.at[pl.ds(k * part, part)], sems.at[4 * n + k]
        )
        for n, (src, dst) in enumerate(((v_ref, p_hbm), (out_ref, out_hbm)))
        for k in range(4)
    ]
    for copy in copies[:4]:
        copy.start()
    ah, gh = Halo(ax, ac, az, ay), Halo(gx, gc, gz, gy)
    m_of, mb, ma = fine_mobility(m_ref, ah)
    v_of, vb, va = fine_values(v_ref, gh)

    def emit(i, diagonal, around, centre):
        out_ref[i] = (rhs_ref[i] - diagonal * centre + around) / diagonal
        if i % part == part - 1:
            copies[4 + i // part].start()

    fine_walk(m_of, v_of, mb, ma, vb, va, emit)
    for copy in copies:
        copy.wait()


def swap(x, axis, odd):
    n = lax.axis_size(axis)
    pairs = []
    for i in range(n):
        partner = i ^ 1 if odd == 0 else ((i + 1) % n if i % 2 else (i - 1) % n)
        pairs.append((i, partner))
    return lax.ppermute(x, axis, pairs)


def exchange(sx, sc, sz, sy):
    return swap(sx, "az", 1), swap(sc, "az", 0), swap(sz, "gz", 0), swap(sy, "gz", 1)


def gathered(x, sides):
    groups = [[a * N_GZ + g for a in range(c, N_AZ, 2) for g in range(N_GZ)] for c in range(2)]
    own = lax.all_to_all(x, ("az", "gz"), 0, 0, tiled=True, axis_index_groups=groups)
    own = own.reshape(own.shape[0] * own.shape[1], own.shape[2])
    own, *sides = lax.optimization_barrier((own, *sides))
    return own, swap(own, "az", 0), sides


def faces(planes, rows, width):
    return [struct(planes, width)] * 2 + [struct(rows, width)] * 2


def vmem(*shape):
    return pltpu.VMEM(shape, F32)


def body(pressure, divergence, void_fraction, bubble_volume, bubble_count, bubble_cell):
    block = struct(NA, NH, NR)
    wide = struct(A1, T1, R1)
    cell = bubble_cell.reshape(1, SLOTS)
    volume = bubble_volume.reshape(1, SLOTS)
    pairs = vmem(A1 * NH, NR)
    halves = vmem(A2 * T1, R1)

    m0, m1, m2 = call(
        mobilities, [block, wide, struct(A2 * H2, R2)], (void_fraction,), [pairs, halves]
    )
    send = call(
        first_faces,
        faces(3 * NH, 2 * NA + A1, NR),
        (pressure, m0, m1, volume, bubble_count),
        smem=(4,),
    )
    ha = exchange(*send)
    rhs, v0, *send = call(
        presmooth, [block, block] + faces(NH, NA, NR), (pressure, divergence, m0, cell, *ha)
    )
    hb = exchange(*send)
    b1, v1, *send = call(
        restrict,
        [wide, wide] + faces(5 * T1, 5 * A1, R1),
        (rhs, v0, m0, m1, *ha, *hb),
        [pairs],
    )
    hc = exchange(*send)
    copies, b1, v1, m1, kx, kc = call(
        restrict1,
        [struct(64, 2 * A2 * H2, R2), wide, wide, wide] + [struct(2 * T1, R1)] * 2,
        (b1, v1, m1, m2, *hc),
        [halves],
    )
    corners = swap(kx, "az", 1), swap(kc, "az", 0)
    own, oth, corners = gathered(copies, corners)
    ring = vmem(AZ2 + 4, 2, G2, R2)
    ends = vmem(HALF + 2, G2, R2)
    third = vmem(AZ3, G2, R2)
    out, *send = call(
        coarse,
        [block] + faces(NH, NA, NR),
        (own, oth, b1, v1, m1, *hc[:2], *corners, rhs, v0, m0, *ha, *hb),
        [
            ring,
            ring,
            vmem(7, HALF, G2, R2),
            third,
            ends,
            ring,
            ring,
            third,
            vmem(HALF, G2, R2),
            ends,
            ends,
            third,
            vmem(A2 + 2, 2, G2, R2),
            vmem(4 * (A2 + 2), R2),
            vmem((A1 + 2) * T1, R1),
            vmem((A1 + 2) * NH + 2 * A1, NR),
        ],
    )
    hg = exchange(*send)
    return tuple(
        call(
            final,
            [block, block],
            (rhs, out, m0, *ha, *hg),
            [vmem(NA, NH, NR), pltpu.SemaphoreType.DMA((8,))],
            hbm_out=(0, 1),
        )
    )


def solution(mesh):
    return jax.shard_map(
        body,
        mesh=mesh,
        in_specs=(
            P("az", "gz", None),
            P("az", "gz", None),
            P("az", "gz", None),
            P(("az", "gz")),
            P(("az", "gz")),
            P(("az", "gz")),
        ),
        out_specs=(P("az", "gz", None), P("az", "gz", None)),
        check_vma=False,
    )
```

```python
import functools
import math

import jax
import jax.numpy as jnp
from jax import lax
from jax.experimental import pallas as pl
from jax.experimental.pallas import tpu as pltpu
from jax.sharding import PartitionSpec as P

SIGMA = 0.02
OMEGA = 0.8
COARSE_SWEEPS = 32
F32 = jnp.float32
BF16 = jnp.bfloat16

NA, NH, NR = 32, 8, 512
A1, H1, R1 = 16, 4, 256
A2, H2, R2 = 8, 2, 128
AZ2, G2 = 128, 8
AZ3 = 64
N_AZ, N_GZ = 16, 8
SLOTS = 128


def struct(*shape):
    return jax.ShapeDtypeStruct(shape, F32)


def call(kernel, outs, ins, scratch=(), smem=(), hbm=(), hbm_out=(), limit=16):
    def space(i, far):
        return pltpu.HBM if i in far else pltpu.SMEM if i in smem else pltpu.VMEM

    specs = [pl.BlockSpec(memory_space=space(i, hbm)) for i in range(len(ins))]
    return pl.pallas_call(
        kernel,
        out_shape=outs,
        in_specs=specs,
        out_specs=[
            pl.BlockSpec(memory_space=pltpu.HBM if i in hbm_out else pltpu.VMEM)
            for i in range(len(outs))
        ],
        scratch_shapes=list(scratch),
        compiler_params=pltpu.CompilerParams(vmem_limit_bytes=limit * 1024 * 1024),
    )(*ins)


def iota(shape, dim):
    return lax.broadcasted_iota(jnp.int32, shape, dim)


def parts(x):
    high = x.astype(BF16)
    rest = x - high.astype(F32)
    mid = rest.astype(BF16)
    return high, mid, (rest - mid.astype(F32)).astype(BF16)


def dot(a, b):
    if b.dtype == BF16:
        p = [jnp.dot(x, b, preferred_element_type=F32) for x in parts(a)]
    else:
        p = [jnp.dot(a, x, preferred_element_type=F32) for x in parts(b)]
    return (p[2] + p[1]) + p[0]


def radial_consts(shape, size, step, rad):
    i = rad.astype(F32)
    metric = ((i + 0.5) * step) ** 2
    ca = 0.5 / metric
    ri = jnp.where(rad > 0, 0.5 * i / (i + 0.5), 0.0)
    ro = jnp.where(rad < size - 1, 0.5 * (i + 1.0) / (i + 0.5), 0.0)
    return ca, ri, ro


def hot(mask):
    return mask.astype(F32).astype(BF16)


def pair_cols(n):
    return hot(iota((n, n // 2), 0) // 2 == iota((n, n // 2), 1))


def dup_cols(n):
    return hot(iota((n, 2 * n), 0) == iota((n, 2 * n), 1) // 2)


def row_sums(planes, out, first, per):
    o, r = iota((planes * out, planes * per), 0), iota((planes * out, planes * per), 1)
    h = r % per - first
    return hot((o // out == r // per) & (h >= 0) & (h // 2 == o % out))


def widened(planes):
    o, r = iota((planes * 8, planes * 8), 0), iota((planes * 8, planes * 8), 1)
    return hot((o // 8 == r // 8) & (o % 8 == (r % 8) // 2 + 2))


def position():
    return lax.axis_index("az"), lax.axis_index("gz")


def pick(par, even, odd):
    return jnp.where(par == 0, even, odd)


class Halo:
    def __init__(self, x_ref, c_ref, z_ref, y_ref):
        a, g = position()
        self.pa, self.pg = a % 2, g % 2
        self.x, self.c, self.z, self.y = x_ref, c_ref, z_ref, y_ref

    def prev(self, rows, lanes):
        return pick(self.pa, self.x[rows, lanes], self.c[rows, lanes])

    def next(self, rows, lanes):
        return pick(self.pa, self.c[rows, lanes], self.x[rows, lanes])

    def below(self, rows, lanes):
        return pick(self.pg, self.y[rows, lanes], self.z[rows, lanes])

    def above(self, rows, lanes):
        return pick(self.pg, self.z[rows, lanes], self.y[rows, lanes])


def fine_walk(m_of, v_of, mb, ma, vb, va, emit):
    a, g = position()
    sub = iota((NH, NR), 0)
    lane = iota((NH, NR), 1)
    ca, ri, ro = radial_consts((NH, NR), NR, 2.0 * math.pi / (NA * N_AZ), lane)
    zlo = jnp.where((sub == 0) & (g == 0), 0.0, 0.5)
    zhi = jnp.where((sub == NH - 1) & (g == N_GZ - 1), 0.0, 0.5)
    first, final = sub == 0, sub == NH - 1
    mp, mc = m_of(-1), m_of(0)
    vp, vc = v_of(-1), v_of(0)
    wa = ca * (mp + mc)
    for i in range(NA):
        mn, vn = m_of(i + 1), v_of(i + 1)
        wan = ca * (mc + mn)
        m_lo = jnp.where(first, mb(i), pltpu.roll(mc, 1, 0))
        m_hi = jnp.where(final, ma(i), pltpu.roll(mc, NH - 1, 0))
        v_lo = jnp.where(first, vb(i), pltpu.roll(vc, 1, 0))
        v_hi = jnp.where(final, va(i), pltpu.roll(vc, NH - 1, 0))
        wl, wh = zlo * (mc + m_lo), zhi * (mc + m_hi)
        wi = ri * (mc + pltpu.roll(mc, 1, 1))
        wo = ro * (mc + pltpu.roll(mc, NR - 1, 1))
        diagonal = (wa + wan) + (wl + wh) + (wi + wo) + SIGMA
        around = (wa * vp + wan * vn) + (wl * v_lo + wh * v_hi)
        around = around + (wi * pltpu.roll(vc, 1, 1) + wo * pltpu.roll(vc, NR - 1, 1))
        emit(i, diagonal, around, vc)
        mp, mc, vp, vc, wa = mc, mn, vc, vn, wan


T1 = 8


def level1_walk(m_of, v_of, first, count, emit):
    a, g = position()
    sub = iota((T1, R1), 0)
    lane = iota((T1, R1), 1)
    height = g * H1 + sub - 2
    ca, ri, ro = radial_consts((T1, R1), R1, 2.0 * math.pi / (A1 * N_AZ), lane)
    zlo = jnp.where(height <= 0, 0.0, 0.5)
    zhi = jnp.where(height >= H1 * N_GZ - 1, 0.0, 0.5)
    mp, mc = m_of(first - 1), m_of(first)
    if v_of is not None:
        vp, vc = v_of(first - 1), v_of(first)
    wa = ca * (mp + mc)
    for i in range(first, first + count):
        mn = m_of(i + 1)
        wan = ca * (mc + mn)
        w = (
            wa,
            wan,
            zlo * (mc + pltpu.roll(mc, 1, 0)),
            zhi * (mc + pltpu.roll(mc, T1 - 1, 0)),
            ri * (mc + pltpu.roll(mc, 1, 1)),
            ro * (mc + pltpu.roll(mc, R1 - 1, 1)),
        )
        diagonal = total_weight(w) + SIGMA * 4.0
        if v_of is None:
            emit(i, diagonal, None, None)
        else:
            vn = v_of(i + 1)
            n = (
                vp,
                vn,
                pltpu.roll(vc, 1, 0),
                pltpu.roll(vc, T1 - 1, 0),
                pltpu.roll(vc, 1, 1),
                pltpu.roll(vc, R1 - 1, 1),
            )
            emit(i, diagonal, weighted(w, n), vc)
            vp, vc = vc, vn
        mp, mc, wa = mc, mn, wan


def weighted(w, n):
    return (w[0] * n[0] + w[1] * n[1]) + (w[2] * n[2] + w[3] * n[3]) + (w[4] * n[4] + w[5] * n[5])


ALL = slice(None)


def store_faces(ref, x_ref, c_ref, z_ref, y_ref, planes_at=0, rows_at=0):
    a, g = position()
    pa, pg = a % 2, g % 2
    c_plane = jnp.where(pa == 0, NA - 1, 0)
    x_plane = NA - 1 - c_plane
    c_ref[planes_at : planes_at + NH, :] = ref[c_plane]
    x_ref[planes_at : planes_at + NH, :] = ref[x_plane]
    z_row = jnp.where(pg == 0, NH - 1, 0)
    y_row = NH - 1 - z_row
    for i in range(NA):
        z_ref[rows_at + i : rows_at + i + 1, :] = ref[i, pl.ds(z_row, 1), :]
        y_ref[rows_at + i : rows_at + i + 1, :] = ref[i, pl.ds(y_row, 1), :]


def mobilities(void_ref, m0_ref, m1_ref, m2_ref, pairs, halves):
    for i in range(0, NA, 2):
        u = 1.0 / (1.0 - void_ref[i])
        v = 1.0 / (1.0 - void_ref[i + 1])
        m0_ref[i] = u
        m0_ref[i + 1] = v
        pairs[(i // 2) * NH : (i // 2 + 1) * NH, :] = u + v
    m1_ref[...] = 0.125 * dot(widened(A1), dot(pairs[...], pair_cols(NR))).reshape(A1, T1, R1)
    for i in range(A2):
        halves[i * T1 : (i + 1) * T1, :] = m1_ref[2 * i] + m1_ref[2 * i + 1]
    m2_ref[...] = 0.125 * dot(row_sums(A2, H2, 2, T1), dot(halves[...], pair_cols(R1)))


def first_faces(p_ref, m0_ref, m1_ref, vol_ref, cnt_ref, sx, sc, sz, sy):
    a, g = position()
    pa, pg = a % 2, g % 2
    store_faces(p_ref, sx, sc, sz, sy, 0, 0)
    store_faces(m0_ref, sx, sc, sz, sy, NH, NA)
    rest = slice(2 * NH, 3 * NH)
    sx[rest, R1:NR] = jnp.zeros((NH, NR - R1), F32)
    sc[rest, R1:NR] = jnp.zeros((NH, NR - R1), F32)
    c_plane = jnp.where(pa == 0, A1 - 1, 0)
    sc[rest, 0:R1] = m1_ref[c_plane]
    sx[rest, 0:R1] = m1_ref[A1 - 1 - c_plane]
    for ref in (sz, sy):
        ref[2 * NA : 2 * NA + A1, R1:NR] = jnp.zeros((A1, NR - R1), F32)
    z_row = jnp.where(pg == 0, H1 + 1, 2)
    for i in range(A1):
        at = slice(2 * NA + i, 2 * NA + i + 1)
        sz[at, 0:R1] = m1_ref[i, pl.ds(z_row, 1), :]
        sy[at, 0:R1] = m1_ref[i, pl.ds(H1 + 3 - z_row, 1), :]
    live = jnp.where(iota((1, SLOTS), 1) < cnt_ref[0], vol_ref[...], 0.0)
    for ref in (sx, sc):
        ref[2 * NH : 2 * NH + 1, R1 : R1 + SLOTS] = live


def fine_mobility(m_ref, ah):
    def m_of(i):
        if i < 0:
            return ah.prev(slice(NH, 2 * NH), ALL)
        if i >= NA:
            return ah.next(slice(NH, 2 * NH), ALL)
        return m_ref[i]

    return (
        m_of,
        lambda i: ah.below(slice(NA + i, NA + i + 1), ALL),
        lambda i: ah.above(slice(NA + i, NA + i + 1), ALL),
    )


def fine_values(v_ref, vh):
    def v_of(i):
        if i < 0:
            return vh.prev(slice(0, NH), ALL)
        if i >= NA:
            return vh.next(slice(0, NH), ALL)
        return v_ref[i]

    return (
        v_of,
        lambda i: vh.below(slice(i, i + 1), ALL),
        lambda i: vh.above(slice(i, i + 1), ALL),
    )


def presmooth(p_ref, div_ref, m_ref, cell_ref, ax, ac, az, ay, rhs_ref, v_ref, sx, sc, sz, sy):
    ah = Halo(ax, ac, az, ay)
    arrived = ah.prev(slice(2 * NH, 2 * NH + 1), slice(R1, R1 + SLOTS))
    cell = cell_ref[...]
    plane_hot = hot(iota((NA * NH, SLOTS), 0) == lax.shift_right_logical(cell, 9))
    radius_hot = jnp.where(iota((NR, SLOTS), 0) == (cell & (NR - 1)), arrived, 0.0)
    deposit = [
        lax.dot_general(plane_hot, x, (((1,), (1,)), ((), ())), preferred_element_type=F32)
        for x in parts(radius_hot)
    ]
    deposit = (deposit[2] + deposit[1]) + deposit[0]
    rhs_ref[...] = div_ref[...] + deposit.reshape(NA, NH, NR)
    m_of, mb, ma = fine_mobility(m_ref, ah)
    v_of, vb, va = fine_values(p_ref, ah)

    def emit(i, diagonal, around, centre):
        v_ref[i] = (1.0 - OMEGA) * centre + OMEGA * (rhs_ref[i] + around) / diagonal

    fine_walk(m_of, v_of, mb, ma, vb, va, emit)
    store_faces(v_ref, sx, sc, sz, sy)


def restrict(
    rhs_ref, v_ref, m_ref, m1_ref, ax, ac, az, ay, bx, bc, bz, by, b1_ref, v1_ref, sx, sc, sz, sy, pairs
):
    ah, bh = Halo(ax, ac, az, ay), Halo(bx, bc, bz, by)
    m_of, mb, ma = fine_mobility(m_ref, ah)
    v_of, vb, va = fine_values(v_ref, bh)
    kept = []

    def emit(i, diagonal, around, centre):
        r = rhs_ref[i] - diagonal * centre + around
        if i % 2 == 0:
            kept.append(r)
        else:
            pairs[(i // 2) * NH : (i // 2 + 1) * NH, :] = kept.pop() + r

    fine_walk(m_of, v_of, mb, ma, vb, va, emit)
    b1_ref[...] = 0.5 * dot(widened(A1), dot(pairs[...], pair_cols(NR))).reshape(A1, T1, R1)

    sub = iota((T1, R1), 0)

    def m1_of(i):
        if i < 0:
            return ah.prev(slice(2 * NH, 3 * NH), slice(0, R1))
        if i >= A1:
            return ah.next(slice(2 * NH, 3 * NH), slice(0, R1))
        at = slice(2 * NA + i, 2 * NA + i + 1)
        below, above = ah.below(at, slice(0, R1)), ah.above(at, slice(0, R1))
        return jnp.where(sub == 1, below, jnp.where(sub == H1 + 2, above, m1_ref[i]))

    def emit1(i, diagonal, around, centre):
        v1_ref[i] = OMEGA * b1_ref[i] / diagonal

    level1_walk(m1_of, None, 0, A1, emit1)
    a, g = position()
    for layer in range(2):
        c_plane = jnp.where(a % 2 == 0, A1 - 1 - layer, layer)
        z_row = jnp.where(g % 2 == 0, H1 + 1 - layer, 2 + layer)
        y_row = H1 + 3 - z_row
        sources = (v1_ref, m1_ref) if layer else (v1_ref, m1_ref, b1_ref)
        for n, ref in enumerate(sources):
            for i in range(A1):
                at = (2 * n + layer) * A1 + i
                sz[at : at + 1, :] = ref[i, pl.ds(z_row, 1), :]
                sy[at : at + 1, :] = ref[i, pl.ds(y_row, 1), :]
            at = (2 * n + layer) * T1
            sc[at : at + T1, :] = ref[c_plane]
            sx[at : at + T1, :] = ref[A1 - 1 - c_plane]


def widen(pairs, halo):
    sub = iota((T1, R1), 0)
    for n, (src, dst) in enumerate(pairs):
        for i in range(A1):
            tile = src[i]
            for layer in range(2 if n < 2 else 1):
                at = (2 * n + layer) * A1 + i
                at = slice(at, at + 1)
                tile = jnp.where(sub == 1 - layer, halo.below(at, ALL), tile)
                tile = jnp.where(sub == H1 + 2 + layer, halo.above(at, ALL), tile)
            dst[i] = tile


def wide_planes(ref, halo, n, i, corners=None):
    if corners is not None and i == -1:
        return corners.prev(slice(n * T1, (n + 1) * T1), ALL)
    if corners is not None and i == A1:
        return corners.next(slice(n * T1, (n + 1) * T1), ALL)
    if i < 0:
        at = (2 * n - 1 - i) * T1
        return halo.prev(slice(at, at + T1), ALL)
    if i >= A1:
        at = (2 * n + i - A1) * T1
        return halo.next(slice(at, at + T1), ALL)
    return ref[i]


def restrict1(
    b1_ref, v1_ref, m1_ref, m2_ref, cx, cc, cz, cy,
    out_hbm, sx, sc,
    bw, vw, mw, halves, several, sems,
):
    halo = Halo(cx, cc, cz, cy)
    widen(((v1_ref, vw), (m1_ref, mw), (b1_ref, bw)), halo)
    c_plane = jnp.where(lax.axis_index("az") % 2 == 0, A1 - 1, 0)
    for n, ref in enumerate((vw, mw)):
        sc[n * T1 : (n + 1) * T1, :] = ref[c_plane]
        sx[n * T1 : (n + 1) * T1, :] = ref[A1 - 1 - c_plane]
    kept = []

    def emit(i, diagonal, around, centre):
        r = (1.0 - OMEGA) * bw[i] + around
        if i % 2 == 0:
            kept.append(r)
        else:
            halves[(i // 2) * T1 : (i // 2 + 1) * T1, :] = kept.pop() + r

    level1_walk(
        lambda i: wide_planes(mw, halo, 1, i), lambda i: wide_planes(vw, halo, 0, i), 0, A1, emit
    )
    b2 = 0.5 * dot(row_sums(A2, H2, 2, T1), dot(halves[...], pair_cols(R1)))
    m2 = m2_ref[...]
    rows = A2 * H2
    count = several.shape[0]
    for k in range(count):
        several[k, 0:rows, :] = b2
        several[k, rows : 2 * rows, :] = m2
    writes = [
        pltpu.make_async_copy(several, out_hbm.at[pl.ds(k * count, count)], sems.at[k])
        for k in range(out_hbm.shape[0] // count)
    ]
    for write in writes:
        write.start()
    for write in writes:
        write.wait()


def hand_on(own, kx, kc, out):
    pass


def level2_plane(consts, face, mc, mn):
    ca, ri, ro, zlo, zhi = consts
    mid = 0.5 * (mc[0] + mc[1])
    lows = (zlo * (mc[0] + pltpu.roll(mc[1], 1, 0)), mid)
    highs = (mid, zhi * (mc[1] + pltpu.roll(mc[0], G2 - 1, 0)))
    nxt = level2_face(consts, mc, mn)
    out = []
    for p in range(2):
        m = mc[p]
        wi, wo = ri * (m + pltpu.roll(m, 1, 1)), ro * (m + pltpu.roll(m, R2 - 1, 1))
        out.append((face[p], nxt[p], lows[p], highs[p], wi, wo))
    return out, nxt


def level2_face(consts, mp, mc):
    return (consts[0] * (mp[0] + mc[0]), consts[0] * (mp[1] + mc[1]))


def level2_around(vp, vc, vn):
    lows = (pltpu.roll(vc[1], 1, 0), vc[0])
    highs = (vc[1], pltpu.roll(vc[0], G2 - 1, 0))
    return [
        (vp[p], vn[p], lows[p], highs[p], pltpu.roll(vc[p], 1, 1), pltpu.roll(vc[p], R2 - 1, 1))
        for p in range(2)
    ]


def total_weight(w):
    return (w[0] + w[1]) + (w[2] + w[3]) + (w[4] + w[5])


def height_walls():
    sub = iota((G2, R2), 0)
    return jnp.where(sub == 0, 0.0, 0.5), jnp.where(sub == G2 - 1, 0.0, 0.5)


def level2_consts():
    lane = iota((G2, R2), 1)
    return radial_consts((G2, R2), R2, 2.0 * math.pi / AZ2, lane) + height_walls()


def both(ref, s):
    return (ref[s, 0], ref[s, 1])


def close_ring(ref):
    ref[0:2] = ref[AZ2 : AZ2 + 2]
    ref[AZ2 + 2 : AZ2 + 4] = ref[2:4]


HALF = AZ3 // 2


def packed(ref):
    row_i, col_i = iota((R2, R2), 0), iota((R2, R2), 1)
    left = hot(row_i // 2 == col_i)
    right = hot(row_i // 2 + R2 // 2 == col_i)
    lower = ref[0:HALF].reshape(HALF * G2, R2)
    upper = ref[HALF:AZ3].reshape(HALF * G2, R2)
    return (dot(lower, left) + dot(upper, right)).reshape(HALF, G2, R2)


def wrap(ref):
    ref[0] = pltpu.roll(ref[HALF], R2 // 2, 1)
    ref[HALF + 1] = pltpu.roll(ref[1], R2 // 2, 1)


STEP = 8


def coarse_weights(own, oth, m2, d2, w3, sum_m, m3):
    a, g = position()
    pa = a % 2
    rows = A2 * H2
    def lay(own, oth):
        for k in range(N_AZ):
            base = (k // 2) * N_GZ * 2 * rows + rows
            ref = oth if k % 2 else own
            for i in range(A2):
                for p in range(2):
                    at = pl.ds(base + i * 2 + p, G2, stride=2 * rows)
                    m2[k * A2 + i + 2, p] = ref[at, :]

    pl.when(pa == 0)(lambda: lay(own, oth))
    pl.when(pa == 1)(lambda: lay(oth, own))
    close_ring(m2)
    consts = level2_consts()

    def diagonals(k, carry):
        s = STEP * k + 2
        mp, mc = both(m2, s - 1), both(m2, s)
        face = level2_face(consts, mp, mc)
        for d in range(STEP):
            mn = both(m2, s + d + 1)
            w, face = level2_plane(consts, face, mc, mn)
            for p in range(2):
                d2[s + d, p] = OMEGA / (total_weight(w[p]) + SIGMA * 16.0)
            if d % 2:
                sum_m[(STEP // 2) * k + d // 2] = (mp[0] + mp[1]) + (mc[0] + mc[1])
            mp, mc = mc, mn
        return carry

    lax.fori_loop(0, AZ2 // STEP, diagonals, 0)
    close_ring(d2)
    m3[1 : HALF + 1] = 0.125 * packed(sum_m)
    wrap(m3)
    lane = iota((G2, R2), 1) % (R2 // 2)
    ca, ri, ro = radial_consts((G2, R2), R2 // 2, 2.0 * math.pi / AZ3, lane)
    zlo, zhi = height_walls()
    mp, mc = m3[0], m3[1]
    for i in range(HALF):
        mn = m3[i + 2]
        w = (
            ca * (mc + mp),
            ca * (mc + mn),
            zlo * (mc + pltpu.roll(mc, 1, 0)),
            zhi * (mc + pltpu.roll(mc, G2 - 1, 0)),
            ri * (mc + pltpu.roll(mc, 1, 1)),
            ro * (mc + pltpu.roll(mc, R2 - 1, 1)),
        )
        scale = OMEGA / (total_weight(w) + SIGMA * 64.0)
        for f in range(6):
            w3[f, i] = w[f] * scale
        w3[6, i] = scale
        mp, mc = mc, mn


def coarse(
    own, oth, b1_ref, v1_ref, m1_ref, cx, cc, cz, cy, kx, kc, rhs_ref, v_ref, m_ref, ax, ac, az, ay, bx, bc, bz, by,
    out_ref, sx, sc, sz, sy,
    m2, d2, w3, sum_m, m3, b2, v2, sum_r, add, va, vb, e2, v2f, src, v1f, e_ref, bw, vw, mw,
):
    coarse_weights(own, oth, m2, d2, w3, sum_m, m3)
    a, g = position()
    pa = a % 2
    rows = A2 * H2

    def lay(own, oth):
        for k in range(N_AZ):
            base = (k // 2) * N_GZ * 2 * rows
            ref = oth if k % 2 else own
            for i in range(A2):
                s = k * A2 + i + 2
                for p in range(2):
                    b = ref[pl.ds(base + i * 2 + p, G2, stride=2 * rows), :]
                    b2[s, p] = b
                    v2[s, p] = b * d2[s, p]

    pl.when(pa == 0)(lambda: lay(own, oth))
    pl.when(pa == 1)(lambda: lay(oth, own))
    close_ring(b2)
    close_ring(v2)
    consts = level2_consts()

    def residuals(k, carry):
        s = STEP * k + 2
        mc = both(m2, s)
        vp, vc = both(v2, s - 1), both(v2, s)
        face = level2_face(consts, both(m2, s - 1), mc)
        total = None
        for d in range(STEP):
            mn, vn = both(m2, s + d + 1), both(v2, s + d + 1)
            w, face = level2_plane(consts, face, mc, mn)
            n = level2_around(vp, vc, vn)
            b = both(b2, s + d)
            r = ((1.0 - OMEGA) * (b[0] + b[1]) + weighted(w[0], n[0])) + weighted(w[1], n[1])
            if d % 2:
                sum_r[(STEP // 2) * k + d // 2] = total + r
            total, mc, vp, vc = r, mn, vc, vn
        return carry

    lax.fori_loop(0, AZ2 // STEP, residuals, 0)

    b3 = 0.5 * packed(sum_r)
    for i in range(HALF):
        start = b3[i] * w3[6, i]
        add[i] = start
        va[i + 1] = start
    wrap(va)

    def sweep(src_ref, dst_ref):
        vp, vc = src_ref[0], src_ref[1]
        for i in range(HALF):
            vn = src_ref[i + 2]
            n = (
                vp,
                vn,
                pltpu.roll(vc, 1, 0),
                pltpu.roll(vc, G2 - 1, 0),
                pltpu.roll(vc, 1, 1),
                pltpu.roll(vc, R2 - 1, 1),
            )
            w = [w3[f, i] for f in range(6)]
            dst_ref[i + 1] = ((1.0 - OMEGA) * vc + add[i]) + weighted(w, n)
            vp, vc = vc, vn
        wrap(dst_ref)

    def two(k, carry):
        sweep(va, vb)
        sweep(vb, va)
        return carry

    lax.fori_loop(0, (COARSE_SWEEPS - 2) // 2, two, 0)
    sweep(va, vb)

    row_i, col_i = iota((R2, R2), 0), iota((R2, R2), 1)
    solved = vb[1 : HALF + 1].reshape(HALF * G2, R2)
    e2[0:HALF] = dot(solved, hot(row_i == col_i // 2)).reshape(HALF, G2, R2)
    e2[HALF:AZ3] = dot(solved, hot(row_i == col_i // 2 + R2 // 2)).reshape(HALF, G2, R2)

    at = a * A2
    values = []
    for k in range(A2 + 4):
        e = e2[(a * (A2 // 2) - 1 + k // 2 + AZ3) % AZ3]
        values.append((v2[at + k, 0] + e, v2[at + k, 1] + e))
    mc = both(m2, at + 1)
    face = level2_face(consts, both(m2, at), mc)
    for k in range(1, A2 + 3):
        mn = both(m2, at + k + 1)
        w, face = level2_plane(consts, face, mc, mn)
        n = level2_around(*values[k - 1 : k + 2])
        for p in range(2):
            gain = b2[at + k, p] + weighted(w[p], n[p])
            v2f[k - 1, p] = (1.0 - OMEGA) * values[k][p] + d2[at + k, p] * gain
        mc = mn

    low, high = jnp.maximum(g - 1, 0), jnp.minimum(g + 1, N_GZ - 1)
    for j in range(A2 + 2):
        for q, (p, row) in enumerate(((1, low), (0, g), (1, g), (0, high))):
            src[4 * j + q : 4 * j + q + 1, :] = v2f[j, p, pl.ds(row, 1), :]
    o, c = iota((8 * (A2 + 2), 4 * (A2 + 2)), 0), iota((8 * (A2 + 2), 4 * (A2 + 2)), 1)
    e1 = dot(hot(o // 2 == c), dot(src[...], dup_cols(R2)))
    halo, corners = Halo(cx, cc, cz, cy), Halo(kx, kc, None, None)
    widen(((v1_ref, vw), (m1_ref, mw), (b1_ref, bw)), halo)

    def v1_of(i):
        j = (i + 2) // 2
        return wide_planes(vw, halo, 0, i, corners) + e1[T1 * j : T1 * (j + 1)]

    def emit1(i, diagonal, around, centre):
        b = wide_planes(bw, halo, 2, i)
        at = (i + 1) * T1
        v1f[at : at + T1, :] = (1.0 - OMEGA) * centre + OMEGA * (b + around) / diagonal

    level1_walk(lambda i: wide_planes(mw, halo, 1, i, corners), v1_of, -1, A1 + 2, emit1)

    own_rows = (A1 + 2) * NH
    shape = (own_rows + 2 * A1, (A1 + 2) * T1)
    o, c = iota(shape, 0), iota(shape, 1)
    j = jnp.where(o < own_rows, o // NH, (o - own_rows) % A1 + 1)
    h = jnp.where(o < own_rows, (o % NH) // 2 + 2, jnp.where(o < own_rows + A1, 1, H1 + 2))
    e_ref[...] = dot(dot(hot(c == j * T1 + h), v1f[...]), dup_cols(R1))
    ah, bh = Halo(ax, ac, az, ay), Halo(bx, bc, bz, by)
    m_of, mb, ma = fine_mobility(m_ref, ah)
    old, ob, oa = fine_values(v_ref, bh)

    def v_of(i):
        at = (i // 2 + 1) * NH
        return old(i) + e_ref[at : at + NH, :]

    def around_row(value, start):
        def row(i):
            at = start + i // 2
            return value(i) + e_ref[at : at + 1, :]

        return row

    def emit(i, diagonal, around, centre):
        out_ref[i] = (1.0 - OMEGA) * centre + OMEGA * (rhs_ref[i] + around) / diagonal

    fine_walk(
        m_of, v_of, mb, ma, around_row(ob, own_rows), around_row(oa, own_rows + A1), emit
    )
    store_faces(out_ref, sx, sc, sz, sy)


def final(rhs_ref, v_ref, m_ref, ax, ac, az, ay, gx, gc, gz, gy, p_hbm, out_hbm, out_ref, sems):
    part = NA // 4
    copies = [
        pltpu.make_async_copy(
            src.at[pl.ds(k * part, part)], dst.at[pl.ds(k * part, part)], sems.at[4 * n + k]
        )
        for n, (src, dst) in enumerate(((v_ref, p_hbm), (out_ref, out_hbm)))
        for k in range(4)
    ]
    for copy in copies[:4]:
        copy.start()
    ah, gh = Halo(ax, ac, az, ay), Halo(gx, gc, gz, gy)
    m_of, mb, ma = fine_mobility(m_ref, ah)
    v_of, vb, va = fine_values(v_ref, gh)

    def emit(i, diagonal, around, centre):
        out_ref[i] = (rhs_ref[i] - diagonal * centre + around) / diagonal
        if i % part == part - 1:
            copies[4 + i // part].start()

    fine_walk(m_of, v_of, mb, ma, vb, va, emit)
    for copy in copies:
        copy.wait()


def swap(x, axis, odd):
    n = lax.axis_size(axis)
    pairs = []
    for i in range(n):
        partner = i ^ 1 if odd == 0 else ((i + 1) % n if i % 2 else (i - 1) % n)
        pairs.append((i, partner))
    return lax.ppermute(x, axis, pairs)


def exchange(sx, sc, sz, sy):
    return swap(sx, "az", 1), swap(sc, "az", 0), swap(sz, "gz", 0), swap(sy, "gz", 1)


def gathered(x, sides):
    groups = [[a * N_GZ + g for a in range(c, N_AZ, 2) for g in range(N_GZ)] for c in range(2)]
    own = lax.all_to_all(x, ("az", "gz"), 0, 0, tiled=True, axis_index_groups=groups)
    own = own.reshape(own.shape[0] * own.shape[1], own.shape[2])
    anywhere, near = pl.BlockSpec(memory_space=pl.ANY), pl.BlockSpec(memory_space=pltpu.VMEM)
    own = pl.pallas_call(
        hand_on,
        out_shape=struct(*own.shape),
        in_specs=[anywhere, near, near],
        out_specs=anywhere,
        input_output_aliases={0: 0},
    )(own, *sides)
    return own, swap(own, "az", 0)


def faces(planes, rows, width):
    return [struct(planes, width)] * 2 + [struct(rows, width)] * 2


def vmem(*shape):
    return pltpu.VMEM(shape, F32)


def body(pressure, divergence, void_fraction, bubble_volume, bubble_count, bubble_cell):
    block = struct(NA, NH, NR)
    wide = struct(A1, T1, R1)
    cell = bubble_cell.reshape(1, SLOTS)
    volume = bubble_volume.reshape(1, SLOTS)
    pairs = vmem(A1 * NH, NR)
    halves = vmem(A2 * T1, R1)

    m0, m1, m2 = call(
        mobilities, [block, wide, struct(A2 * H2, R2)], (void_fraction,), [pairs, halves]
    )
    send = call(
        first_faces,
        faces(3 * NH, 2 * NA + A1, NR),
        (pressure, m0, m1, volume, bubble_count),
        smem=(4,),
    )
    ha = exchange(*send)
    rhs, v0, *send = call(
        presmooth, [block, block] + faces(NH, NA, NR), (pressure, divergence, m0, cell, *ha)
    )
    hb = exchange(*send)
    b1, v1, *send = call(
        restrict,
        [wide, wide] + faces(5 * T1, 5 * A1, R1),
        (rhs, v0, m0, m1, *ha, *hb),
        [pairs],
    )
    hc = exchange(*send)
    planes = vmem(A1, T1, R1)
    copies, kx, kc = call(
        restrict1,
        [struct(64, 2 * A2 * H2, R2)] + [struct(2 * T1, R1)] * 2,
        (b1, v1, m1, m2, *hc),
        [
            planes,
            planes,
            planes,
            halves,
            vmem(8, 2 * A2 * H2, R2),
            pltpu.SemaphoreType.DMA((8,)),
        ],
        hbm_out=(0,),
    )
    corners = swap(kx, "az", 1), swap(kc, "az", 0)
    own, oth = gathered(copies, corners)
    ring = vmem(AZ2 + 4, 2, G2, R2)
    ends = vmem(HALF + 2, G2, R2)
    third = vmem(AZ3, G2, R2)
    out, *send = call(
        coarse,
        [block] + faces(NH, NA, NR),
        (own, oth, b1, v1, m1, *hc, *corners, rhs, v0, m0, *ha, *hb),
        [
            ring,
            ring,
            vmem(7, HALF, G2, R2),
            third,
            ends,
            ring,
            ring,
            third,
            vmem(HALF, G2, R2),
            ends,
            ends,
            third,
            vmem(A2 + 2, 2, G2, R2),
            vmem(4 * (A2 + 2), R2),
            vmem((A1 + 2) * T1, R1),
            vmem((A1 + 2) * NH + 2 * A1, NR),
            planes,
            planes,
            planes,
        ],
        limit=24,
    )
    hg = exchange(*send)
    return tuple(
        call(
            final,
            [block, block],
            (rhs, out, m0, *ha, *hg),
            [vmem(NA, NH, NR), pltpu.SemaphoreType.DMA((8,))],
            hbm_out=(0, 1),
        )
    )


def solution(mesh):
    return jax.shard_map(
        body,
        mesh=mesh,
        in_specs=(
            P("az", "gz", None),
            P("az", "gz", None),
            P("az", "gz", None),
            P(("az", "gz")),
            P(("az", "gz")),
            P(("az", "gz")),
        ),
        out_specs=(P("az", "gz", None), P("az", "gz", None)),
        check_vma=False,
    )
```

```python
import functools
import math

import jax
import jax.numpy as jnp
from jax import lax
from jax.experimental import pallas as pl
from jax.experimental.pallas import tpu as pltpu
from jax.sharding import PartitionSpec as P

SIGMA = 0.02
OMEGA = 0.8
COARSE_SWEEPS = 32
F32 = jnp.float32
BF16 = jnp.bfloat16

NA, NH, NR = 32, 8, 512
A1, H1, R1 = 16, 4, 256
A2, H2, R2 = 8, 2, 128
AZ2, G2 = 128, 8
AZ3 = 64
N_AZ, N_GZ = 16, 8
SLOTS = 128


def struct(*shape):
    return jax.ShapeDtypeStruct(shape, F32)


def call(kernel, outs, ins, scratch=(), smem=(), hbm=(), hbm_out=(), limit=48):
    def space(i, far):
        return pltpu.HBM if i in far else pltpu.SMEM if i in smem else pltpu.VMEM

    specs = [pl.BlockSpec(memory_space=space(i, hbm)) for i in range(len(ins))]
    return pl.pallas_call(
        kernel,
        out_shape=outs,
        in_specs=specs,
        out_specs=[
            pl.BlockSpec(memory_space=pltpu.HBM if i in hbm_out else pltpu.VMEM)
            for i in range(len(outs))
        ],
        scratch_shapes=list(scratch),
        compiler_params=pltpu.CompilerParams(vmem_limit_bytes=limit * 1024 * 1024),
    )(*ins)


def iota(shape, dim):
    return lax.broadcasted_iota(jnp.int32, shape, dim)


def parts(x):
    high = x.astype(BF16)
    rest = x - high.astype(F32)
    mid = rest.astype(BF16)
    return high, mid, (rest - mid.astype(F32)).astype(BF16)


def dot(a, b):
    if b.dtype == BF16:
        p = [jnp.dot(x, b, preferred_element_type=F32) for x in parts(a)]
    else:
        p = [jnp.dot(a, x, preferred_element_type=F32) for x in parts(b)]
    return (p[2] + p[1]) + p[0]


def radial_consts(shape, size, step, rad):
    i = rad.astype(F32)
    metric = ((i + 0.5) * step) ** 2
    ca = 0.5 / metric
    ri = jnp.where(rad > 0, 0.5 * i / (i + 0.5), 0.0)
    ro = jnp.where(rad < size - 1, 0.5 * (i + 1.0) / (i + 0.5), 0.0)
    return ca, ri, ro


def hot(mask):
    return mask.astype(F32).astype(BF16)


def pair_cols(n):
    return hot(iota((n, n // 2), 0) // 2 == iota((n, n // 2), 1))


def dup_cols(n):
    return hot(iota((n, 2 * n), 0) == iota((n, 2 * n), 1) // 2)


def row_sums(planes, out, first, per):
    o, r = iota((planes * out, planes * per), 0), iota((planes * out, planes * per), 1)
    h = r % per - first
    return hot((o // out == r // per) & (h >= 0) & (h // 2 == o % out))


def widened(planes):
    o, r = iota((planes * 8, planes * 8), 0), iota((planes * 8, planes * 8), 1)
    return hot((o // 8 == r // 8) & (o % 8 == (r % 8) // 2 + 2))


def position():
    return lax.axis_index("az"), lax.axis_index("gz")


def pick(par, even, odd):
    return jnp.where(par == 0, even, odd)


class Halo:
    def __init__(self, x_ref, c_ref, z_ref, y_ref):
        a, g = position()
        self.pa, self.pg = a % 2, g % 2
        self.x, self.c, self.z, self.y = x_ref, c_ref, z_ref, y_ref

    def prev(self, rows, lanes):
        return pick(self.pa, self.x[rows, lanes], self.c[rows, lanes])

    def next(self, rows, lanes):
        return pick(self.pa, self.c[rows, lanes], self.x[rows, lanes])

    def below(self, rows, lanes):
        return pick(self.pg, self.y[rows, lanes], self.z[rows, lanes])

    def above(self, rows, lanes):
        return pick(self.pg, self.z[rows, lanes], self.y[rows, lanes])


def fine_walk(m_of, v_of, mb, ma, vb, va, emit):
    a, g = position()
    sub = iota((NH, NR), 0)
    lane = iota((NH, NR), 1)
    ca, ri, ro = radial_consts((NH, NR), NR, 2.0 * math.pi / (NA * N_AZ), lane)
    zlo = jnp.where((sub == 0) & (g == 0), 0.0, 0.5)
    zhi = jnp.where((sub == NH - 1) & (g == N_GZ - 1), 0.0, 0.5)
    first, final = sub == 0, sub == NH - 1
    mp, mc = m_of(-1), m_of(0)
    vp, vc = v_of(-1), v_of(0)
    wa = ca * (mp + mc)
    for i in range(NA):
        mn, vn = m_of(i + 1), v_of(i + 1)
        wan = ca * (mc + mn)
        m_lo = jnp.where(first, mb(i), pltpu.roll(mc, 1, 0))
        m_hi = jnp.where(final, ma(i), pltpu.roll(mc, NH - 1, 0))
        v_lo = jnp.where(first, vb(i), pltpu.roll(vc, 1, 0))
        v_hi = jnp.where(final, va(i), pltpu.roll(vc, NH - 1, 0))
        wl, wh = zlo * (mc + m_lo), zhi * (mc + m_hi)
        wi = ri * (mc + pltpu.roll(mc, 1, 1))
        wo = ro * (mc + pltpu.roll(mc, NR - 1, 1))
        diagonal = (wa + wan) + (wl + wh) + (wi + wo) + SIGMA
        around = (wa * vp + wan * vn) + (wl * v_lo + wh * v_hi)
        around = around + (wi * pltpu.roll(vc, 1, 1) + wo * pltpu.roll(vc, NR - 1, 1))
        emit(i, diagonal, around, vc)
        mp, mc, vp, vc, wa = mc, mn, vc, vn, wan


T1 = 8


def level1_walk(m_of, v_of, first, count, emit):
    a, g = position()
    sub = iota((T1, R1), 0)
    lane = iota((T1, R1), 1)
    height = g * H1 + sub - 2
    ca, ri, ro = radial_consts((T1, R1), R1, 2.0 * math.pi / (A1 * N_AZ), lane)
    zlo = jnp.where(height <= 0, 0.0, 0.5)
    zhi = jnp.where(height >= H1 * N_GZ - 1, 0.0, 0.5)
    mp, mc = m_of(first - 1), m_of(first)
    if v_of is not None:
        vp, vc = v_of(first - 1), v_of(first)
    wa = ca * (mp + mc)
    for i in range(first, first + count):
        mn = m_of(i + 1)
        wan = ca * (mc + mn)
        w = (
            wa,
            wan,
            zlo * (mc + pltpu.roll(mc, 1, 0)),
            zhi * (mc + pltpu.roll(mc, T1 - 1, 0)),
            ri * (mc + pltpu.roll(mc, 1, 1)),
            ro * (mc + pltpu.roll(mc, R1 - 1, 1)),
        )
        diagonal = total_weight(w) + SIGMA * 4.0
        if v_of is None:
            emit(i, diagonal, None, None)
        else:
            vn = v_of(i + 1)
            n = (
                vp,
                vn,
                pltpu.roll(vc, 1, 0),
                pltpu.roll(vc, T1 - 1, 0),
                pltpu.roll(vc, 1, 1),
                pltpu.roll(vc, R1 - 1, 1),
            )
            emit(i, diagonal, weighted(w, n), vc)
            vp, vc = vc, vn
        mp, mc, wa = mc, mn, wan


def weighted(w, n):
    return (w[0] * n[0] + w[1] * n[1]) + (w[2] * n[2] + w[3] * n[3]) + (w[4] * n[4] + w[5] * n[5])


ALL = slice(None)


def store_faces(ref, x_ref, c_ref, z_ref, y_ref, planes_at=0, rows_at=0):
    a, g = position()
    pa, pg = a % 2, g % 2
    c_plane = jnp.where(pa == 0, NA - 1, 0)
    x_plane = NA - 1 - c_plane
    c_ref[planes_at : planes_at + NH, :] = ref[c_plane]
    x_ref[planes_at : planes_at + NH, :] = ref[x_plane]
    z_row = jnp.where(pg == 0, NH - 1, 0)
    y_row = NH - 1 - z_row
    for i in range(NA):
        z_ref[rows_at + i : rows_at + i + 1, :] = ref[i, pl.ds(z_row, 1), :]
        y_ref[rows_at + i : rows_at + i + 1, :] = ref[i, pl.ds(y_row, 1), :]


def mobilities(
    void_hbm, vol_hbm, cnt_ref,
    m0_ref, m1_ref, m2_ref, live_ref,
    pairs, halves, void_ref, vol_ref, sems,
):
    part = NA // 4
    reads = [
        pltpu.make_async_copy(
            void_hbm.at[pl.ds(k * part, part)], void_ref.at[pl.ds(k * part, part)], sems.at[k]
        )
        for k in range(4)
    ]
    reads.append(pltpu.make_async_copy(vol_hbm, vol_ref, sems.at[4]))
    for read in reads:
        read.start()
    for i in range(0, NA, 2):
        if i % part == 0:
            reads[i // part].wait()
        u = 1.0 / (1.0 - void_ref[i])
        v = 1.0 / (1.0 - void_ref[i + 1])
        m0_ref[i] = u
        m0_ref[i + 1] = v
        pairs[(i // 2) * NH : (i // 2 + 1) * NH, :] = u + v
    m1_ref[...] = 0.125 * dot(widened(A1), dot(pairs[...], pair_cols(NR))).reshape(A1, T1, R1)
    for i in range(A2):
        halves[i * T1 : (i + 1) * T1, :] = m1_ref[2 * i] + m1_ref[2 * i + 1]
    m2_ref[...] = 0.125 * dot(row_sums(A2, H2, 2, T1), dot(halves[...], pair_cols(R1)))
    for read in reads[4:]:
        read.wait()
    live_ref[...] = jnp.where(iota((1, SLOTS), 1) < cnt_ref[0], vol_ref[...], 0.0)


def first_faces(p_ref, m0_ref, m1_ref, live_ref, sx, sc, sz, sy):
    a, g = position()
    pa, pg = a % 2, g % 2
    store_faces(p_ref, sx, sc, sz, sy, 0, 0)
    store_faces(m0_ref, sx, sc, sz, sy, NH, NA)
    rest = slice(2 * NH, 3 * NH)
    sx[rest, R1:NR] = jnp.zeros((NH, NR - R1), F32)
    sc[rest, R1:NR] = jnp.zeros((NH, NR - R1), F32)
    c_plane = jnp.where(pa == 0, A1 - 1, 0)
    sc[rest, 0:R1] = m1_ref[c_plane]
    sx[rest, 0:R1] = m1_ref[A1 - 1 - c_plane]
    for ref in (sz, sy):
        ref[2 * NA : 2 * NA + A1, R1:NR] = jnp.zeros((A1, NR - R1), F32)
    z_row = jnp.where(pg == 0, H1 + 1, 2)
    for i in range(A1):
        at = slice(2 * NA + i, 2 * NA + i + 1)
        sz[at, 0:R1] = m1_ref[i, pl.ds(z_row, 1), :]
        sy[at, 0:R1] = m1_ref[i, pl.ds(H1 + 3 - z_row, 1), :]
    for ref in (sx, sc):
        ref[2 * NH : 2 * NH + 1, R1 : R1 + SLOTS] = live_ref[...]


def fine_mobility(m_ref, ah):
    def m_of(i):
        if i < 0:
            return ah.prev(slice(NH, 2 * NH), ALL)
        if i >= NA:
            return ah.next(slice(NH, 2 * NH), ALL)
        return m_ref[i]

    return (
        m_of,
        lambda i: ah.below(slice(NA + i, NA + i + 1), ALL),
        lambda i: ah.above(slice(NA + i, NA + i + 1), ALL),
    )


def fine_values(v_ref, vh):
    def v_of(i):
        if i < 0:
            return vh.prev(slice(0, NH), ALL)
        if i >= NA:
            return vh.next(slice(0, NH), ALL)
        return v_ref[i]

    return (
        v_of,
        lambda i: vh.below(slice(i, i + 1), ALL),
        lambda i: vh.above(slice(i, i + 1), ALL),
    )


def presmooth(p_ref, div_ref, m_ref, cell_ref, ax, ac, az, ay, rhs_ref, v_ref, sx, sc, sz, sy):
    ah = Halo(ax, ac, az, ay)
    arrived = ah.prev(slice(2 * NH, 2 * NH + 1), slice(R1, R1 + SLOTS))
    cell = cell_ref[...]
    plane_hot = hot(iota((NA * NH, SLOTS), 0) == lax.shift_right_logical(cell, 9))
    radius_hot = jnp.where(iota((NR, SLOTS), 0) == (cell & (NR - 1)), arrived, 0.0)
    deposit = [
        lax.dot_general(plane_hot, x, (((1,), (1,)), ((), ())), preferred_element_type=F32)
        for x in parts(radius_hot)
    ]
    deposit = (deposit[2] + deposit[1]) + deposit[0]
    rhs_ref[...] = div_ref[...] + deposit.reshape(NA, NH, NR)
    m_of, mb, ma = fine_mobility(m_ref, ah)
    v_of, vb, va = fine_values(p_ref, ah)

    def emit(i, diagonal, around, centre):
        v_ref[i] = (1.0 - OMEGA) * centre + OMEGA * (rhs_ref[i] + around) / diagonal

    fine_walk(m_of, v_of, mb, ma, vb, va, emit)
    store_faces(v_ref, sx, sc, sz, sy)


def restrict(
    rhs_ref, v_ref, m_ref, m1_ref, ax, ac, az, ay, bx, bc, bz, by, b1_ref, v1_ref, sz, sy, pairs
):
    ah, bh = Halo(ax, ac, az, ay), Halo(bx, bc, bz, by)
    m_of, mb, ma = fine_mobility(m_ref, ah)
    v_of, vb, va = fine_values(v_ref, bh)
    kept = []

    def emit(i, diagonal, around, centre):
        r = rhs_ref[i] - diagonal * centre + around
        if i % 2 == 0:
            kept.append(r)
        else:
            pairs[(i // 2) * NH : (i // 2 + 1) * NH, :] = kept.pop() + r

    fine_walk(m_of, v_of, mb, ma, vb, va, emit)
    b1_ref[...] = 0.5 * dot(widened(A1), dot(pairs[...], pair_cols(NR))).reshape(A1, T1, R1)

    sub = iota((T1, R1), 0)

    def m1_of(i):
        if i < 0:
            return ah.prev(slice(2 * NH, 3 * NH), slice(0, R1))
        if i >= A1:
            return ah.next(slice(2 * NH, 3 * NH), slice(0, R1))
        at = slice(2 * NA + i, 2 * NA + i + 1)
        below, above = ah.below(at, slice(0, R1)), ah.above(at, slice(0, R1))
        return jnp.where(sub == 1, below, jnp.where(sub == H1 + 2, above, m1_ref[i]))

    def emit1(i, diagonal, around, centre):
        v1_ref[i] = OMEGA * b1_ref[i] / diagonal

    level1_walk(m1_of, None, 0, A1, emit1)
    g = lax.axis_index("gz")
    for layer in range(2):
        z_row = jnp.where(g % 2 == 0, H1 + 1 - layer, 2 + layer)
        y_row = H1 + 3 - z_row
        sources = (v1_ref, m1_ref) if layer else (v1_ref, m1_ref, b1_ref)
        for n, ref in enumerate(sources):
            for i in range(A1):
                at = (2 * n + layer) * A1 + i
                sz[at : at + 1, :] = ref[i, pl.ds(z_row, 1), :]
                sy[at : at + 1, :] = ref[i, pl.ds(y_row, 1), :]


def widen(b1_ref, v1_ref, m1_ref, z_ref, y_ref, vw, mw, bw, sx, sc):
    a, g = position()
    sub = iota((T1, R1), 0)
    halo = Halo(None, None, z_ref, y_ref)
    for n, (src, dst) in enumerate(((v1_ref, vw), (m1_ref, mw), (b1_ref, bw))):
        for i in range(A1):
            tile = src[i]
            for layer in range(2 if n < 2 else 1):
                at = (2 * n + layer) * A1 + i
                at = slice(at, at + 1)
                tile = jnp.where(sub == 1 - layer, halo.below(at, ALL), tile)
                tile = jnp.where(sub == H1 + 2 + layer, halo.above(at, ALL), tile)
            dst[i] = tile
    for layer in range(2):
        c_plane = jnp.where(a % 2 == 0, A1 - 1 - layer, layer)
        x_plane = A1 - 1 - c_plane
        for n, ref in enumerate((vw, mw) if layer else (vw, mw, bw)):
            at = (2 * n + layer) * T1
            sc[at : at + T1, :] = ref[c_plane]
            sx[at : at + T1, :] = ref[x_plane]


def wide_planes(ref, halo, n, i):
    if i < 0:
        at = (2 * n - 1 - i) * T1
        return halo.prev(slice(at, at + T1), ALL)
    if i >= A1:
        at = (2 * n + i - A1) * T1
        return halo.next(slice(at, at + T1), ALL)
    return ref[i]


def restrict1(bw, vw, mw, m2_ref, cx, cc, out_ref, halves):
    halo = Halo(cx, cc, None, None)
    kept = []

    def emit(i, diagonal, around, centre):
        r = (1.0 - OMEGA) * bw[i] + around
        if i % 2 == 0:
            kept.append(r)
        else:
            halves[(i // 2) * T1 : (i // 2 + 1) * T1, :] = kept.pop() + r

    level1_walk(
        lambda i: wide_planes(mw, halo, 1, i), lambda i: wide_planes(vw, halo, 0, i), 0, A1, emit
    )
    b2 = 0.5 * dot(row_sums(A2, H2, 2, T1), dot(halves[...], pair_cols(R1)))
    m2 = m2_ref[...]
    rows = A2 * H2
    for k in range(out_ref.shape[0]):
        out_ref[k, 0:rows, :] = b2
        out_ref[k, rows : 2 * rows, :] = m2


def level2_plane(consts, face, mc, mn):
    ca, ri, ro, zlo, zhi = consts
    mid = 0.5 * (mc[0] + mc[1])
    lows = (zlo * (mc[0] + pltpu.roll(mc[1], 1, 0)), mid)
    highs = (mid, zhi * (mc[1] + pltpu.roll(mc[0], G2 - 1, 0)))
    nxt = level2_face(consts, mc, mn)
    out = []
    for p in range(2):
        m = mc[p]
        wi, wo = ri * (m + pltpu.roll(m, 1, 1)), ro * (m + pltpu.roll(m, R2 - 1, 1))
        out.append((face[p], nxt[p], lows[p], highs[p], wi, wo))
    return out, nxt


def level2_face(consts, mp, mc):
    return (consts[0] * (mp[0] + mc[0]), consts[0] * (mp[1] + mc[1]))


def level2_around(vp, vc, vn):
    lows = (pltpu.roll(vc[1], 1, 0), vc[0])
    highs = (vc[1], pltpu.roll(vc[0], G2 - 1, 0))
    return [
        (vp[p], vn[p], lows[p], highs[p], pltpu.roll(vc[p], 1, 1), pltpu.roll(vc[p], R2 - 1, 1))
        for p in range(2)
    ]


def total_weight(w):
    return (w[0] + w[1]) + (w[2] + w[3]) + (w[4] + w[5])


def height_walls():
    sub = iota((G2, R2), 0)
    return jnp.where(sub == 0, 0.0, 0.5), jnp.where(sub == G2 - 1, 0.0, 0.5)


def level2_consts():
    lane = iota((G2, R2), 1)
    return radial_consts((G2, R2), R2, 2.0 * math.pi / AZ2, lane) + height_walls()


def both(ref, s):
    return (ref[s, 0], ref[s, 1])


def close_ring(ref):
    ref[0:2] = ref[AZ2 : AZ2 + 2]
    ref[AZ2 + 2 : AZ2 + 4] = ref[2:4]


HALF = AZ3 // 2


def packed(ref):
    row_i, col_i = iota((R2, R2), 0), iota((R2, R2), 1)
    left = hot(row_i // 2 == col_i)
    right = hot(row_i // 2 + R2 // 2 == col_i)
    lower = ref[0:HALF].reshape(HALF * G2, R2)
    upper = ref[HALF:AZ3].reshape(HALF * G2, R2)
    return (dot(lower, left) + dot(upper, right)).reshape(HALF, G2, R2)


def wrap(ref):
    ref[0] = pltpu.roll(ref[HALF], R2 // 2, 1)
    ref[HALF + 1] = pltpu.roll(ref[1], R2 // 2, 1)


def coarse_weights(own, oth, m2, d2, w3, sum_m, m3):
    a, g = position()
    pa = a % 2
    rows = A2 * H2
    def lay(own, oth):
        for k in range(N_AZ):
            base = (k // 2) * N_GZ * 2 * rows + rows
            ref = oth if k % 2 else own
            for i in range(A2):
                for p in range(2):
                    at = pl.ds(base + i * 2 + p, G2, stride=2 * rows)
                    m2[k * A2 + i + 2, p] = ref[at, :]

    pl.when(pa == 0)(lambda: lay(own, oth))
    pl.when(pa == 1)(lambda: lay(oth, own))
    close_ring(m2)
    consts = level2_consts()

    mp, mc = both(m2, 1), both(m2, 2)
    face = level2_face(consts, mp, mc)
    for d in range(AZ2):
        mn = both(m2, d + 3)
        w, face = level2_plane(consts, face, mc, mn)
        for p in range(2):
            d2[d + 2, p] = OMEGA / (total_weight(w[p]) + SIGMA * 16.0)
        if d % 2:
            sum_m[d // 2] = (mp[0] + mp[1]) + (mc[0] + mc[1])
        mp, mc = mc, mn
    close_ring(d2)
    m3[1 : HALF + 1] = 0.125 * packed(sum_m)
    wrap(m3)
    lane = iota((G2, R2), 1) % (R2 // 2)
    ca, ri, ro = radial_consts((G2, R2), R2 // 2, 2.0 * math.pi / AZ3, lane)
    zlo, zhi = height_walls()
    mp, mc = m3[0], m3[1]
    for i in range(HALF):
        mn = m3[i + 2]
        w = (
            ca * (mc + mp),
            ca * (mc + mn),
            zlo * (mc + pltpu.roll(mc, 1, 0)),
            zhi * (mc + pltpu.roll(mc, G2 - 1, 0)),
            ri * (mc + pltpu.roll(mc, 1, 1)),
            ro * (mc + pltpu.roll(mc, R2 - 1, 1)),
        )
        scale = OMEGA / (total_weight(w) + SIGMA * 64.0)
        for f in range(6):
            w3[f, i] = w[f] * scale
        w3[6, i] = scale
        mp, mc = mc, mn


def coarse(
    own, oth, bw, vw, mw, cx, cc, rhs_ref, v_ref, m_ref, ax, ac, az, ay, bx, bc, bz, by,
    out_ref, sx, sc, sz, sy,
    m2, d2, w3, sum_m, m3, b2, v2, sum_r, add, va, vb, e2, v2f, src, v1f, e_ref,
):
    coarse_weights(own, oth, m2, d2, w3, sum_m, m3)
    a, g = position()
    pa = a % 2
    rows = A2 * H2

    def lay(own, oth):
        for k in range(N_AZ):
            base = (k // 2) * N_GZ * 2 * rows
            ref = oth if k % 2 else own
            for i in range(A2):
                s = k * A2 + i + 2
                for p in range(2):
                    b = ref[pl.ds(base + i * 2 + p, G2, stride=2 * rows), :]
                    b2[s, p] = b
                    v2[s, p] = b * d2[s, p]

    pl.when(pa == 0)(lambda: lay(own, oth))
    pl.when(pa == 1)(lambda: lay(oth, own))
    close_ring(b2)
    close_ring(v2)
    consts = level2_consts()

    mc = both(m2, 2)
    vp, vc = both(v2, 1), both(v2, 2)
    face = level2_face(consts, both(m2, 1), mc)
    total = None
    for d in range(AZ2):
        mn, vn = both(m2, d + 3), both(v2, d + 3)
        w, face = level2_plane(consts, face, mc, mn)
        n = level2_around(vp, vc, vn)
        b = both(b2, d + 2)
        r = ((1.0 - OMEGA) * (b[0] + b[1]) + weighted(w[0], n[0])) + weighted(w[1], n[1])
        if d % 2:
            sum_r[d // 2] = total + r
        total, mc, vp, vc = r, mn, vc, vn

    b3 = 0.5 * packed(sum_r)
    for i in range(HALF):
        start = b3[i] * w3[6, i]
        add[i] = start
        va[i + 1] = start
    wrap(va)

    def sweep(src_ref, dst_ref):
        vp, vc = src_ref[0], src_ref[1]
        for i in range(HALF):
            vn = src_ref[i + 2]
            n = (
                vp,
                vn,
                pltpu.roll(vc, 1, 0),
                pltpu.roll(vc, G2 - 1, 0),
                pltpu.roll(vc, 1, 1),
                pltpu.roll(vc, R2 - 1, 1),
            )
            w = [w3[f, i] for f in range(6)]
            dst_ref[i + 1] = ((1.0 - OMEGA) * vc + add[i]) + weighted(w, n)
            vp, vc = vc, vn
        wrap(dst_ref)

    def two(k, carry):
        sweep(va, vb)
        sweep(vb, va)
        return carry

    lax.fori_loop(0, (COARSE_SWEEPS - 2) // 2, two, 0)
    sweep(va, vb)

    row_i, col_i = iota((R2, R2), 0), iota((R2, R2), 1)
    solved = vb[1 : HALF + 1].reshape(HALF * G2, R2)
    e2[0:HALF] = dot(solved, hot(row_i == col_i // 2)).reshape(HALF, G2, R2)
    e2[HALF:AZ3] = dot(solved, hot(row_i == col_i // 2 + R2 // 2)).reshape(HALF, G2, R2)

    at = a * A2
    values = []
    for k in range(A2 + 4):
        e = e2[(a * (A2 // 2) - 1 + k // 2 + AZ3) % AZ3]
        values.append((v2[at + k, 0] + e, v2[at + k, 1] + e))
    mc = both(m2, at + 1)
    face = level2_face(consts, both(m2, at), mc)
    for k in range(1, A2 + 3):
        mn = both(m2, at + k + 1)
        w, face = level2_plane(consts, face, mc, mn)
        n = level2_around(*values[k - 1 : k + 2])
        for p in range(2):
            gain = b2[at + k, p] + weighted(w[p], n[p])
            v2f[k - 1, p] = (1.0 - OMEGA) * values[k][p] + d2[at + k, p] * gain
        mc = mn

    low, high = jnp.maximum(g - 1, 0), jnp.minimum(g + 1, N_GZ - 1)
    for j in range(A2 + 2):
        for q, (p, row) in enumerate(((1, low), (0, g), (1, g), (0, high))):
            src[4 * j + q : 4 * j + q + 1, :] = v2f[j, p, pl.ds(row, 1), :]
    o, c = iota((8 * (A2 + 2), 4 * (A2 + 2)), 0), iota((8 * (A2 + 2), 4 * (A2 + 2)), 1)
    e1 = dot(hot(o // 2 == c), dot(src[...], dup_cols(R2)))
    halo = Halo(cx, cc, None, None)

    def v1_of(i):
        j = (i + 2) // 2
        return wide_planes(vw, halo, 0, i) + e1[T1 * j : T1 * (j + 1)]

    def emit1(i, diagonal, around, centre):
        b = wide_planes(bw, halo, 2, i)
        at = (i + 1) * T1
        v1f[at : at + T1, :] = (1.0 - OMEGA) * centre + OMEGA * (b + around) / diagonal

    level1_walk(lambda i: wide_planes(mw, halo, 1, i), v1_of, -1, A1 + 2, emit1)

    own_rows = (A1 + 2) * NH
    shape = (own_rows + 2 * A1, (A1 + 2) * T1)
    o, c = iota(shape, 0), iota(shape, 1)
    j = jnp.where(o < own_rows, o // NH, (o - own_rows) % A1 + 1)
    h = jnp.where(o < own_rows, (o % NH) // 2 + 2, jnp.where(o < own_rows + A1, 1, H1 + 2))
    e_ref[...] = dot(dot(hot(c == j * T1 + h), v1f[...]), dup_cols(R1))
    ah, bh = Halo(ax, ac, az, ay), Halo(bx, bc, bz, by)
    m_of, mb, ma = fine_mobility(m_ref, ah)
    old, ob, oa = fine_values(v_ref, bh)

    def v_of(i):
        at = (i // 2 + 1) * NH
        return old(i) + e_ref[at : at + NH, :]

    def around_row(value, start):
        def row(i):
            at = start + i // 2
            return value(i) + e_ref[at : at + 1, :]

        return row

    def emit(i, diagonal, around, centre):
        out_ref[i] = (1.0 - OMEGA) * centre + OMEGA * (rhs_ref[i] + around) / diagonal

    fine_walk(
        m_of, v_of, mb, ma, around_row(ob, own_rows), around_row(oa, own_rows + A1), emit
    )
    store_faces(out_ref, sx, sc, sz, sy)


def final(rhs_ref, v_ref, m_ref, ax, ac, az, ay, gx, gc, gz, gy, p_hbm, out_hbm, out_ref, sems):
    part = NA // 4
    copies = [
        pltpu.make_async_copy(
            src.at[pl.ds(k * part, part)], dst.at[pl.ds(k * part, part)], sems.at[4 * n + k]
        )
        for n, (src, dst) in enumerate(((v_ref, p_hbm), (out_ref, out_hbm)))
        for k in range(4)
    ]
    for copy in copies[:4]:
        copy.start()
    ah, gh = Halo(ax, ac, az, ay), Halo(gx, gc, gz, gy)
    m_of, mb, ma = fine_mobility(m_ref, ah)
    v_of, vb, va = fine_values(v_ref, gh)

    def emit(i, diagonal, around, centre):
        out_ref[i] = (rhs_ref[i] - diagonal * centre + around) / diagonal
        if i % part == part - 1:
            copies[4 + i // part].start()

    fine_walk(m_of, v_of, mb, ma, vb, va, emit)
    for copy in copies:
        copy.wait()


def swap(x, axis, odd):
    n = lax.axis_size(axis)
    pairs = []
    for i in range(n):
        partner = i ^ 1 if odd == 0 else ((i + 1) % n if i % 2 else (i - 1) % n)
        pairs.append((i, partner))
    return lax.ppermute(x, axis, pairs)


def exchange(sx, sc, sz, sy):
    return swap(sx, "az", 1), swap(sc, "az", 0), swap(sz, "gz", 0), swap(sy, "gz", 1)


def gathered(x):
    groups = [[a * N_GZ + g for a in range(c, N_AZ, 2) for g in range(N_GZ)] for c in range(2)]
    own = lax.all_to_all(x, ("az", "gz"), 0, 0, tiled=True, axis_index_groups=groups)
    own = own.reshape(own.shape[0] * own.shape[1], own.shape[2])
    return own, swap(own, "az", 0)


def faces(planes, rows, width):
    return [struct(planes, width)] * 2 + [struct(rows, width)] * 2


def vmem(*shape):
    return pltpu.VMEM(shape, F32)


def body(pressure, divergence, void_fraction, bubble_volume, bubble_count, bubble_cell):
    block = struct(NA, NH, NR)
    wide = struct(A1, T1, R1)
    cell = bubble_cell.reshape(1, SLOTS)
    volume = bubble_volume.reshape(1, SLOTS)
    pairs = vmem(A1 * NH, NR)
    halves = vmem(A2 * T1, R1)

    far = [
        pltpu.with_memory_space_constraint(x, pltpu.HBM)
        for x in (void_fraction, volume)
    ]
    m0, m1, m2, live = call(
        mobilities,
        [block, wide, struct(A2 * H2, R2), struct(1, SLOTS)],
        (*far, bubble_count),
        [
            pairs,
            halves,
            vmem(NA, NH, NR),
            vmem(1, SLOTS),
            pltpu.SemaphoreType.DMA((5,)),
        ],
        hbm=(0, 1),
        smem=(2,),
    )
    send = call(
        first_faces,
        faces(3 * NH, 2 * NA + A1, NR),
        (pressure, m0, m1, live),
    )
    ha = exchange(*send)
    rhs, v0, *send = call(
        presmooth, [block, block] + faces(NH, NA, NR), (pressure, divergence, m0, cell, *ha)
    )
    hb = exchange(*send)
    b1, v1, sz, sy = call(
        restrict,
        [wide, wide] + [struct(5 * A1, R1)] * 2,
        (rhs, v0, m0, m1, *ha, *hb),
        [pairs],
    )
    v1, m1, b1, sx, sc = call(
        widen,
        [wide, wide, wide] + [struct(5 * T1, R1)] * 2,
        (b1, v1, m1, swap(sz, "gz", 0), swap(sy, "gz", 1)),
    )
    hc = swap(sx, "az", 1), swap(sc, "az", 0)
    (copies,) = call(restrict1, [struct(64, 2 * A2 * H2, R2)], (b1, v1, m1, m2, *hc), [halves])
    ring = vmem(AZ2 + 4, 2, G2, R2)
    ends = vmem(HALF + 2, G2, R2)
    third = vmem(AZ3, G2, R2)
    out, *send = call(
        coarse,
        [block] + faces(NH, NA, NR),
        (*gathered(copies), b1, v1, m1, *hc, rhs, v0, m0, *ha, *hb),
        [
            ring,
            ring,
            vmem(7, HALF, G2, R2),
            third,
            ends,
            ring,
            ring,
            third,
            vmem(HALF, G2, R2),
            ends,
            ends,
            third,
            vmem(A2 + 2, 2, G2, R2),
            vmem(4 * (A2 + 2), R2),
            vmem((A1 + 2) * T1, R1),
            vmem((A1 + 2) * NH + 2 * A1, NR),
        ],
    )
    hg = exchange(*send)
    return tuple(
        call(
            final,
            [block, block],
            (rhs, out, m0, *ha, *hg),
            [vmem(NA, NH, NR), pltpu.SemaphoreType.DMA((8,))],
            hbm_out=(0, 1),
        )
    )


def solution(mesh):
    return jax.shard_map(
        body,
        mesh=mesh,
        in_specs=(
            P("az", "gz", None),
            P("az", "gz", None),
            P("az", "gz", None),
            P(("az", "gz")),
            P(("az", "gz")),
            P(("az", "gz")),
        ),
        out_specs=(P("az", "gz", None), P("az", "gz", None)),
        check_vma=False,
    )
```

```python
import functools
import math

import jax
import jax.numpy as jnp
from jax import lax
from jax.experimental import pallas as pl
from jax.experimental.pallas import tpu as pltpu
from jax.sharding import PartitionSpec as P

SIGMA = 0.02
OMEGA = 0.8
COARSE_SWEEPS = 32
F32 = jnp.float32
BF16 = jnp.bfloat16

NA, NH, NR = 32, 8, 512
A1, H1, R1 = 16, 4, 256
A2, H2, R2 = 8, 2, 128
AZ2, G2 = 128, 8
AZ3 = 64
N_AZ, N_GZ = 16, 8
SLOTS = 128


def struct(*shape):
    return jax.ShapeDtypeStruct(shape, F32)


def call(kernel, outs, ins, scratch=(), smem=(), hbm=(), hbm_out=(), limit=48):
    def space(i, far):
        return pltpu.HBM if i in far else pltpu.SMEM if i in smem else pltpu.VMEM

    specs = [pl.BlockSpec(memory_space=space(i, hbm)) for i in range(len(ins))]
    return pl.pallas_call(
        kernel,
        out_shape=outs,
        in_specs=specs,
        out_specs=[
            pl.BlockSpec(memory_space=pltpu.HBM if i in hbm_out else pltpu.VMEM)
            for i in range(len(outs))
        ],
        scratch_shapes=list(scratch),
        compiler_params=pltpu.CompilerParams(vmem_limit_bytes=limit * 1024 * 1024),
    )(*ins)


def iota(shape, dim):
    return lax.broadcasted_iota(jnp.int32, shape, dim)


def parts(x):
    high = x.astype(BF16)
    rest = x - high.astype(F32)
    mid = rest.astype(BF16)
    return high, mid, (rest - mid.astype(F32)).astype(BF16)


def dot(a, b):
    if b.dtype == BF16:
        p = [jnp.dot(x, b, preferred_element_type=F32) for x in parts(a)]
    else:
        p = [jnp.dot(a, x, preferred_element_type=F32) for x in parts(b)]
    return (p[2] + p[1]) + p[0]


def radial_consts(shape, size, step, rad):
    i = rad.astype(F32)
    metric = ((i + 0.5) * step) ** 2
    ca = 0.5 / metric
    ri = jnp.where(rad > 0, 0.5 * i / (i + 0.5), 0.0)
    ro = jnp.where(rad < size - 1, 0.5 * (i + 1.0) / (i + 0.5), 0.0)
    return ca, ri, ro


def hot(mask):
    return mask.astype(F32).astype(BF16)


def pair_cols(n):
    return hot(iota((n, n // 2), 0) // 2 == iota((n, n // 2), 1))


def dup_cols(n):
    return hot(iota((n, 2 * n), 0) == iota((n, 2 * n), 1) // 2)


def row_sums(planes, out, first, per):
    o, r = iota((planes * out, planes * per), 0), iota((planes * out, planes * per), 1)
    h = r % per - first
    return hot((o // out == r // per) & (h >= 0) & (h // 2 == o % out))


def widened(planes):
    o, r = iota((planes * 8, planes * 8), 0), iota((planes * 8, planes * 8), 1)
    return hot((o // 8 == r // 8) & (o % 8 == (r % 8) // 2 + 2))


def position():
    return lax.axis_index("az"), lax.axis_index("gz")


def pick(par, even, odd):
    return jnp.where(par == 0, even, odd)


class Halo:
    def __init__(self, x_ref, c_ref, z_ref, y_ref):
        a, g = position()
        self.pa, self.pg = a % 2, g % 2
        self.x, self.c, self.z, self.y = x_ref, c_ref, z_ref, y_ref

    def prev(self, rows, lanes):
        return pick(self.pa, self.x[rows, lanes], self.c[rows, lanes])

    def next(self, rows, lanes):
        return pick(self.pa, self.c[rows, lanes], self.x[rows, lanes])

    def below(self, rows, lanes):
        return pick(self.pg, self.y[rows, lanes], self.z[rows, lanes])

    def above(self, rows, lanes):
        return pick(self.pg, self.z[rows, lanes], self.y[rows, lanes])


def fine_walk(m_of, v_of, mb, ma, vb, va, emit):
    a, g = position()
    sub = iota((NH, NR), 0)
    lane = iota((NH, NR), 1)
    ca, ri, ro = radial_consts((NH, NR), NR, 2.0 * math.pi / (NA * N_AZ), lane)
    zlo = jnp.where((sub == 0) & (g == 0), 0.0, 0.5)
    zhi = jnp.where((sub == NH - 1) & (g == N_GZ - 1), 0.0, 0.5)
    first, final = sub == 0, sub == NH - 1
    mp, mc = m_of(-1), m_of(0)
    vp, vc = v_of(-1), v_of(0)
    wa = ca * (mp + mc)
    for i in range(NA):
        mn, vn = m_of(i + 1), v_of(i + 1)
        wan = ca * (mc + mn)
        m_lo = jnp.where(first, mb(i), pltpu.roll(mc, 1, 0))
        m_hi = jnp.where(final, ma(i), pltpu.roll(mc, NH - 1, 0))
        v_lo = jnp.where(first, vb(i), pltpu.roll(vc, 1, 0))
        v_hi = jnp.where(final, va(i), pltpu.roll(vc, NH - 1, 0))
        wl, wh = zlo * (mc + m_lo), zhi * (mc + m_hi)
        wi = ri * (mc + pltpu.roll(mc, 1, 1))
        wo = ro * (mc + pltpu.roll(mc, NR - 1, 1))
        diagonal = (wa + wan) + (wl + wh) + (wi + wo) + SIGMA
        around = (wa * vp + wan * vn) + (wl * v_lo + wh * v_hi)
        around = around + (wi * pltpu.roll(vc, 1, 1) + wo * pltpu.roll(vc, NR - 1, 1))
        emit(i, diagonal, around, vc)
        mp, mc, vp, vc, wa = mc, mn, vc, vn, wan


T1 = 8


def level1_walk(m_of, v_of, first, count, emit):
    a, g = position()
    sub = iota((T1, R1), 0)
    lane = iota((T1, R1), 1)
    height = g * H1 + sub - 2
    ca, ri, ro = radial_consts((T1, R1), R1, 2.0 * math.pi / (A1 * N_AZ), lane)
    zlo = jnp.where(height <= 0, 0.0, 0.5)
    zhi = jnp.where(height >= H1 * N_GZ - 1, 0.0, 0.5)
    mp, mc = m_of(first - 1), m_of(first)
    if v_of is not None:
        vp, vc = v_of(first - 1), v_of(first)
    wa = ca * (mp + mc)
    for i in range(first, first + count):
        mn = m_of(i + 1)
        wan = ca * (mc + mn)
        w = (
            wa,
            wan,
            zlo * (mc + pltpu.roll(mc, 1, 0)),
            zhi * (mc + pltpu.roll(mc, T1 - 1, 0)),
            ri * (mc + pltpu.roll(mc, 1, 1)),
            ro * (mc + pltpu.roll(mc, R1 - 1, 1)),
        )
        diagonal = total_weight(w) + SIGMA * 4.0
        if v_of is None:
            emit(i, diagonal, None, None)
        else:
            vn = v_of(i + 1)
            n = (
                vp,
                vn,
                pltpu.roll(vc, 1, 0),
                pltpu.roll(vc, T1 - 1, 0),
                pltpu.roll(vc, 1, 1),
                pltpu.roll(vc, R1 - 1, 1),
            )
            emit(i, diagonal, weighted(w, n), vc)
            vp, vc = vc, vn
        mp, mc, wa = mc, mn, wan


def weighted(w, n):
    return (w[0] * n[0] + w[1] * n[1]) + (w[2] * n[2] + w[3] * n[3]) + (w[4] * n[4] + w[5] * n[5])


ALL = slice(None)


def store_faces(ref, x_ref, c_ref, z_ref, y_ref, planes_at=0, rows_at=0):
    a, g = position()
    pa, pg = a % 2, g % 2
    c_plane = jnp.where(pa == 0, NA - 1, 0)
    x_plane = NA - 1 - c_plane
    c_ref[planes_at : planes_at + NH, :] = ref[c_plane]
    x_ref[planes_at : planes_at + NH, :] = ref[x_plane]
    z_row = jnp.where(pg == 0, NH - 1, 0)
    y_row = NH - 1 - z_row
    for i in range(NA):
        z_ref[rows_at + i : rows_at + i + 1, :] = ref[i, pl.ds(z_row, 1), :]
        y_ref[rows_at + i : rows_at + i + 1, :] = ref[i, pl.ds(y_row, 1), :]


def mobilities(
    void_hbm, vol_hbm, cnt_ref,
    m0_ref, m1_ref, m2_ref, live_ref,
    pairs, halves, void_ref, vol_ref, sems,
):
    part = NA // 4
    reads = [
        pltpu.make_async_copy(
            void_hbm.at[pl.ds(k * part, part)], void_ref.at[pl.ds(k * part, part)], sems.at[k]
        )
        for k in range(4)
    ]
    reads.append(pltpu.make_async_copy(vol_hbm, vol_ref, sems.at[4]))
    for read in reads:
        read.start()
    for i in range(0, NA, 2):
        if i % part == 0:
            reads[i // part].wait()
        u = 1.0 / (1.0 - void_ref[i])
        v = 1.0 / (1.0 - void_ref[i + 1])
        m0_ref[i] = u
        m0_ref[i + 1] = v
        pairs[(i // 2) * NH : (i // 2 + 1) * NH, :] = u + v
    m1_ref[...] = 0.125 * dot(widened(A1), dot(pairs[...], pair_cols(NR))).reshape(A1, T1, R1)
    for i in range(A2):
        halves[i * T1 : (i + 1) * T1, :] = m1_ref[2 * i] + m1_ref[2 * i + 1]
    m2_ref[...] = 0.125 * dot(row_sums(A2, H2, 2, T1), dot(halves[...], pair_cols(R1)))
    for read in reads[4:]:
        read.wait()
    live_ref[...] = jnp.where(iota((1, SLOTS), 1) < cnt_ref[0], vol_ref[...], 0.0)


def packed_row(i):
    at, lane = 2 * NA + i // 2, (i % 2) * R1
    return slice(at, at + 1), slice(lane, lane + R1)


def first_faces(p_ref, m0_ref, m1_ref, live_ref, sx, sc, sz, sy):
    a, g = position()
    pa, pg = a % 2, g % 2
    store_faces(p_ref, sx, sc, sz, sy, 0, 0)
    store_faces(m0_ref, sx, sc, sz, sy, NH, NA)
    rest = slice(2 * NH, 3 * NH)
    sx[rest, R1:NR] = jnp.zeros((NH, NR - R1), F32)
    sc[rest, R1:NR] = jnp.zeros((NH, NR - R1), F32)
    c_plane = jnp.where(pa == 0, A1 - 1, 0)
    sc[rest, 0:R1] = m1_ref[c_plane]
    sx[rest, 0:R1] = m1_ref[A1 - 1 - c_plane]
    z_row = jnp.where(pg == 0, H1 + 1, 2)
    for i in range(A1):
        at, lanes = packed_row(i)
        sz[at, lanes] = m1_ref[i, pl.ds(z_row, 1), :]
        sy[at, lanes] = m1_ref[i, pl.ds(H1 + 3 - z_row, 1), :]
    for ref in (sx, sc):
        ref[2 * NH : 2 * NH + 1, R1 : R1 + SLOTS] = live_ref[...]


def fine_mobility(m_ref, ah):
    def m_of(i):
        if i < 0:
            return ah.prev(slice(NH, 2 * NH), ALL)
        if i >= NA:
            return ah.next(slice(NH, 2 * NH), ALL)
        return m_ref[i]

    return (
        m_of,
        lambda i: ah.below(slice(NA + i, NA + i + 1), ALL),
        lambda i: ah.above(slice(NA + i, NA + i + 1), ALL),
    )


def fine_values(v_ref, vh):
    def v_of(i):
        if i < 0:
            return vh.prev(slice(0, NH), ALL)
        if i >= NA:
            return vh.next(slice(0, NH), ALL)
        return v_ref[i]

    return (
        v_of,
        lambda i: vh.below(slice(i, i + 1), ALL),
        lambda i: vh.above(slice(i, i + 1), ALL),
    )


def presmooth(p_ref, div_ref, m_ref, cell_ref, ax, ac, az, ay, rhs_ref, v_ref, sx, sc, sz, sy):
    ah = Halo(ax, ac, az, ay)
    arrived = ah.prev(slice(2 * NH, 2 * NH + 1), slice(R1, R1 + SLOTS))
    cell = cell_ref[...]
    plane_hot = hot(iota((NA * NH, SLOTS), 0) == lax.shift_right_logical(cell, 9))
    radius_hot = jnp.where(iota((NR, SLOTS), 0) == (cell & (NR - 1)), arrived, 0.0)
    deposit = [
        lax.dot_general(plane_hot, x, (((1,), (1,)), ((), ())), preferred_element_type=F32)
        for x in parts(radius_hot)
    ]
    deposit = (deposit[2] + deposit[1]) + deposit[0]
    rhs_ref[...] = div_ref[...] + deposit.reshape(NA, NH, NR)
    m_of, mb, ma = fine_mobility(m_ref, ah)
    v_of, vb, va = fine_values(p_ref, ah)

    def emit(i, diagonal, around, centre):
        v_ref[i] = (1.0 - OMEGA) * centre + OMEGA * (rhs_ref[i] + around) / diagonal

    fine_walk(m_of, v_of, mb, ma, vb, va, emit)
    store_faces(v_ref, sx, sc, sz, sy)


def restrict(
    rhs_ref, v_ref, m_ref, m1_ref, ax, ac, az, ay, bx, bc, bz, by, b1_ref, v1_ref, sz, sy, pairs
):
    ah, bh = Halo(ax, ac, az, ay), Halo(bx, bc, bz, by)
    m_of, mb, ma = fine_mobility(m_ref, ah)
    v_of, vb, va = fine_values(v_ref, bh)
    kept = []

    def emit(i, diagonal, around, centre):
        r = rhs_ref[i] - diagonal * centre + around
        if i % 2 == 0:
            kept.append(r)
        else:
            pairs[(i // 2) * NH : (i // 2 + 1) * NH, :] = kept.pop() + r

    fine_walk(m_of, v_of, mb, ma, vb, va, emit)
    b1_ref[...] = 0.5 * dot(widened(A1), dot(pairs[...], pair_cols(NR))).reshape(A1, T1, R1)

    sub = iota((T1, R1), 0)

    def m1_of(i):
        if i < 0:
            return ah.prev(slice(2 * NH, 3 * NH), slice(0, R1))
        if i >= A1:
            return ah.next(slice(2 * NH, 3 * NH), slice(0, R1))
        below, above = ah.below(*packed_row(i)), ah.above(*packed_row(i))
        return jnp.where(sub == 1, below, jnp.where(sub == H1 + 2, above, m1_ref[i]))

    def emit1(i, diagonal, around, centre):
        v1_ref[i] = OMEGA * b1_ref[i] / diagonal

    level1_walk(m1_of, None, 0, A1, emit1)
    g = lax.axis_index("gz")
    for layer in range(2):
        z_row = jnp.where(g % 2 == 0, H1 + 1 - layer, 2 + layer)
        y_row = H1 + 3 - z_row
        sources = (v1_ref, m1_ref) if layer else (v1_ref, m1_ref, b1_ref)
        for n, ref in enumerate(sources):
            for i in range(A1):
                at = (2 * n + layer) * A1 + i
                sz[at : at + 1, :] = ref[i, pl.ds(z_row, 1), :]
                sy[at : at + 1, :] = ref[i, pl.ds(y_row, 1), :]


def widen(b1_ref, v1_ref, m1_ref, z_ref, y_ref, vw, mw, bw, sx, sc):
    a, g = position()
    sub = iota((T1, R1), 0)
    halo = Halo(None, None, z_ref, y_ref)
    for n, (src, dst) in enumerate(((v1_ref, vw), (m1_ref, mw), (b1_ref, bw))):
        for i in range(A1):
            tile = src[i]
            for layer in range(2 if n < 2 else 1):
                at = (2 * n + layer) * A1 + i
                at = slice(at, at + 1)
                tile = jnp.where(sub == 1 - layer, halo.below(at, ALL), tile)
                tile = jnp.where(sub == H1 + 2 + layer, halo.above(at, ALL), tile)
            dst[i] = tile
    for layer in range(2):
        c_plane = jnp.where(a % 2 == 0, A1 - 1 - layer, layer)
        x_plane = A1 - 1 - c_plane
        for n, ref in enumerate((vw, mw) if layer else (vw, mw, bw)):
            at = (2 * n + layer) * T1
            sc[at : at + T1, :] = ref[c_plane]
            sx[at : at + T1, :] = ref[x_plane]


def wide_planes(ref, halo, n, i):
    if i < 0:
        at = (2 * n - 1 - i) * T1
        return halo.prev(slice(at, at + T1), ALL)
    if i >= A1:
        at = (2 * n + i - A1) * T1
        return halo.next(slice(at, at + T1), ALL)
    return ref[i]


def restrict1(bw, vw, mw, m2_ref, cx, cc, out_ref, halves):
    halo = Halo(cx, cc, None, None)
    kept = []

    def emit(i, diagonal, around, centre):
        r = (1.0 - OMEGA) * bw[i] + around
        if i % 2 == 0:
            kept.append(r)
        else:
            halves[(i // 2) * T1 : (i // 2 + 1) * T1, :] = kept.pop() + r

    level1_walk(
        lambda i: wide_planes(mw, halo, 1, i), lambda i: wide_planes(vw, halo, 0, i), 0, A1, emit
    )
    b2 = 0.5 * dot(row_sums(A2, H2, 2, T1), dot(halves[...], pair_cols(R1)))
    m2 = m2_ref[...]
    rows = A2 * H2
    for k in range(out_ref.shape[0]):
        out_ref[k, 0:rows, :] = b2
        out_ref[k, rows : 2 * rows, :] = m2


def level2_plane(consts, face, mc, mn):
    ca, ri, ro, zlo, zhi = consts
    mid = 0.5 * (mc[0] + mc[1])
    lows = (zlo * (mc[0] + pltpu.roll(mc[1], 1, 0)), mid)
    highs = (mid, zhi * (mc[1] + pltpu.roll(mc[0], G2 - 1, 0)))
    nxt = level2_face(consts, mc, mn)
    out = []
    for p in range(2):
        m = mc[p]
        wi, wo = ri * (m + pltpu.roll(m, 1, 1)), ro * (m + pltpu.roll(m, R2 - 1, 1))
        out.append((face[p], nxt[p], lows[p], highs[p], wi, wo))
    return out, nxt


def level2_face(consts, mp, mc):
    return (consts[0] * (mp[0] + mc[0]), consts[0] * (mp[1] + mc[1]))


def level2_around(vp, vc, vn):
    lows = (pltpu.roll(vc[1], 1, 0), vc[0])
    highs = (vc[1], pltpu.roll(vc[0], G2 - 1, 0))
    return [
        (vp[p], vn[p], lows[p], highs[p], pltpu.roll(vc[p], 1, 1), pltpu.roll(vc[p], R2 - 1, 1))
        for p in range(2)
    ]


def total_weight(w):
    return (w[0] + w[1]) + (w[2] + w[3]) + (w[4] + w[5])


def height_walls():
    sub = iota((G2, R2), 0)
    return jnp.where(sub == 0, 0.0, 0.5), jnp.where(sub == G2 - 1, 0.0, 0.5)


def level2_consts():
    lane = iota((G2, R2), 1)
    return radial_consts((G2, R2), R2, 2.0 * math.pi / AZ2, lane) + height_walls()


def both(ref, s):
    return (ref[s, 0], ref[s, 1])


def close_ring(ref):
    ref[0:2] = ref[AZ2 : AZ2 + 2]
    ref[AZ2 + 2 : AZ2 + 4] = ref[2:4]


HALF = AZ3 // 2


def packed(ref):
    row_i, col_i = iota((R2, R2), 0), iota((R2, R2), 1)
    left = hot(row_i // 2 == col_i)
    right = hot(row_i // 2 + R2 // 2 == col_i)
    lower = ref[0:HALF].reshape(HALF * G2, R2)
    upper = ref[HALF:AZ3].reshape(HALF * G2, R2)
    return (dot(lower, left) + dot(upper, right)).reshape(HALF, G2, R2)


def wrap(ref):
    ref[0] = pltpu.roll(ref[HALF], R2 // 2, 1)
    ref[HALF + 1] = pltpu.roll(ref[1], R2 // 2, 1)


def coarse_weights(own, oth, m2, d2, w3, sum_m, m3):
    a, g = position()
    pa = a % 2
    rows = A2 * H2
    def lay(own, oth):
        for k in range(N_AZ):
            base = (k // 2) * N_GZ * 2 * rows + rows
            ref = oth if k % 2 else own
            for i in range(A2):
                for p in range(2):
                    at = pl.ds(base + i * 2 + p, G2, stride=2 * rows)
                    m2[k * A2 + i + 2, p] = ref[at, :]

    pl.when(pa == 0)(lambda: lay(own, oth))
    pl.when(pa == 1)(lambda: lay(oth, own))
    close_ring(m2)
    consts = level2_consts()

    mp, mc = both(m2, 1), both(m2, 2)
    face = level2_face(consts, mp, mc)
    for d in range(AZ2):
        mn = both(m2, d + 3)
        w, face = level2_plane(consts, face, mc, mn)
        for p in range(2):
            d2[d + 2, p] = OMEGA / (total_weight(w[p]) + SIGMA * 16.0)
        if d % 2:
            sum_m[d // 2] = (mp[0] + mp[1]) + (mc[0] + mc[1])
        mp, mc = mc, mn
    close_ring(d2)
    m3[1 : HALF + 1] = 0.125 * packed(sum_m)
    wrap(m3)
    lane = iota((G2, R2), 1) % (R2 // 2)
    ca, ri, ro = radial_consts((G2, R2), R2 // 2, 2.0 * math.pi / AZ3, lane)
    zlo, zhi = height_walls()
    mp, mc = m3[0], m3[1]
    for i in range(HALF):
        mn = m3[i + 2]
        w = (
            ca * (mc + mp),
            ca * (mc + mn),
            zlo * (mc + pltpu.roll(mc, 1, 0)),
            zhi * (mc + pltpu.roll(mc, G2 - 1, 0)),
            ri * (mc + pltpu.roll(mc, 1, 1)),
            ro * (mc + pltpu.roll(mc, R2 - 1, 1)),
        )
        scale = OMEGA / (total_weight(w) + SIGMA * 64.0)
        for f in range(6):
            w3[f, i] = w[f] * scale
        w3[6, i] = scale
        mp, mc = mc, mn


def coarse(
    own, oth, bw, vw, mw, cx, cc, rhs_ref, v_ref, m_ref, ax, ac, az, ay, bx, bc, bz, by,
    out_ref, sx, sc, sz, sy,
    m2, d2, w3, sum_m, m3, b2, v2, sum_r, add, va, vb, e2, v2f, src, v1f, e_ref,
):
    coarse_weights(own, oth, m2, d2, w3, sum_m, m3)
    a, g = position()
    pa = a % 2
    rows = A2 * H2

    def lay(own, oth):
        for k in range(N_AZ):
            base = (k // 2) * N_GZ * 2 * rows
            ref = oth if k % 2 else own
            for i in range(A2):
                s = k * A2 + i + 2
                for p in range(2):
                    b = ref[pl.ds(base + i * 2 + p, G2, stride=2 * rows), :]
                    b2[s, p] = b
                    v2[s, p] = b * d2[s, p]

    pl.when(pa == 0)(lambda: lay(own, oth))
    pl.when(pa == 1)(lambda: lay(oth, own))
    close_ring(b2)
    close_ring(v2)
    consts = level2_consts()

    mc = both(m2, 2)
    vp, vc = both(v2, 1), both(v2, 2)
    face = level2_face(consts, both(m2, 1), mc)
    total = None
    for d in range(AZ2):
        mn, vn = both(m2, d + 3), both(v2, d + 3)
        w, face = level2_plane(consts, face, mc, mn)
        n = level2_around(vp, vc, vn)
        b = both(b2, d + 2)
        r = ((1.0 - OMEGA) * (b[0] + b[1]) + weighted(w[0], n[0])) + weighted(w[1], n[1])
        if d % 2:
            sum_r[d // 2] = total + r
        total, mc, vp, vc = r, mn, vc, vn

    b3 = 0.5 * packed(sum_r)
    for i in range(HALF):
        start = b3[i] * w3[6, i]
        add[i] = start
        va[i + 1] = start
    wrap(va)

    def sweep(src_ref, dst_ref):
        vp, vc = src_ref[0], src_ref[1]
        for i in range(HALF):
            vn = src_ref[i + 2]
            n = (
                vp,
                vn,
                pltpu.roll(vc, 1, 0),
                pltpu.roll(vc, G2 - 1, 0),
                pltpu.roll(vc, 1, 1),
                pltpu.roll(vc, R2 - 1, 1),
            )
            w = [w3[f, i] for f in range(6)]
            dst_ref[i + 1] = ((1.0 - OMEGA) * vc + add[i]) + weighted(w, n)
            vp, vc = vc, vn
        wrap(dst_ref)

    def two(k, carry):
        sweep(va, vb)
        sweep(vb, va)
        return carry

    lax.fori_loop(0, (COARSE_SWEEPS - 2) // 2, two, 0)
    sweep(va, vb)

    row_i, col_i = iota((R2, R2), 0), iota((R2, R2), 1)
    solved = vb[1 : HALF + 1].reshape(HALF * G2, R2)
    e2[0:HALF] = dot(solved, hot(row_i == col_i // 2)).reshape(HALF, G2, R2)
    e2[HALF:AZ3] = dot(solved, hot(row_i == col_i // 2 + R2 // 2)).reshape(HALF, G2, R2)

    at = a * A2
    values = []
    for k in range(A2 + 4):
        e = e2[(a * (A2 // 2) - 1 + k // 2 + AZ3) % AZ3]
        values.append((v2[at + k, 0] + e, v2[at + k, 1] + e))
    mc = both(m2, at + 1)
    face = level2_face(consts, both(m2, at), mc)
    for k in range(1, A2 + 3):
        mn = both(m2, at + k + 1)
        w, face = level2_plane(consts, face, mc, mn)
        n = level2_around(*values[k - 1 : k + 2])
        for p in range(2):
            gain = b2[at + k, p] + weighted(w[p], n[p])
            v2f[k - 1, p] = (1.0 - OMEGA) * values[k][p] + d2[at + k, p] * gain
        mc = mn

    low, high = jnp.maximum(g - 1, 0), jnp.minimum(g + 1, N_GZ - 1)
    for j in range(A2 + 2):
        for q, (p, row) in enumerate(((1, low), (0, g), (1, g), (0, high))):
            src[4 * j + q : 4 * j + q + 1, :] = v2f[j, p, pl.ds(row, 1), :]
    o, c = iota((8 * (A2 + 2), 4 * (A2 + 2)), 0), iota((8 * (A2 + 2), 4 * (A2 + 2)), 1)
    e1 = dot(hot(o // 2 == c), dot(src[...], dup_cols(R2)))
    halo = Halo(cx, cc, None, None)

    def v1_of(i):
        j = (i + 2) // 2
        return wide_planes(vw, halo, 0, i) + e1[T1 * j : T1 * (j + 1)]

    def emit1(i, diagonal, around, centre):
        b = wide_planes(bw, halo, 2, i)
        at = (i + 1) * T1
        v1f[at : at + T1, :] = (1.0 - OMEGA) * centre + OMEGA * (b + around) / diagonal

    level1_walk(lambda i: wide_planes(mw, halo, 1, i), v1_of, -1, A1 + 2, emit1)

    own_rows = (A1 + 2) * NH
    shape = (own_rows + 2 * A1, (A1 + 2) * T1)
    o, c = iota(shape, 0), iota(shape, 1)
    j = jnp.where(o < own_rows, o // NH, (o - own_rows) % A1 + 1)
    h = jnp.where(o < own_rows, (o % NH) // 2 + 2, jnp.where(o < own_rows + A1, 1, H1 + 2))
    e_ref[...] = dot(dot(hot(c == j * T1 + h), v1f[...]), dup_cols(R1))
    ah, bh = Halo(ax, ac, az, ay), Halo(bx, bc, bz, by)
    m_of, mb, ma = fine_mobility(m_ref, ah)
    old, ob, oa = fine_values(v_ref, bh)

    def v_of(i):
        at = (i // 2 + 1) * NH
        return old(i) + e_ref[at : at + NH, :]

    def around_row(value, start):
        def row(i):
            at = start + i // 2
            return value(i) + e_ref[at : at + 1, :]

        return row

    def emit(i, diagonal, around, centre):
        out_ref[i] = (1.0 - OMEGA) * centre + OMEGA * (rhs_ref[i] + around) / diagonal

    fine_walk(
        m_of, v_of, mb, ma, around_row(ob, own_rows), around_row(oa, own_rows + A1), emit
    )
    store_faces(out_ref, sx, sc, sz, sy)


def final(rhs_ref, v_ref, m_ref, ax, ac, az, ay, gx, gc, gz, gy, p_hbm, out_hbm, out_ref, sems):
    part = NA // 4
    copies = [
        pltpu.make_async_copy(
            src.at[pl.ds(k * part, part)], dst.at[pl.ds(k * part, part)], sems.at[4 * n + k]
        )
        for n, (src, dst) in enumerate(((v_ref, p_hbm), (out_ref, out_hbm)))
        for k in range(4)
    ]
    for copy in copies[:4]:
        copy.start()
    ah, gh = Halo(ax, ac, az, ay), Halo(gx, gc, gz, gy)
    m_of, mb, ma = fine_mobility(m_ref, ah)
    v_of, vb, va = fine_values(v_ref, gh)

    def emit(i, diagonal, around, centre):
        out_ref[i] = (rhs_ref[i] - diagonal * centre + around) / diagonal
        if i % part == part - 1:
            copies[4 + i // part].start()

    fine_walk(m_of, v_of, mb, ma, vb, va, emit)
    for copy in copies:
        copy.wait()


def swap(x, axis, odd):
    n = lax.axis_size(axis)
    pairs = []
    for i in range(n):
        partner = i ^ 1 if odd == 0 else ((i + 1) % n if i % 2 else (i - 1) % n)
        pairs.append((i, partner))
    return lax.ppermute(x, axis, pairs)


def exchange(sx, sc, sz, sy):
    return swap(sx, "az", 1), swap(sc, "az", 0), swap(sz, "gz", 0), swap(sy, "gz", 1)


def gathered(x):
    groups = [[a * N_GZ + g for a in range(c, N_AZ, 2) for g in range(N_GZ)] for c in range(2)]
    own = lax.all_to_all(x, ("az", "gz"), 0, 0, tiled=True, axis_index_groups=groups)
    own = own.reshape(own.shape[0] * own.shape[1], own.shape[2])
    return own, swap(own, "az", 0)


def faces(planes, rows, width):
    return [struct(planes, width)] * 2 + [struct(rows, width)] * 2


def vmem(*shape):
    return pltpu.VMEM(shape, F32)


def body(pressure, divergence, void_fraction, bubble_volume, bubble_count, bubble_cell):
    block = struct(NA, NH, NR)
    wide = struct(A1, T1, R1)
    cell = bubble_cell.reshape(1, SLOTS)
    volume = bubble_volume.reshape(1, SLOTS)
    pairs = vmem(A1 * NH, NR)
    halves = vmem(A2 * T1, R1)

    far = [
        pltpu.with_memory_space_constraint(x, pltpu.HBM)
        for x in (void_fraction, volume)
    ]
    m0, m1, m2, live = call(
        mobilities,
        [block, wide, struct(A2 * H2, R2), struct(1, SLOTS)],
        (*far, bubble_count),
        [
            pairs,
            halves,
            vmem(NA, NH, NR),
            vmem(1, SLOTS),
            pltpu.SemaphoreType.DMA((5,)),
        ],
        hbm=(0, 1),
        smem=(2,),
    )
    send = call(
        first_faces,
        faces(3 * NH, 2 * NA + A1 // 2, NR),
        (pressure, m0, m1, live),
    )
    ha = exchange(*send)
    rhs, v0, *send = call(
        presmooth, [block, block] + faces(NH, NA, NR), (pressure, divergence, m0, cell, *ha)
    )
    hb = exchange(*send)
    b1, v1, sz, sy = call(
        restrict,
        [wide, wide] + [struct(5 * A1, R1)] * 2,
        (rhs, v0, m0, m1, *ha, *hb),
        [pairs],
    )
    v1, m1, b1, sx, sc = call(
        widen,
        [wide, wide, wide] + [struct(5 * T1, R1)] * 2,
        (b1, v1, m1, swap(sz, "gz", 0), swap(sy, "gz", 1)),
    )
    hc = swap(sx, "az", 1), swap(sc, "az", 0)
    (copies,) = call(restrict1, [struct(64, 2 * A2 * H2, R2)], (b1, v1, m1, m2, *hc), [halves])
    ring = vmem(AZ2 + 4, 2, G2, R2)
    ends = vmem(HALF + 2, G2, R2)
    third = vmem(AZ3, G2, R2)
    out, *send = call(
        coarse,
        [block] + faces(NH, NA, NR),
        (*gathered(copies), b1, v1, m1, *hc, rhs, v0, m0, *ha, *hb),
        [
            ring,
            ring,
            vmem(7, HALF, G2, R2),
            third,
            ends,
            ring,
            ring,
            third,
            vmem(HALF, G2, R2),
            ends,
            ends,
            third,
            vmem(A2 + 2, 2, G2, R2),
            vmem(4 * (A2 + 2), R2),
            vmem((A1 + 2) * T1, R1),
            vmem((A1 + 2) * NH + 2 * A1, NR),
        ],
    )
    hg = exchange(*send)
    return tuple(
        call(
            final,
            [block, block],
            (rhs, out, m0, *ha, *hg),
            [vmem(NA, NH, NR), pltpu.SemaphoreType.DMA((8,))],
            hbm_out=(0, 1),
        )
    )


def solution(mesh):
    return jax.shard_map(
        body,
        mesh=mesh,
        in_specs=(
            P("az", "gz", None),
            P("az", "gz", None),
            P("az", "gz", None),
            P(("az", "gz")),
            P(("az", "gz")),
            P(("az", "gz")),
        ),
        out_specs=(P("az", "gz", None), P("az", "gz", None)),
        check_vma=False,
    )
```
